128 devices in a mesh: section: 2 (over y_lo), dp: 64 (over y_hi, z, x, core).
Axes of the slice: x: 4, y: 4 (y_hi: 2, y_lo: 2; y = y_hi * 2 + y_lo), z: 4, core: 2. Of those that a mesh axis runs over, the one named last changes fastest.
Arguments:
- tokens: bfloat16 [2, 8192, 1024], P(None, 'dp'), may hold values from -6 to 6
- positions: int32 [2, 8192], P(None, 'dp'), may hold values from 0 to 127, as said below
- cotangent: bfloat16 [2, 8192, 1024], P(None, 'dp'), may hold values from -16 to 16
- w_qkv: bfloat16 [2, 1024, 3072], P('section', 'dp'), may hold values from -0.1875 to 0.1875
- b_query: bfloat16 [2, 1024], P('section', 'dp'), may hold values from -3 to 3
- b_value: bfloat16 [2, 1024], P('section', 'dp'), may hold values from -3 to 3
- w_out: bfloat16 [2, 1024, 1024], P('section', 'dp'), may hold values from -0.75 to 0.75
- b_out: bfloat16 [2, 1024], P('section', 'dp'), may hold values from -3 to 3
- w_up: bfloat16 [2, 1024, 4096], P('section', 'dp'), may hold values from -0.1875 to 0.1875
- b_up: bfloat16 [2, 4096], P('section', 'dp'), may hold values from -3 to 3
- w_down: bfloat16 [2, 4096, 1024], P('section', 'dp'), may hold values from -0.09375 to 0.09375
- b_down: bfloat16 [2, 1024], P('section', 'dp'), may hold values from -3 to 3
- gain_one: bfloat16 [2, 1024], P('section', 'dp'), may hold values from 0.5 to 1.5
- shift_one: bfloat16 [2, 1024], P('section', 'dp'), may hold values from -2 to 2
- gain_two: bfloat16 [2, 1024], P('section', 'dp'), may hold values from 0.5 to 1.5
- shift_two: bfloat16 [2, 1024], P('section', 'dp'), may hold values from -2 to 2
Outputs:
- layer_out: bfloat16 [2, 2, 8192, 1024], P('section', None, 'dp')
- input_grad: bfloat16 [2, 2, 8192, 1024], P('section', None, 'dp')
- grad_w_qkv: float32 [2, 1024, 3072], P('section', 'dp')
- grad_b_query: float32 [2, 1024], P('section', 'dp')
- grad_b_value: float32 [2, 1024], P('section', 'dp')
- grad_w_out: float32 [2, 1024, 1024], P('section', 'dp')
- grad_b_out: float32 [2, 1024], P('section', 'dp')
- grad_w_up: float32 [2, 1024, 4096], P('section', 'dp')
- grad_b_up: float32 [2, 4096], P('section', 'dp')
- grad_w_down: float32 [2, 4096, 1024], P('section', 'dp')
- grad_b_down: float32 [2, 1024], P('section', 'dp')
- grad_gain_one: float32 [2, 1024], P('section', 'dp')
- grad_shift_one: float32 [2, 1024], P('section', 'dp')
- grad_gain_two: float32 [2, 1024], P('section', 'dp')
- grad_shift_two: float32 [2, 1024], P('section', 'dp')
The draws below stay inside these ranges and needn't reach their ends.
Inputs may be any that keep to these rules, and one draw needn't show every extreme that they name: positions counts up by one along each sequence from 0; a sequence lies within one block of 128 rows of one device and micro-batch, each block begins a sequence, and some sequence is 128 long.
All inputs are finite; a program needn't handle non-finite values.
Results may differ from the reference program's by a relative error of at most 0.015.
Values may be sent and summed in bfloat16 or wider, within the bound.
A program may use at most 320 MiB of HBM per device.

```python
import jax
import jax.numpy as jnp
from jax import lax

D = 1024
HEADS = 16
HEAD = 64
FF = 4096
ROWS = 128
MB = 2
SECTIONS = 2
GROUP_ROWS = 8192


def draw_positions(key, part):
    key = jax.random.fold_in(key, 11)
    cut_key, full_key = jax.random.split(key)
    block_count = MB * GROUP_ROWS // ROWS
    starts = jax.random.randint(cut_key, (block_count, ROWS), 0, 20) == 0
    column = jnp.arange(ROWS, dtype=jnp.int32)
    chosen = jax.random.randint(full_key, (), 0, block_count)
    whole_block = (jnp.arange(block_count, dtype=jnp.int32) == chosen)[:, None]
    starts = jnp.where(whole_block, False, starts) | (column == 0)[None, :]
    begin = lax.cummax(jnp.where(starts, column[None, :], 0), axis=1)
    return (column[None, :] - begin).reshape(MB, GROUP_ROWS).astype(jnp.int32)


def strengthened(entries, own_key, source, target, blocks, factor):
    owner, partner = [(jnp.arange(entries.shape[dim]) // (entries.shape[dim] // blocks)).reshape([-1 if axis == dim else 1 for axis in range(entries.ndim)]) for dim in (source, target)]
    chosen = jax.random.permutation(own_key, blocks)[partner]
    strong = (owner == chosen) | (owner == (partner + blocks // 2) % blocks)
    return jnp.where(strong, factor * entries, entries)


def steps_of(key, shape, cuts, least, largest):
    level = 1.0
    for axis_at, shards_of in cuts:
        steps = jax.random.uniform(jax.random.fold_in(jax.random.fold_in(key, 6), axis_at), (shards_of,), jnp.float32, least / len(cuts), largest / len(cuts))
        level = level * jnp.repeat(jnp.exp(steps), shape[axis_at] // shards_of).reshape((-1,) + (1,) * (len(shape) - 1 - axis_at))
    return level


def centred(own_key, shape, width, most, cuts=(), kind=jnp.bfloat16):
    entries = width * jax.random.normal(own_key, shape, jnp.float32)
    if cuts:
        entries = entries * steps_of(own_key, shape, cuts, -0.22, 0.18)
    return jnp.clip(entries, -most, most).astype(kind)


def noise_with(key, dims, scale, bound, cuts, heavy, kind=jnp.bfloat16):
    drawn = scale * jax.random.normal(key, dims, jnp.float32)
    if cuts:
        drawn = drawn * steps_of(key, dims, cuts, -0.22, 0.18)
    return jnp.clip(strengthened(drawn, jax.random.fold_in(key, 3), *heavy), -bound, bound).astype(kind)


def setup_inputs(seed: int = 0) -> dict:
    arg_keys = jax.random.split(jax.random.key(seed), 17)
    tokens = centred(arg_keys[0], (MB, GROUP_ROWS, D), 1.0, 6.0, ((1, 64),))
    positions = draw_positions(jax.random.fold_in(arg_keys[16], 71), 0)
    cotangent = noise_with(arg_keys[2], (MB, GROUP_ROWS, D), 1.0, 16.0, ((1, 64),), (1, 2, 64, 4.0))
    w_qkv = centred(arg_keys[3], (SECTIONS, D, 3 * D), D ** -0.5, 0.1875, ((0, 2), (1, 64)))
    b_query = centred(arg_keys[4], (SECTIONS, D), 0.5, 3.0, ((0, 2), (1, 64)))
    b_value = centred(arg_keys[5], (SECTIONS, D), 0.5, 3.0, ((0, 2), (1, 64)))
    w_out = centred(arg_keys[6], (SECTIONS, D, D), HEAD ** -0.5, 0.75, ((0, 2), (1, 64)))
    b_out = centred(arg_keys[7], (SECTIONS, D), 0.5, 3.0, ((0, 2), (1, 64)))
    w_up = centred(arg_keys[8], (SECTIONS, D, FF), D ** -0.5, 0.1875, ((0, 2), (1, 64)))
    b_up = centred(arg_keys[9], (SECTIONS, FF), 0.5, 3.0, ((0, 2), (1, 64)))
    w_down = centred(arg_keys[10], (SECTIONS, FF, D), FF ** -0.5, 0.09375, ((0, 2), (1, 64)))
    b_down = centred(arg_keys[11], (SECTIONS, D), 0.5, 3.0, ((0, 2), (1, 64)))
    gain_one = jnp.clip(1.0 + 0.1 * jax.random.normal(arg_keys[12], (SECTIONS, D), jnp.float32), 0.5, 1.5).astype(jnp.bfloat16)
    shift_one = centred(arg_keys[13], (SECTIONS, D), 0.3, 2.0, ((0, 2), (1, 64)))
    gain_two = jnp.clip(1.0 + 0.1 * jax.random.normal(arg_keys[14], (SECTIONS, D), jnp.float32), 0.5, 1.5).astype(jnp.bfloat16)
    shift_two = centred(arg_keys[15], (SECTIONS, D), 0.3, 2.0, ((0, 2), (1, 64)))
    return {"tokens": tokens, "positions": positions, "cotangent": cotangent, "w_qkv": w_qkv, "b_query": b_query, "b_value": b_value, "w_out": w_out, "b_out": b_out, "w_up": w_up, "b_up": b_up, "w_down": w_down, "b_down": b_down, "gain_one": gain_one, "shift_one": shift_one, "gain_two": gain_two, "shift_two": shift_two}


@jax.custom_vjp
def low(v):
    return lax.optimization_barrier(v.astype(jnp.bfloat16)).astype(jnp.float32)

@jax.custom_vjp
def low_back(v):
    return v

def low_keep(v):
    return (low(v), None)

def low_pass(kept, grad):
    return (grad,)

def back_keep(v):
    return (v, None)

def back_low(kept, grad):
    return (low(grad),)
low.defvjp(low_keep, low_pass)
low_back.defvjp(back_keep, back_low)
epsilon = 1e-05
masked_value = -1000000000.0

def matmul(left, right):
    return jnp.dot(left, right, precision=lax.Precision.HIGHEST, preferred_element_type=jnp.float32)

def norm_rows(values, gain, shift):
    center = values - lax.optimization_barrier(jnp.mean(values, axis=-1, keepdims=True))
    spread = lax.optimization_barrier(jnp.mean(center * center, axis=-1, keepdims=True))
    return center * lax.rsqrt(spread + epsilon) * gain + shift

def split_heads(tensor, row_count):
    return tensor.reshape(-1, row_count, HEADS, HEAD)

def block_layer(hidden_in, params, distance, allowed):
    w_qkv, b_query, b_value, w_out, b_out, w_up, b_up, w_down, b_down, gain_one, shift_one, gain_two, shift_two = params
    model_width = hidden_in.shape[-1]
    row_count = allowed.shape[-1]
    normed = low(norm_rows(hidden_in, gain_one, shift_one))
    mixed_proj = matmul(normed, w_qkv)
    queries = low(low_back(mixed_proj[:, :model_width] + b_query))
    keys_all = low(low_back(mixed_proj[:, model_width:2 * model_width]))
    values_all = low(low_back(mixed_proj[:, 2 * model_width:] + b_value))
    slopes = 2.0 ** (-8.0 * jnp.arange(1, HEADS + 1, dtype=jnp.float32) / HEADS)
    scores = jnp.einsum('bqhd,bkhd->bhqk', split_heads(queries, row_count), split_heads(keys_all, row_count), precision=lax.Precision.HIGHEST) * HEAD ** (-0.5)
    scores = low_back(scores - slopes[None, :, None, None] * distance[None, None])
    masked = jnp.where(allowed[:, None], scores, masked_value)
    softmax_probs = low(jax.nn.softmax(masked, axis=-1))
    attended = jnp.einsum('bhqk,bkhd->bqhd', softmax_probs, split_heads(values_all, row_count), precision=lax.Precision.HIGHEST)
    attended = low(low_back(attended.reshape(-1, model_width)))
    branch = low_back(matmul(attended, w_out) + b_out)
    middle = hidden_in + branch
    normed_two = low(norm_rows(middle, gain_two, shift_two))
    upward = low_back(matmul(normed_two, w_up) + b_up)
    activated = low(jax.nn.gelu(upward, approximate=True))
    downward = low_back(matmul(activated, w_down) + b_down)
    return middle + downward

def reference(tokens, positions, cotangent, w_qkv, b_query, b_value, w_out, b_out, w_up, b_up, w_down, b_down, gain_one, shift_one, gain_two, shift_two):
    params = [weight.astype(jnp.float32) for weight in (w_qkv, b_query, b_value, w_out, b_out, w_up, b_up, w_down, b_down, gain_one, shift_one, gain_two, shift_two)]
    block_places = positions.reshape(-1, ROWS)
    query_index = jnp.arange(ROWS, dtype=jnp.int32)[:, None]
    key_index = jnp.arange(ROWS, dtype=jnp.int32)[None, :]
    distance = (query_index - key_index).astype(jnp.float32)
    allowed = (query_index >= key_index)[None] & ((query_index - key_index)[None] <= block_places[:, :, None])
    inputs = tokens.astype(jnp.float32).reshape(-1, D)
    probe = jnp.zeros_like(inputs)

    def network(hidden, probe_value, first, second):
        first_out = block_layer(hidden, first, distance, allowed)
        passed = low(low_back(first_out + probe_value))
        return (first_out, block_layer(passed, second, distance, allowed))
    first_params = tuple((weight[0] for weight in params))
    second_params = tuple((weight[1] for weight in params))
    outputs, backward = jax.vjp(network, inputs, probe, first_params, second_params)
    grad_inputs, grad_probe, grad_first, grad_second = backward((jnp.zeros_like(inputs), cotangent.astype(jnp.float32).reshape(-1, D)))
    shape_out = (MB, GROUP_ROWS, D)
    layer_out = jnp.stack([outputs[0].reshape(shape_out), outputs[1].reshape(shape_out)]).astype(jnp.bfloat16)
    input_grad = jnp.stack([grad_inputs.reshape(shape_out), grad_probe.reshape(shape_out)]).astype(jnp.bfloat16)
    grads = [jnp.stack([one, two]) for one, two in zip(grad_first, grad_second)]
    return (layer_out, input_grad, grads[0], grads[1], grads[2], grads[3], grads[4], grads[5], grads[6], grads[7], grads[8], grads[9], grads[10], grads[11], grads[12])
```

```python
from functools import partial

import jax
import jax.numpy as jnp
from jax import lax
from jax.experimental import pallas as pl
from jax.experimental.pallas import tpu as pltpu
from jax.sharding import Mesh
from jax.sharding import PartitionSpec as P

HEADS = 16
D = 1024
FF = 4096
ROWS = 256
BLOCK = 128
NA = 8192 + 128
AXES = ("section", "dp_0", "dp_1", "dp_2", "dp_3")
DP = AXES[1:]
MESH = pl.DeviceIdType.MESH
EPSILON = 1e-05
FAR = 1e30
ANY = pl.BlockSpec(memory_space=pl.ANY)
VMEM = pl.BlockSpec(memory_space=pltpu.VMEM)
SMEM = pl.BlockSpec(memory_space=pltpu.SMEM)
bf16 = jnp.bfloat16
f32 = jnp.float32


class Place:
    def __init__(self):
        self.s, self.yh, self.z, self.x, self.c = [lax.axis_index(a) for a in AXES]
        self.p = jnp.where(self.c == 0, self.z, self.x)
        self.q = jnp.where(self.c == 0, self.x, self.z)

    def zx(self, dp, dq):
        pp, qq = lax.rem(self.p + (dp + 4), 4), lax.rem(self.q + (dq + 4), 4)
        return jnp.where(self.c == 0, pp, qq), jnp.where(self.c == 0, qq, pp)

    def at(self, dp, dq):
        z, x = self.zx(dp, dq)
        return (self.s, self.yh, z, x, self.c)

    def half(self, r):
        return lax.rem(self.yh + r, 2)

    def over_y(self):
        return (self.s, 1 - self.yh, self.z, self.x, self.c)

    def other_core(self):
        return (self.s, self.yh, self.z, self.x, 1 - self.c)

    def neighbours(self):
        return (
            self.over_y(),
            self.other_core(),
            self.at(1, 0),
            self.at(-1, 0),
            self.at(0, 1),
            self.at(0, -1),
        )


def greet(devices):
    barrier = pltpu.get_barrier_semaphore()
    for device in devices:
        pl.semaphore_signal(barrier, inc=1, device_id=device, device_id_type=MESH)
    pl.semaphore_wait(barrier, len(devices))


class Mail:
    def __init__(self, send, recv):
        self.send, self.recv, self.sent, self.number = send, recv, [], {}

    def post(self, name, src, dst, device):
        k = self.number.setdefault(name, len(self.number))
        copy = pltpu.make_async_remote_copy(
            src_ref=src,
            dst_ref=dst,
            send_sem=self.send.at[k],
            recv_sem=self.recv.at[k],
            device_id=device,
            device_id_type=MESH,
        )
        copy.start()
        self.sent.append(copy)

    def take(self, name, dst, device):
        k = self.number[name]
        pltpu.make_async_remote_copy(
            src_ref=dst,
            dst_ref=dst,
            send_sem=self.send.at[k],
            recv_sem=self.recv.at[k],
            device_id=device,
            device_id_type=MESH,
        ).wait_recv()

    def finish(self):
        for copy in self.sent:
            copy.wait_send()


GATHER_COPIES = 2 * (1 + 6 + 24 + 32)


def gather_kernel(a_ref, b_ref, ga, gb, send, recv, own):
    at = Place()
    mail = Mail(send, recv)
    greet(at.neighbours())
    outs = (ga, gb)
    local = []
    z0, x0 = at.zx(0, 0)
    for t, (src, out) in enumerate(((a_ref, ga), (b_ref, gb))):
        copy = pltpu.make_async_copy(src, out.at[at.yh, z0, x0, at.c], own.at[t])
        copy.start()
        local.append(copy)

    def view(t, r, dp, dq, core=None):
        z, x = at.zx(dp, dq)
        return outs[t].at[at.half(r), z, x, at.c if core is None else core]

    def post(kind, t, r, dp, dq, device):
        mine = (r, dp, dq) == (0, 0, 0)
        src = (a_ref, b_ref)[t] if mine else view(t, r, dp, dq)
        mail.post((kind, t, r, dp, dq), src, view(t, r, dp, dq), device)

    def spread(r, dq, both=True):
        for t in (0, 1):
            post("PR", t, r, 0, dq, at.at(1, 0))
            post("PL", t, r, 0, dq, at.at(-1, 0))
        hand_over(r, 0, dq)

    def hand_over(r, dp, dq):
        for t in (0, 1):
            post("C", t, r, dp, dq, at.other_core())

    def take(kind, t, sent, got, device):
        mail.take((kind, t, *sent), view(t, *got), device)

    for t in (0, 1):
        post("Y", t, 0, 0, 0, at.over_y())
    for t in (0, 1):
        post("QR", t, 0, 0, 0, at.at(0, 1))
        post("QL", t, 0, 0, 0, at.at(0, -1))
    spread(0, 0)
    for t in (0, 1):
        take("Y", t, (0, 0, 0), (1, 0, 0), at.over_y())
        post("QR", t, 1, 0, 0, at.at(0, 1))
        post("QL", t, 1, 0, 0, at.at(0, -1))
    spread(1, 0)
    for t in (0, 1):
        take("QR", t, (0, 0, 0), (0, 0, -1), at.at(0, 1))
        post("QR2", t, 0, 0, -1, at.at(0, 1))
    spread(0, -1)
    for t in (0, 1):
        take("QL", t, (0, 0, 0), (0, 0, 1), at.at(0, 1))
    spread(0, 1)

    def pass_on(dq):
        for t in (0, 1):
            take("PR", t, (0, 0, dq), (0, -1, dq), at.at(1, 0))
            post("PR2", t, 0, -1, dq, at.at(1, 0))
        for t in (0, 1):
            take("PL", t, (1, 0, dq), (1, 1, dq), at.at(1, 0))
            post("PL2", t, 1, 1, dq, at.at(-1, 0))
        hand_over(0, -1, dq)
        hand_over(1, 1, dq)
        for t in (0, 1):
            take("PL", t, (0, 0, dq), (0, 1, dq), at.at(1, 0))
            take("PR", t, (1, 0, dq), (1, -1, dq), at.at(1, 0))
        hand_over(0, 1, dq)
        hand_over(1, -1, dq)

    for t in (0, 1):
        take("QL", t, (1, 0, 0), (1, 0, 1), at.at(0, 1))
        post("QL2", t, 1, 0, 1, at.at(0, -1))
    spread(1, 1)
    for t in (0, 1):
        take("QR", t, (1, 0, 0), (1, 0, -1), at.at(0, 1))
    spread(1, -1)
    pass_on(0)
    for t in (0, 1):
        take("QR2", t, (0, 0, -1), (0, 0, -2), at.at(0, 1))
    spread(0, 2)
    for t in (0, 1):
        take("QL2", t, (1, 0, 1), (1, 0, 2), at.at(0, 1))
    spread(1, 2)
    for dq in (-1, 1, 2):
        pass_on(dq)
    for dq in (0, -1, 1, 2):
        for t in (0, 1):
            take("PR2", t, (0, -1, dq), (0, -2, dq), at.at(1, 0))
            take("PL2", t, (1, 1, dq), (1, 2, dq), at.at(1, 0))
        hand_over(0, 2, dq)
        hand_over(1, 2, dq)
    for name in [n for n in mail.number if n[0] == "C"]:
        _, t, r, dp, dq = name
        mail.take(name, view(t, r, dq, dp, 1 - at.c), at.other_core())
    mail.finish()
    for copy in local:
        copy.wait()


def gather(a, b):
    return pl.pallas_call(
        gather_kernel,
        out_shape=(
            jax.ShapeDtypeStruct((2, 4, 4, 2, 16, NA), bf16),
            jax.ShapeDtypeStruct((2, 4, 4, 2, 64, D), bf16),
        ),
        in_specs=[ANY, ANY],
        out_specs=(ANY, ANY),
        scratch_shapes=[
            pltpu.SemaphoreType.DMA((GATHER_COPIES,)),
            pltpu.SemaphoreType.DMA((GATHER_COPIES,)),
            pltpu.SemaphoreType.DMA((2,)),
        ],
        compiler_params=pltpu.CompilerParams(collective_id=0, has_side_effects=True),
        name="gather_weights",
    )(a, b)


def dot(a, b, dims=((1,), (0,))):
    return lax.dot_general(a, b, (dims, ((), ())), preferred_element_type=f32)


NT = ((1,), (1,))
TN = ((0,), (0,))


def cols(j, width):
    return pl.ds(pl.multiple_of(j * width, width), width)


B_QUERY, B_VALUE, B_OUT, B_DOWN, G_ONE, S_ONE, G_TWO, S_TWO = range(8)


def layer_kernel(
    tokens,
    places,
    cotangent,
    slopes,
    vec,
    b_up,
    w_rows,
    w_down,
    layer_out,
    input_grad,
    n_t,
    a_t,
    n2_t,
    act_t,
    g_mixed,
    g_branch,
    g_upward,
    g_y,
    g_vec,
    g_bup,
    xin,
    gyin,
    gxout,
    w1,
    w2,
    xhat1,
    rstd1,
    xhat2,
    rstd2,
    mixed,
    far,
    probs,
    wide,
    middle,
    gprime,
    act,
    grad,
    load,
    send,
    recv,
):
    section = lax.axis_index("section")
    loads = {}
    pieces = [("qkv", j * 1024, 1024) for j in range(3)]
    pieces += [("out", 3072, 1024)] + [("up", 4096 + j * 1024, 1024) for j in range(4)]
    for k, (name, at, width) in enumerate(pieces):
        copy = pltpu.make_async_copy(
            w_rows.at[:, pl.ds(at, width)], w1.at[:, pl.ds(at, width)], load.at[k]
        )
        copy.start()
        loads.setdefault(name, []).append(copy)
    copy = pltpu.make_async_copy(w_down, w2, load.at[len(pieces)])
    copy.start()
    loads["down"] = [copy]

    def loaded(name):
        for item in loads[name]:
            item.wait()

    other = {"section": 1 - section}
    greet((other,))
    forth = pltpu.make_async_remote_copy(
        src_ref=layer_out,
        dst_ref=xin,
        send_sem=send.at[0],
        recv_sem=recv.at[0],
        device_id=other,
        device_id_type=MESH,
    )
    back = pltpu.make_async_remote_copy(
        src_ref=gxout,
        dst_ref=gyin,
        send_sem=send.at[1],
        recv_sem=recv.at[1],
        device_id=other,
        device_id_type=MESH,
    )

    row = lax.broadcasted_iota(jnp.int32, (BLOCK, BLOCK), 0)
    col = lax.broadcasted_iota(jnp.int32, (BLOCK, BLOCK), 1)
    distance = row - col
    for b in range(2):
        allowed = (distance >= 0) & (distance <= places[pl.ds(b * BLOCK, BLOCK), :])
        far[b] = jnp.where(allowed, distance.astype(f32), FAR)
    low_lane = lax.broadcasted_iota(jnp.int32, (BLOCK, BLOCK), 1) < 64

    @pl.when(section == 0)
    def _():
        xin[...] = tokens[...]

    @pl.when(section == 1)
    def _():
        forth.wait_recv()
        gyin[...] = cotangent[...]

    chunk = 32

    def rows_loop(body):
        @pl.loop(0, ROWS // chunk)
        def _(i):
            body(pl.ds(pl.multiple_of(i * chunk, chunk), chunk))

    def norm_rows(rows, v, xhat, rstd, gain, shift):
        center = v - jnp.mean(v, axis=-1, keepdims=True)
        r = lax.rsqrt(jnp.mean(center * center, axis=-1, keepdims=True) + EPSILON)
        h = center * r
        xhat[rows, :] = h
        rstd[rows, :] = jnp.broadcast_to(r, (chunk, 128))
        return h * vec[pl.ds(gain, 1), :] + vec[pl.ds(shift, 1), :]

    def transpose_into(dst, src, width):
        @pl.loop(0, width // 256)
        def _(j):
            dst[cols(j, 256), :] = src[:, cols(j, 256)].T

    def one(rows):
        v = xin[rows, :].astype(f32)
        g_branch[rows, :] = norm_rows(rows, v, xhat1, rstd1, G_ONE, S_ONE).astype(bf16)

    rows_loop(one)
    transpose_into(n_t, g_branch, D)

    loaded("qkv")

    @pl.loop(0, 6)
    def _(j):
        y = dot(g_branch[...], w1[:, cols(j, 512)])
        mixed[:, cols(j, 512)] = (y + wide[pl.ds(0, 1), cols(j, 512)]).astype(bf16)

    def pair(value):
        zero = jnp.zeros_like(value)
        return jnp.concatenate(
            [jnp.where(low_lane, value, zero), jnp.where(low_lane, zero, value)], axis=0
        )

    def unpair(value):
        return jnp.where(low_lane, value[:BLOCK], value[BLOCK:])

    def slope_rows(hp):
        first = lax.broadcasted_iota(jnp.int32, (2 * BLOCK, 1), 0) < BLOCK
        return jnp.where(first, slopes[2 * hp], slopes[2 * hp + 1])

    def heads(ref, b, part, hp):
        at = pl.multiple_of(part * D + hp * 128, 128)
        return ref[pl.ds(b * BLOCK, BLOCK), pl.ds(at, 128)]

    @pl.loop(0, 8)
    def _(hp):
        for b in range(2):
            queries = pair(heads(mixed, b, 0, hp))
            scores = dot(queries, heads(mixed, b, 1, hp), NT) * 0.125
            gap = jnp.concatenate([far[b], far[b]], axis=0)
            scores = scores - slope_rows(hp) * gap
            e = jnp.exp(scores - jnp.max(scores, axis=-1, keepdims=True))
            p = e * (1.0 / jnp.sum(e, axis=-1, keepdims=True))
            probs[2 * hp + b] = p
            out = unpair(dot(p.astype(bf16), heads(mixed, b, 2, hp)))
            g_y[pl.ds(b * BLOCK, BLOCK), pl.ds(pl.multiple_of(hp * 128, 128), 128)] = (
                out.astype(bf16)
            )

    transpose_into(a_t, g_y, D)
    loaded("out")

    @pl.loop(0, 2)
    def _(j):
        y = dot(g_y[...], w1[:, pl.ds(pl.multiple_of(3072 + j * 512, 512), 512)])
        middle[:, cols(j, 512)] = (
            xin[:, cols(j, 512)].astype(f32) + y + vec[pl.ds(B_OUT, 1), cols(j, 512)]
        )

    def two(rows):
        g_branch[rows, :] = norm_rows(
            rows, middle[rows, :], xhat2, rstd2, G_TWO, S_TWO
        ).astype(bf16)

    rows_loop(two)
    transpose_into(n2_t, g_branch, D)
    loaded("up")

    @pl.loop(0, 8)
    def _(j):
        y = dot(g_branch[...], w1[:, pl.ds(pl.multiple_of(4096 + j * 512, 512), 512)])
        u = y + b_up[pl.ds(0, 1), cols(j, 512)]
        c = 0.7978845608028654
        uu = u * u
        t = jnp.tanh(c * (u + 0.044715 * u * uu))
        half = 0.5 * (1.0 + t)
        a = (u * half).astype(bf16)
        act[:, cols(j, 512)] = a
        act_t[cols(j, 512), :] = a.T
        gprime[:, cols(j, 512)] = half + 0.5 * u * (1.0 - t * t) * (
            c * (1.0 + (3 * 0.044715) * uu)
        )

    loaded("down")

    @pl.loop(0, 2)
    def _(j):
        y = dot(act[...], w2[:, cols(j, 512)])
        y = middle[:, cols(j, 512)] + y + vec[pl.ds(B_DOWN, 1), cols(j, 512)]
        layer_out[:, cols(j, 512)] = y.astype(bf16)

    @pl.when(section == 0)
    def _():
        forth.start()
        back.wait_recv()

    g_y[...] = gyin[...]
    g_vec[...] = jnp.zeros_like(g_vec)

    @pl.loop(0, 8)
    def _(j):
        g = dot(g_y[...], w2[cols(j, 512), :], NT)
        g = (g * gprime[:, cols(j, 512)]).astype(bf16)
        g_upward[:, cols(j, 512)] = g
        g_bup[:, cols(j, 512)] = jnp.broadcast_to(
            jnp.sum(g.astype(f32), axis=0, keepdims=True), (8, 512)
        )

    @pl.loop(0, 4)
    def _(j):
        grad[:, cols(j, 256)] = dot(g_upward[...], w1[cols(j, 256), pl.ds(4096, 4096)], NT)

    def add(index, value):
        g_vec[pl.ds(index, 1), :] = g_vec[pl.ds(index, 1), :] + jnp.sum(
            value, axis=0, keepdims=True
        )

    def norm_back(rows, xhat, rstd, gain, shift):
        dy = grad[rows, :]
        h = xhat[rows, :]
        add(gain, dy * h)
        add(shift, dy)
        dh = dy * vec[pl.ds(gain, 1), :]
        m1 = jnp.mean(dh, axis=-1, keepdims=True)
        m2 = jnp.mean(dh * h, axis=-1, keepdims=True)
        return rstd[rows, pl.ds(0, 1)] * (dh - m1 - h * m2)

    def three(rows):
        gy = g_y[rows, :].astype(f32)
        gm = gy + norm_back(rows, xhat2, rstd2, G_TWO, S_TWO)
        add(B_DOWN, gy)
        middle[rows, :] = gm
        low = gm.astype(bf16)
        g_branch[rows, :] = low
        add(B_OUT, low.astype(f32))

    rows_loop(three)

    @pl.loop(0, 4)
    def _(j):
        y = dot(g_branch[...], w1[cols(j, 256), pl.ds(3072, 1024)], NT)
        act[:, cols(j, 256)] = y.astype(bf16)

    @pl.loop(0, 8)
    def _(hp):
        for b in range(2):
            queries = pair(heads(mixed, b, 0, hp))
            keys, values = heads(mixed, b, 1, hp), heads(mixed, b, 2, hp)
            da = pair(heads(act, b, 0, hp))
            p = probs[2 * hp + b]
            dv = dot(p.astype(bf16), da, TN)
            dp = dot(da, values, NT)
            delta = jnp.sum(p * dp, axis=-1, keepdims=True)
            ds = (p * (dp - delta)).astype(bf16)
            dq = unpair(dot(ds, keys)) * 0.125
            dk = dot(ds, queries, TN) * 0.125
            for part, value in enumerate((dq, dk, dv)):
                at = pl.multiple_of(part * D + hp * 128, 128)
                g_mixed[pl.ds(b * BLOCK, BLOCK), pl.ds(at, 128)] = value.astype(bf16)

    @pl.loop(0, 4)
    def _(j):
        grad[:, cols(j, 256)] = dot(g_mixed[...], w1[cols(j, 256), pl.ds(0, 3072)], NT)

    def four(rows):
        gx = middle[rows, :] + norm_back(rows, xhat1, rstd1, G_ONE, S_ONE)
        gxout[rows, :] = gx.astype(bf16)
        add(B_QUERY, g_mixed[rows, pl.ds(0, D)].astype(f32))
        add(B_VALUE, g_mixed[rows, pl.ds(2 * D, D)].astype(f32))

    rows_loop(four)

    @pl.when(section == 1)
    def _():
        back.start()

    input_grad[...] = gxout[...]

    @pl.when(section == 0)
    def _():
        forth.wait_send()

    @pl.when(section == 1)
    def _():
        back.wait_send()


def layer_kernel_with_bias(tokens, places, cotangent, slopes, vec, *refs):
    wide = refs[SCRATCH_WIDE]
    wide[pl.ds(0, 1), pl.ds(0, D)] = vec[pl.ds(B_QUERY, 1), :]
    wide[pl.ds(0, 1), pl.ds(D, D)] = jnp.zeros((1, D), f32)
    wide[pl.ds(0, 1), pl.ds(2 * D, D)] = vec[pl.ds(B_VALUE, 1), :]
    layer_kernel(tokens, places, cotangent, slopes, vec, *refs)


SCRATCH_WIDE = 3 + 12 + 12


def layer(tokens, places, cotangent, slopes, vec, b_up, w_rows, w_down):
    def out(rows, columns, kind=bf16):
        return jax.ShapeDtypeStruct((rows, columns), kind)

    return pl.pallas_call(
        layer_kernel_with_bias,
        out_shape=(
            out(ROWS, D),
            out(ROWS, D),
            out(D, ROWS),
            out(D, ROWS),
            out(D, ROWS),
            out(FF, ROWS),
            out(ROWS, 3 * D),
            out(ROWS, D),
            out(ROWS, FF),
            out(ROWS, D),
            out(8, D, f32),
            out(8, FF, f32),
        ),
        in_specs=[VMEM, VMEM, VMEM, SMEM, VMEM, VMEM, ANY, ANY],
        out_specs=(VMEM,) * 12,
        scratch_shapes=[
            pltpu.VMEM((ROWS, D), bf16),
            pltpu.VMEM((ROWS, D), bf16),
            pltpu.VMEM((ROWS, D), bf16),
            pltpu.VMEM((D, 8192), bf16),
            pltpu.VMEM((FF, D), bf16),
            pltpu.VMEM((ROWS, D), f32),
            pltpu.VMEM((ROWS, 128), f32),
            pltpu.VMEM((ROWS, D), f32),
            pltpu.VMEM((ROWS, 128), f32),
            pltpu.VMEM((ROWS, 3 * D), bf16),
            pltpu.VMEM((2, BLOCK, BLOCK), f32),
            pltpu.VMEM((16, 2 * BLOCK, BLOCK), f32),
            pltpu.VMEM((8, 3 * D), f32),
            pltpu.VMEM((ROWS, D), f32),
            pltpu.VMEM((ROWS, FF), f32),
            pltpu.VMEM((ROWS, FF), bf16),
            pltpu.VMEM((ROWS, D), f32),
            pltpu.SemaphoreType.DMA((9,)),
            pltpu.SemaphoreType.DMA((2,)),
            pltpu.SemaphoreType.DMA((2,)),
        ],
        compiler_params=pltpu.CompilerParams(
            collective_id=1, has_side_effects=True, vmem_limit_bytes=60 * 2**20
        ),
        name="layer",
    )(tokens, places, cotangent, slopes, vec, b_up, w_rows, w_down)


KINDS = ((64, D), (16, FF), (16, 3 * D), (16, D))
SCATTER_COPIES = 4 * (2 + 6 + 6 + 1)


def scatter_kernel(*refs):
    lhs_in, rhs_in, outs = refs[0:4], refs[4:8], refs[8:12]
    lhs, rhs, own, ring_p, ring_q, last = [refs[12 + 4 * k : 16 + 4 * k] for k in range(6)]
    block, block_down, send, recv, load = refs[36:]
    at = Place()
    mail = Mail(send, recv)
    greet(at.neighbours())
    local = []
    for a in range(4):
        here, there = pl.ds(0, ROWS), pl.ds(ROWS, ROWS)
        mail.post(
            ("L", a),
            lhs_in[a].at[:, :, :, 1 - at.c],
            lhs[a].at[:, :, :, :, there],
            at.other_core(),
        )
        mail.post(("R", a), rhs_in[a], rhs[a].at[there, :], at.other_core())
        copies = (
            pltpu.make_async_copy(
                lhs_in[a].at[:, :, :, at.c], lhs[a].at[:, :, :, :, here], load.at[2 * a]
            ),
            pltpu.make_async_copy(rhs_in[a], rhs[a].at[here, :], load.at[2 * a + 1]),
        )
        for copy in copies:
            copy.start()
        local.append(copies)

    def ready(a):
        there = pl.ds(ROWS, ROWS)
        mail.take(("L", a), lhs[a].at[:, :, :, :, there], at.other_core())
        mail.take(("R", a), rhs[a].at[there, :], at.other_core())
        for copy in local[a]:
            copy.wait()

    def products(a, d):
        rows, width = KINDS[a]
        buffer = block_down if rows == 64 else block
        for r in range(2):
            for e in range(4):
                z, x = at.zx(d, e)
                buffer[pl.ds((r * 4 + e) * rows, rows), :] = lhs[a][at.half(r), z, x]

        @pl.loop(0, width // 512)
        def _(j):
            y = dot(buffer[...], rhs[a][:, cols(j, 512)])
            own[a][:, d, :, :, cols(j, 512)] = y.reshape(2, 4, rows, 512).astype(bf16)

    def total(a, dst, terms):
        @pl.loop(0, KINDS[a][1] // 512)
        def _(j):
            value = None
            for term in terms:
                piece = term[..., cols(j, 512)].astype(f32)
                value = piece if value is None else value + piece
            dst[..., cols(j, 512)] = value.astype(dst.dtype)

    right_p, left_p = at.at(1, 0), at.at(-1, 0)
    right_q, left_q = at.at(0, 1), at.at(0, -1)

    def post_p(a, k, r, d, device):
        mail.post(("P", a, k), own[a].at[r, d], ring_p[a].at[k], device)

    def take_p(a, k):
        mail.take(("P", a, k), ring_p[a].at[k], right_p)

    def post_q(a, k, r, e, device):
        mail.post(("Q", a, k), own[a].at[r, 0, e], ring_q[a].at[k], device)

    def take_q(a, k):
        mail.take(("Q", a, k), ring_q[a].at[k], right_q)

    def sum_into(a, dst, *terms):
        total(a, dst, (dst, *terms))

    for a in range(4):
        ready(a)
        products(a, 2)
        post_p(a, 0, 0, 2, right_p)
        post_p(a, 1, 1, 2, left_p)
        products(a, 1)
        post_p(a, 2, 1, 1, right_p)
        products(a, 3)
        post_p(a, 3, 0, 3, left_p)
    for a in range(4):
        take_p(a, 0)
        sum_into(a, own[a].at[0, 1], ring_p[a].at[0])
        post_p(a, 4, 0, 1, right_p)
        take_p(a, 1)
        sum_into(a, own[a].at[1, 3], ring_p[a].at[1])
        post_p(a, 5, 1, 3, left_p)
        products(a, 0)
    for a in range(4):
        for k in (2, 3, 4, 5):
            take_p(a, k)
        sum_into(a, own[a].at[0, 0], ring_p[a].at[4], ring_p[a].at[3])
        sum_into(a, own[a].at[1, 0], ring_p[a].at[2], ring_p[a].at[5])
        post_q(a, 0, 0, 2, right_q)
        post_q(a, 1, 1, 2, left_q)
        post_q(a, 2, 1, 1, right_q)
        post_q(a, 3, 0, 3, left_q)
    for a in range(4):
        take_q(a, 0)
        sum_into(a, own[a].at[0, 0, 1], ring_q[a].at[0])
        post_q(a, 4, 0, 1, right_q)
        take_q(a, 1)
        sum_into(a, own[a].at[1, 0, 3], ring_q[a].at[1])
        post_q(a, 5, 1, 3, left_q)
    for a in range(4):
        for k in (2, 3, 4, 5):
            take_q(a, k)
        sum_into(a, own[a].at[1, 0, 0], ring_q[a].at[2], ring_q[a].at[5])
        mail.post(("Y", a), own[a].at[1, 0, 0], last[a], at.over_y())
    for a in range(4):
        mail.take(("Y", a), last[a], at.over_y())
        terms = (own[a].at[0, 0, 0], ring_q[a].at[4], ring_q[a].at[3], last[a])
        total(a, outs[a], terms)
    mail.finish()


def scatter(lhs, rhs):
    def scratch(*lead):
        return [pltpu.VMEM((*lead, rows, width), bf16) for rows, width in KINDS]

    return pl.pallas_call(
        scatter_kernel,
        out_shape=tuple(jax.ShapeDtypeStruct(kind, f32) for kind in KINDS),
        in_specs=[ANY] * 8,
        out_specs=(VMEM,) * 4,
        scratch_shapes=[
            *[pltpu.VMEM((2, 4, 4, rows, 2 * ROWS), bf16) for rows, _ in KINDS],
            *[pltpu.VMEM((2 * ROWS, width), bf16) for _, width in KINDS],
            *scratch(2, 4, 4),
            *scratch(6, 4),
            *scratch(6),
            *scratch(),
            pltpu.VMEM((128, 2 * ROWS), bf16),
            pltpu.VMEM((512, 2 * ROWS), bf16),
            pltpu.SemaphoreType.DMA((SCATTER_COPIES,)),
            pltpu.SemaphoreType.DMA((SCATTER_COPIES,)),
            pltpu.SemaphoreType.DMA((8,)),
        ],
        compiler_params=pltpu.CompilerParams(
            collective_id=2, has_side_effects=True, vmem_limit_bytes=60 * 2**20
        ),
        name="scatter_gradients",
    )(*lhs, *rhs)


def body(
    tokens,
    positions,
    cotangent,
    w_qkv,
    b_query,
    b_value,
    w_out,
    b_out,
    w_up,
    b_up,
    w_down,
    b_down,
    gain_one,
    shift_one,
    gain_two,
    shift_two,
):
    small = (b_query, b_value, b_out, b_down, gain_one, shift_one, gain_two, shift_two)
    packed = jnp.concatenate([b_up, *small], axis=1)
    packed = jnp.pad(packed, ((0, 0), (0, 2048 - 192))).reshape(16, 128)
    ga, gb = gather(jnp.concatenate([w_qkv[0], w_out[0], w_up[0], packed], axis=1), w_down[0])
    ga, gb = ga.reshape(D, NA), gb.reshape(FF, D)
    vectors = ga[:, 8192:].reshape(64, 2048)[:, :192].astype(f32)
    bup_all = vectors[:, :64].reshape(1, FF)
    vec_all = vectors[:, 64:].reshape(64, 8, 16).transpose(1, 0, 2).reshape(8, D)
    slopes = 2.0 ** (-8.0 * jnp.arange(1, HEADS + 1, dtype=f32) / HEADS)
    results = layer(
        tokens.reshape(ROWS, D),
        positions.reshape(ROWS, 1),
        cotangent.reshape(ROWS, D),
        slopes,
        vec_all,
        jnp.broadcast_to(bup_all, (8, FF)),
        ga,
        gb,
    )
    layer_out, input_grad, n_t, a_t, n2_t, act_t, g_mixed, g_branch, g_up, g_y, g_vec, g_bup = results

    def shards(value, rows):
        return value.reshape(2, 4, 4, 2, rows, ROWS)

    down, up, qkv, out = scatter(
        (shards(act_t, 64), shards(n2_t, 16), shards(n_t, 16), shards(a_t, 16)),
        (g_y, g_up, g_mixed, g_branch),
    )
    own_vec = g_vec.reshape(8, 64, 16).transpose(1, 0, 2).reshape(64, 128)
    both = jnp.concatenate([g_bup[0].reshape(64, 64), own_vec], axis=1)
    mine = lax.psum_scatter(both, DP, scatter_dimension=0, tiled=True)
    gbu, rest = mine[:, :64], mine[:, 64:]
    gv = [rest[:, 16 * k : 16 * k + 16] for k in range(8)]
    return (
        layer_out.reshape(1, 2, BLOCK, D),
        input_grad.reshape(1, 2, BLOCK, D),
        qkv[None],
        gv[B_QUERY],
        gv[B_VALUE],
        out[None],
        gv[B_OUT],
        up[None],
        gbu,
        down[None],
        gv[B_DOWN],
        gv[G_ONE],
        gv[S_ONE],
        gv[G_TWO],
        gv[S_TWO],
    )


def solution(mesh):
    torus = Mesh(mesh.devices.reshape(2, 2, 4, 4, 2), AXES)
    rows, matrix, vector = P(None, DP, None), P("section", DP, None), P("section", DP)
    of_layer = P("section", None, DP, None)
    return jax.shard_map(
        body,
        mesh=torus,
        in_specs=(
            rows,
            P(None, DP),
            rows,
            matrix,
            vector,
            vector,
            matrix,
            vector,
            matrix,
            vector,
            matrix,
            vector,
            vector,
            vector,
            vector,
            vector,
        ),
        out_specs=(
            of_layer,
            of_layer,
            matrix,
            vector,
            vector,
            matrix,
            vector,
            matrix,
            vector,
            matrix,
            vector,
            vector,
            vector,
            vector,
            vector,
        ),
        check_vma=False,
    )
```

```python
from functools import partial

import jax
import jax.numpy as jnp
from jax import lax
from jax.experimental import pallas as pl
from jax.experimental.pallas import tpu as pltpu
from jax.sharding import Mesh
from jax.sharding import PartitionSpec as P

HEADS = 16
D = 1024
FF = 4096
ROWS = 256
BLOCK = 128
NA = 8192 + 128
AXES = ("section", "dp_0", "dp_1", "dp_2", "dp_3")
DP = AXES[1:]
MESH = pl.DeviceIdType.MESH
EPSILON = 1e-05
FAR = 1e30
ANY = pl.BlockSpec(memory_space=pl.ANY)
VMEM = pl.BlockSpec(memory_space=pltpu.VMEM)
SMEM = pl.BlockSpec(memory_space=pltpu.SMEM)
bf16 = jnp.bfloat16
f32 = jnp.float32


class Place:
    def __init__(self):
        self.s, self.yh, self.z, self.x, self.c = [lax.axis_index(a) for a in AXES]
        self.p = jnp.where(self.c == 0, self.z, self.x)
        self.q = jnp.where(self.c == 0, self.x, self.z)

    def zx(self, dp, dq):
        pp, qq = lax.rem(self.p + (dp + 4), 4), lax.rem(self.q + (dq + 4), 4)
        return jnp.where(self.c == 0, pp, qq), jnp.where(self.c == 0, qq, pp)

    def at(self, dp, dq):
        z, x = self.zx(dp, dq)
        return (self.s, self.yh, z, x, self.c)

    def half(self, r):
        return lax.rem(self.yh + r, 2)

    def over_y(self):
        return (self.s, 1 - self.yh, self.z, self.x, self.c)

    def other_core(self):
        return (self.s, self.yh, self.z, self.x, 1 - self.c)

    def neighbours(self):
        return (
            self.over_y(),
            self.other_core(),
            self.at(1, 0),
            self.at(-1, 0),
            self.at(0, 1),
            self.at(0, -1),
        )


def greet(devices):
    barrier = pltpu.get_barrier_semaphore()
    for device in devices:
        pl.semaphore_signal(barrier, inc=1, device_id=device, device_id_type=MESH)
    pl.semaphore_wait(barrier, len(devices))


class Mail:
    def __init__(self, send, recv):
        self.send, self.recv, self.sent, self.number = send, recv, [], {}

    def post(self, name, src, dst, device):
        k = self.number.setdefault(name, len(self.number))
        copy = pltpu.make_async_remote_copy(
            src_ref=src,
            dst_ref=dst,
            send_sem=self.send.at[k],
            recv_sem=self.recv.at[k],
            device_id=device,
            device_id_type=MESH,
        )
        copy.start()
        self.sent.append(copy)

    def take(self, name, dst, device):
        k = self.number[name]
        pltpu.make_async_remote_copy(
            src_ref=dst,
            dst_ref=dst,
            send_sem=self.send.at[k],
            recv_sem=self.recv.at[k],
            device_id=device,
            device_id_type=MESH,
        ).wait_recv()

    def finish(self):
        for copy in self.sent:
            copy.wait_send()


GATHER_COPIES = 2 * (1 + 6 + 24 + 32)


def gather_kernel(a_ref, b_ref, ga, gb, send, recv, own):
    at = Place()
    mail = Mail(send, recv)
    greet(at.neighbours())
    outs = (ga, gb)
    local = []
    z0, x0 = at.zx(0, 0)
    for t, (src, out) in enumerate(((a_ref, ga), (b_ref, gb))):
        copy = pltpu.make_async_copy(src, out.at[at.yh, z0, x0, at.c], own.at[t])
        copy.start()
        local.append(copy)

    def view(t, r, dp, dq, core=None):
        z, x = at.zx(dp, dq)
        return outs[t].at[at.half(r), z, x, at.c if core is None else core]

    def post(kind, t, r, dp, dq, device):
        mine = (r, dp, dq) == (0, 0, 0)
        src = (a_ref, b_ref)[t] if mine else view(t, r, dp, dq)
        mail.post((kind, t, r, dp, dq), src, view(t, r, dp, dq), device)

    def spread(r, dq, both=True):
        for t in (0, 1):
            post("PR", t, r, 0, dq, at.at(1, 0))
            post("PL", t, r, 0, dq, at.at(-1, 0))
        hand_over(r, 0, dq)

    def hand_over(r, dp, dq):
        for t in (0, 1):
            post("C", t, r, dp, dq, at.other_core())

    def take(kind, t, sent, got, device):
        mail.take((kind, t, *sent), view(t, *got), device)

    for t in (0, 1):
        post("Y", t, 0, 0, 0, at.over_y())
    for t in (0, 1):
        post("QR", t, 0, 0, 0, at.at(0, 1))
        post("QL", t, 0, 0, 0, at.at(0, -1))
    spread(0, 0)
    for t in (0, 1):
        take("Y", t, (0, 0, 0), (1, 0, 0), at.over_y())
        post("QR", t, 1, 0, 0, at.at(0, 1))
        post("QL", t, 1, 0, 0, at.at(0, -1))
    spread(1, 0)
    for t in (0, 1):
        take("QR", t, (0, 0, 0), (0, 0, -1), at.at(0, 1))
        post("QR2", t, 0, 0, -1, at.at(0, 1))
    spread(0, -1)
    for t in (0, 1):
        take("QL", t, (0, 0, 0), (0, 0, 1), at.at(0, 1))
    spread(0, 1)

    def pass_on(dq):
        for t in (0, 1):
            take("PR", t, (0, 0, dq), (0, -1, dq), at.at(1, 0))
            post("PR2", t, 0, -1, dq, at.at(1, 0))
        for t in (0, 1):
            take("PL", t, (1, 0, dq), (1, 1, dq), at.at(1, 0))
            post("PL2", t, 1, 1, dq, at.at(-1, 0))
        hand_over(0, -1, dq)
        hand_over(1, 1, dq)
        for t in (0, 1):
            take("PL", t, (0, 0, dq), (0, 1, dq), at.at(1, 0))
            take("PR", t, (1, 0, dq), (1, -1, dq), at.at(1, 0))
        hand_over(0, 1, dq)
        hand_over(1, -1, dq)

    for t in (0, 1):
        take("QL", t, (1, 0, 0), (1, 0, 1), at.at(0, 1))
        post("QL2", t, 1, 0, 1, at.at(0, -1))
    spread(1, 1)
    for t in (0, 1):
        take("QR", t, (1, 0, 0), (1, 0, -1), at.at(0, 1))
    spread(1, -1)
    pass_on(0)
    for t in (0, 1):
        take("QR2", t, (0, 0, -1), (0, 0, -2), at.at(0, 1))
    spread(0, 2)
    for t in (0, 1):
        take("QL2", t, (1, 0, 1), (1, 0, 2), at.at(0, 1))
    spread(1, 2)
    for dq in (-1, 1, 2):
        pass_on(dq)
    for dq in (0, -1, 1, 2):
        for t in (0, 1):
            take("PR2", t, (0, -1, dq), (0, -2, dq), at.at(1, 0))
            take("PL2", t, (1, 1, dq), (1, 2, dq), at.at(1, 0))
        hand_over(0, 2, dq)
        hand_over(1, 2, dq)
    for name in [n for n in mail.number if n[0] == "C"]:
        _, t, r, dp, dq = name
        mail.take(name, view(t, r, dq, dp, 1 - at.c), at.other_core())
    mail.finish()
    for copy in local:
        copy.wait()


def gather(a, b):
    return pl.pallas_call(
        gather_kernel,
        out_shape=(
            jax.ShapeDtypeStruct((2, 4, 4, 2, 16, NA), bf16),
            jax.ShapeDtypeStruct((2, 4, 4, 2, 64, D), bf16),
        ),
        in_specs=[ANY, ANY],
        out_specs=(ANY, ANY),
        scratch_shapes=[
            pltpu.SemaphoreType.DMA((GATHER_COPIES,)),
            pltpu.SemaphoreType.DMA((GATHER_COPIES,)),
            pltpu.SemaphoreType.DMA((2,)),
        ],
        compiler_params=pltpu.CompilerParams(collective_id=0, has_side_effects=True),
        name="gather_weights",
    )(a, b)


def dot(a, b, dims=((1,), (0,))):
    return lax.dot_general(a, b, (dims, ((), ())), preferred_element_type=f32)


NT = ((1,), (1,))
TN = ((0,), (0,))


def cols(j, width):
    return pl.ds(pl.multiple_of(j * width, width), width)


B_QUERY, B_VALUE, B_OUT, B_DOWN, G_ONE, S_ONE, G_TWO, S_TWO = range(8)


def layer_kernel(
    tokens,
    places,
    cotangent,
    slopes,
    vec,
    b_up,
    w_rows,
    w_down,
    layer_out,
    input_grad,
    n_t,
    a_t,
    n2_t,
    act_t,
    g_mixed,
    g_branch,
    g_upward,
    g_y,
    g_vec,
    xin,
    gyin,
    gxout,
    w1,
    w2,
    xhat1,
    rstd1,
    xhat2,
    rstd2,
    mixed,
    far,
    probs,
    wide,
    middle,
    gprime,
    act,
    grad,
    load,
    send,
    recv,
):
    section = lax.axis_index("section")
    loads = {}
    pieces = [("qkv", j * 1024, 1024) for j in range(3)]
    pieces += [("out", 3072, 1024)] + [("up", 4096 + j * 1024, 1024) for j in range(4)]
    for k, (name, at, width) in enumerate(pieces):
        copy = pltpu.make_async_copy(
            w_rows.at[:, pl.ds(at, width)], w1.at[:, pl.ds(at, width)], load.at[k]
        )
        copy.start()
        loads.setdefault(name, []).append(copy)
    copy = pltpu.make_async_copy(w_down, w2, load.at[len(pieces)])
    copy.start()
    loads["down"] = [copy]

    def loaded(name):
        for item in loads[name]:
            item.wait()

    other = {"section": 1 - section}
    greet((other,))
    forth = pltpu.make_async_remote_copy(
        src_ref=layer_out,
        dst_ref=xin,
        send_sem=send.at[0],
        recv_sem=recv.at[0],
        device_id=other,
        device_id_type=MESH,
    )
    back = pltpu.make_async_remote_copy(
        src_ref=gxout,
        dst_ref=gyin,
        send_sem=send.at[1],
        recv_sem=recv.at[1],
        device_id=other,
        device_id_type=MESH,
    )

    row = lax.broadcasted_iota(jnp.int32, (BLOCK, BLOCK), 0)
    col = lax.broadcasted_iota(jnp.int32, (BLOCK, BLOCK), 1)
    distance = row - col
    for b in range(2):
        allowed = (distance >= 0) & (distance <= places[pl.ds(b * BLOCK, BLOCK), :])
        far[b] = jnp.where(allowed, distance.astype(f32), FAR)
    low_lane = lax.broadcasted_iota(jnp.int32, (BLOCK, BLOCK), 1) < 64

    @pl.when(section == 0)
    def _():
        xin[...] = tokens[...]

    @pl.when(section == 1)
    def _():
        forth.wait_recv()
        gyin[...] = cotangent[...]

    chunk = 32

    def rows_loop(body):
        @pl.loop(0, ROWS // chunk)
        def _(i):
            body(pl.ds(pl.multiple_of(i * chunk, chunk), chunk))

    def norm_rows(rows, v, xhat, rstd, gain, shift):
        center = v - jnp.mean(v, axis=-1, keepdims=True)
        r = lax.rsqrt(jnp.mean(center * center, axis=-1, keepdims=True) + EPSILON)
        h = center * r
        xhat[rows, :] = h
        rstd[rows, :] = jnp.broadcast_to(r, (chunk, 128))
        return h * vec[pl.ds(gain, 1), :] + vec[pl.ds(shift, 1), :]

    def transpose_into(dst, src, width):
        @pl.loop(0, width // 256)
        def _(j):
            dst[cols(j, 256), :] = src[:, cols(j, 256)].T

    def one(rows):
        v = xin[rows, :].astype(f32)
        g_branch[rows, :] = norm_rows(rows, v, xhat1, rstd1, G_ONE, S_ONE).astype(bf16)

    rows_loop(one)
    transpose_into(n_t, g_branch, D)

    loaded("qkv")

    @pl.loop(0, 6)
    def _(j):
        y = dot(g_branch[...], w1[:, cols(j, 512)])
        mixed[:, cols(j, 512)] = (y + wide[pl.ds(0, 1), cols(j, 512)]).astype(bf16)

    def pair(value):
        zero = jnp.zeros_like(value)
        return jnp.concatenate(
            [jnp.where(low_lane, value, zero), jnp.where(low_lane, zero, value)], axis=0
        )

    def unpair(value):
        return jnp.where(low_lane, value[:BLOCK], value[BLOCK:])

    def slope_rows(hp):
        first = lax.broadcasted_iota(jnp.int32, (2 * BLOCK, 1), 0) < BLOCK
        return jnp.where(first, slopes[2 * hp], slopes[2 * hp + 1])

    def heads(ref, b, part, hp):
        at = pl.multiple_of(part * D + hp * 128, 128)
        return ref[pl.ds(b * BLOCK, BLOCK), pl.ds(at, 128)]

    @pl.loop(0, 8)
    def _(hp):
        for b in range(2):
            queries = pair(heads(mixed, b, 0, hp))
            scores = dot(queries, heads(mixed, b, 1, hp), NT) * 0.125
            gap = jnp.concatenate([far[b], far[b]], axis=0)
            scores = scores - slope_rows(hp) * gap
            e = jnp.exp(scores - jnp.max(scores, axis=-1, keepdims=True))
            p = e * (1.0 / jnp.sum(e, axis=-1, keepdims=True))
            probs[2 * hp + b] = p
            out = unpair(dot(p.astype(bf16), heads(mixed, b, 2, hp)))
            g_y[pl.ds(b * BLOCK, BLOCK), pl.ds(pl.multiple_of(hp * 128, 128), 128)] = (
                out.astype(bf16)
            )

    transpose_into(a_t, g_y, D)
    loaded("out")

    @pl.loop(0, 2)
    def _(j):
        y = dot(g_y[...], w1[:, pl.ds(pl.multiple_of(3072 + j * 512, 512), 512)])
        middle[:, cols(j, 512)] = (
            xin[:, cols(j, 512)].astype(f32) + y + vec[pl.ds(B_OUT, 1), cols(j, 512)]
        )

    def two(rows):
        g_branch[rows, :] = norm_rows(
            rows, middle[rows, :], xhat2, rstd2, G_TWO, S_TWO
        ).astype(bf16)

    rows_loop(two)
    transpose_into(n2_t, g_branch, D)
    loaded("up")

    @pl.loop(0, 8)
    def _(j):
        y = dot(g_branch[...], w1[:, pl.ds(pl.multiple_of(4096 + j * 512, 512), 512)])
        u = y + b_up[pl.ds(0, 1), cols(j, 512)]
        c = 0.7978845608028654
        uu = u * u
        t = jnp.tanh(c * (u + 0.044715 * u * uu))
        half = 0.5 * (1.0 + t)
        a = (u * half).astype(bf16)
        act[:, cols(j, 512)] = a
        act_t[cols(j, 512), :] = a.T
        gprime[:, cols(j, 512)] = half + 0.5 * u * (1.0 - t * t) * (
            c * (1.0 + (3 * 0.044715) * uu)
        )

    loaded("down")

    @pl.loop(0, 2)
    def _(j):
        y = dot(act[...], w2[:, cols(j, 512)])
        y = middle[:, cols(j, 512)] + y + vec[pl.ds(B_DOWN, 1), cols(j, 512)]
        layer_out[:, cols(j, 512)] = y.astype(bf16)

    @pl.when(section == 0)
    def _():
        forth.start()
        back.wait_recv()

    g_y[...] = gyin[...]
    g_vec[...] = jnp.zeros_like(g_vec)

    @pl.loop(0, 8)
    def _(j):
        g = dot(g_y[...], w2[cols(j, 512), :], NT)
        g = (g * gprime[:, cols(j, 512)]).astype(bf16)
        g_upward[:, cols(j, 512)] = g
        g_vec[pl.ds(8 + j // 2, 1), cols(j % 2, 512)] = jnp.sum(
            g.astype(f32), axis=0, keepdims=True
        )

    @pl.loop(0, 4)
    def _(j):
        grad[:, cols(j, 256)] = dot(g_upward[...], w1[cols(j, 256), pl.ds(4096, 4096)], NT)

    def add(index, value):
        g_vec[pl.ds(index, 1), :] = g_vec[pl.ds(index, 1), :] + jnp.sum(
            value, axis=0, keepdims=True
        )

    def norm_back(rows, xhat, rstd, gain, shift):
        dy = grad[rows, :]
        h = xhat[rows, :]
        add(gain, dy * h)
        add(shift, dy)
        dh = dy * vec[pl.ds(gain, 1), :]
        m1 = jnp.mean(dh, axis=-1, keepdims=True)
        m2 = jnp.mean(dh * h, axis=-1, keepdims=True)
        return rstd[rows, pl.ds(0, 1)] * (dh - m1 - h * m2)

    def three(rows):
        gy = g_y[rows, :].astype(f32)
        gm = gy + norm_back(rows, xhat2, rstd2, G_TWO, S_TWO)
        add(B_DOWN, gy)
        middle[rows, :] = gm
        low = gm.astype(bf16)
        g_branch[rows, :] = low
        add(B_OUT, low.astype(f32))

    rows_loop(three)

    @pl.loop(0, 4)
    def _(j):
        y = dot(g_branch[...], w1[cols(j, 256), pl.ds(3072, 1024)], NT)
        act[:, cols(j, 256)] = y.astype(bf16)

    @pl.loop(0, 8)
    def _(hp):
        for b in range(2):
            queries = pair(heads(mixed, b, 0, hp))
            keys, values = heads(mixed, b, 1, hp), heads(mixed, b, 2, hp)
            da = pair(heads(act, b, 0, hp))
            p = probs[2 * hp + b]
            dv = dot(p.astype(bf16), da, TN)
            dp = dot(da, values, NT)
            delta = jnp.sum(p * dp, axis=-1, keepdims=True)
            ds = (p * (dp - delta)).astype(bf16)
            dq = unpair(dot(ds, keys)) * 0.125
            dk = dot(ds, queries, TN) * 0.125
            for part, value in enumerate((dq, dk, dv)):
                at = pl.multiple_of(part * D + hp * 128, 128)
                g_mixed[pl.ds(b * BLOCK, BLOCK), pl.ds(at, 128)] = value.astype(bf16)

    @pl.loop(0, 4)
    def _(j):
        grad[:, cols(j, 256)] = dot(g_mixed[...], w1[cols(j, 256), pl.ds(0, 3072)], NT)

    def four(rows):
        gx = middle[rows, :] + norm_back(rows, xhat1, rstd1, G_ONE, S_ONE)
        gxout[rows, :] = gx.astype(bf16)
        add(B_QUERY, g_mixed[rows, pl.ds(0, D)].astype(f32))
        add(B_VALUE, g_mixed[rows, pl.ds(2 * D, D)].astype(f32))

    rows_loop(four)

    @pl.when(section == 1)
    def _():
        back.start()

    input_grad[...] = gxout[...]

    @pl.when(section == 0)
    def _():
        forth.wait_send()

    @pl.when(section == 1)
    def _():
        back.wait_send()


def layer_kernel_with_bias(tokens, places, cotangent, slopes, vec, *refs):
    wide = refs[SCRATCH_WIDE]
    wide[pl.ds(0, 1), pl.ds(0, D)] = vec[pl.ds(B_QUERY, 1), :]
    wide[pl.ds(0, 1), pl.ds(D, D)] = jnp.zeros((1, D), f32)
    wide[pl.ds(0, 1), pl.ds(2 * D, D)] = vec[pl.ds(B_VALUE, 1), :]
    layer_kernel(tokens, places, cotangent, slopes, vec, *refs)


SCRATCH_WIDE = 3 + 11 + 12


def layer(tokens, places, cotangent, slopes, vec, b_up, w_rows, w_down):
    def out(rows, columns, kind=bf16):
        return jax.ShapeDtypeStruct((rows, columns), kind)

    return pl.pallas_call(
        layer_kernel_with_bias,
        out_shape=(
            out(ROWS, D),
            out(ROWS, D),
            out(D, ROWS),
            out(D, ROWS),
            out(D, ROWS),
            out(FF, ROWS),
            out(ROWS, 3 * D),
            out(ROWS, D),
            out(ROWS, FF),
            out(ROWS, D),
            out(16, D, f32),
        ),
        in_specs=[VMEM, VMEM, VMEM, SMEM, VMEM, VMEM, ANY, ANY],
        out_specs=(VMEM,) * 11,
        scratch_shapes=[
            pltpu.VMEM((ROWS, D), bf16),
            pltpu.VMEM((ROWS, D), bf16),
            pltpu.VMEM((ROWS, D), bf16),
            pltpu.VMEM((D, 8192), bf16),
            pltpu.VMEM((FF, D), bf16),
            pltpu.VMEM((ROWS, D), f32),
            pltpu.VMEM((ROWS, 128), f32),
            pltpu.VMEM((ROWS, D), f32),
            pltpu.VMEM((ROWS, 128), f32),
            pltpu.VMEM((ROWS, 3 * D), bf16),
            pltpu.VMEM((2, BLOCK, BLOCK), f32),
            pltpu.VMEM((16, 2 * BLOCK, BLOCK), f32),
            pltpu.VMEM((8, 3 * D), f32),
            pltpu.VMEM((ROWS, D), f32),
            pltpu.VMEM((ROWS, FF), f32),
            pltpu.VMEM((ROWS, FF), bf16),
            pltpu.VMEM((ROWS, D), f32),
            pltpu.SemaphoreType.DMA((9,)),
            pltpu.SemaphoreType.DMA((2,)),
            pltpu.SemaphoreType.DMA((2,)),
        ],
        compiler_params=pltpu.CompilerParams(
            collective_id=1, has_side_effects=True, vmem_limit_bytes=60 * 2**20
        ),
        name="layer",
    )(tokens, places, cotangent, slopes, vec, b_up, w_rows, w_down)


KINDS = ((64, D), (16, FF), (16, 3 * D), (16, D))
SCATTER_COPIES = 4 * (2 + 6 + 6 + 1) + 6


def scatter_kernel(*refs):
    lhs_in, rhs_in, vec_in, outs, vec_out = refs[0:4], refs[4:8], refs[8], refs[9:13], refs[13]
    lhs, rhs, own, ring_p, ring_q, last = [refs[14 + 4 * k : 18 + 4 * k] for k in range(6)]
    block, block_down, vec_sum, vec_got, send, recv, load = refs[38:]
    at = Place()
    mail = Mail(send, recv)
    greet(at.neighbours())
    even_p, even_q = 1 - 2 * lax.rem(at.p, 2), 1 - 2 * lax.rem(at.q, 2)
    partners = (
        at.other_core(),
        at.at(even_p, 0),
        at.at(-even_p, 0),
        at.at(0, even_q),
        at.at(0, -even_q),
        at.over_y(),
    )

    def post_vec(k):
        mail.post(("V", k), vec_sum.at[k], vec_got.at[k], partners[k])

    def take_vec(k):
        mail.take(("V", k), vec_got.at[k], partners[k])
        vec_sum[k + 1] = vec_sum[k] + vec_got[k]

    vec_sum[0] = vec_in[...]
    post_vec(0)
    local = []
    for a in range(4):
        here, there = pl.ds(0, ROWS), pl.ds(ROWS, ROWS)
        mail.post(
            ("L", a),
            lhs_in[a].at[:, :, :, 1 - at.c],
            lhs[a].at[:, :, :, :, there],
            at.other_core(),
        )
        mail.post(("R", a), rhs_in[a], rhs[a].at[there, :], at.other_core())
        copies = (
            pltpu.make_async_copy(
                lhs_in[a].at[:, :, :, at.c], lhs[a].at[:, :, :, :, here], load.at[2 * a]
            ),
            pltpu.make_async_copy(rhs_in[a], rhs[a].at[here, :], load.at[2 * a + 1]),
        )
        for copy in copies:
            copy.start()
        local.append(copies)

    def ready(a):
        there = pl.ds(ROWS, ROWS)
        mail.take(("L", a), lhs[a].at[:, :, :, :, there], at.other_core())
        mail.take(("R", a), rhs[a].at[there, :], at.other_core())
        if a == 0:
            take_vec(0)
            post_vec(1)
        for copy in local[a]:
            copy.wait()

    def products(a, d):
        rows, width = KINDS[a]
        buffer = block_down if rows == 64 else block
        for r in range(2):
            for e in range(4):
                z, x = at.zx(d, e)
                buffer[pl.ds((r * 4 + e) * rows, rows), :] = lhs[a][at.half(r), z, x]

        @pl.loop(0, width // 512)
        def _(j):
            y = dot(buffer[...], rhs[a][:, cols(j, 512)])
            own[a][:, d, :, :, cols(j, 512)] = y.reshape(2, 4, rows, 512).astype(bf16)

    def total(a, dst, terms):
        @pl.loop(0, KINDS[a][1] // 512)
        def _(j):
            value = None
            for term in terms:
                piece = term[..., cols(j, 512)].astype(f32)
                value = piece if value is None else value + piece
            dst[..., cols(j, 512)] = value.astype(dst.dtype)

    right_p, left_p = at.at(1, 0), at.at(-1, 0)
    right_q, left_q = at.at(0, 1), at.at(0, -1)

    def post_p(a, k, r, d, device):
        mail.post(("P", a, k), own[a].at[r, d], ring_p[a].at[k], device)

    def take_p(a, k):
        mail.take(("P", a, k), ring_p[a].at[k], right_p)

    def post_q(a, k, r, e, device):
        mail.post(("Q", a, k), own[a].at[r, 0, e], ring_q[a].at[k], device)

    def take_q(a, k):
        mail.take(("Q", a, k), ring_q[a].at[k], right_q)

    def sum_into(a, dst, *terms):
        total(a, dst, (dst, *terms))

    for a in range(4):
        ready(a)
        products(a, 2)
        post_p(a, 0, 0, 2, right_p)
        post_p(a, 1, 1, 2, left_p)
        products(a, 1)
        post_p(a, 2, 1, 1, right_p)
        products(a, 3)
        post_p(a, 3, 0, 3, left_p)
    for a in range(4):
        take_p(a, 0)
        sum_into(a, own[a].at[0, 1], ring_p[a].at[0])
        post_p(a, 4, 0, 1, right_p)
        take_p(a, 1)
        sum_into(a, own[a].at[1, 3], ring_p[a].at[1])
        post_p(a, 5, 1, 3, left_p)
        take_vec(a + 1)
        post_vec(a + 2)
        products(a, 0)
    for a in range(4):
        for k in (2, 3, 4, 5):
            take_p(a, k)
        sum_into(a, own[a].at[0, 0], ring_p[a].at[4], ring_p[a].at[3])
        sum_into(a, own[a].at[1, 0], ring_p[a].at[2], ring_p[a].at[5])
        post_q(a, 0, 0, 2, right_q)
        post_q(a, 1, 1, 2, left_q)
        post_q(a, 2, 1, 1, right_q)
        post_q(a, 3, 0, 3, left_q)
    for a in range(4):
        take_q(a, 0)
        sum_into(a, own[a].at[0, 0, 1], ring_q[a].at[0])
        post_q(a, 4, 0, 1, right_q)
        take_q(a, 1)
        sum_into(a, own[a].at[1, 0, 3], ring_q[a].at[1])
        post_q(a, 5, 1, 3, left_q)
    for a in range(4):
        for k in (2, 3, 4, 5):
            take_q(a, k)
        sum_into(a, own[a].at[1, 0, 0], ring_q[a].at[2], ring_q[a].at[5])
        mail.post(("Y", a), own[a].at[1, 0, 0], last[a], at.over_y())
    take_vec(5)
    vec_out[...] = vec_sum[6]
    for a in range(4):
        mail.take(("Y", a), last[a], at.over_y())
        terms = (own[a].at[0, 0, 0], ring_q[a].at[4], ring_q[a].at[3], last[a])
        total(a, outs[a], terms)
    mail.finish()


def scatter(lhs, rhs, vec):
    def scratch(*lead):
        return [pltpu.VMEM((*lead, rows, width), bf16) for rows, width in KINDS]

    return pl.pallas_call(
        scatter_kernel,
        out_shape=tuple(jax.ShapeDtypeStruct(kind, f32) for kind in (*KINDS, (16, D))),
        in_specs=[*[ANY] * 8, VMEM],
        out_specs=(VMEM,) * 5,
        scratch_shapes=[
            *[pltpu.VMEM((2, 4, 4, rows, 2 * ROWS), bf16) for rows, _ in KINDS],
            *[pltpu.VMEM((2 * ROWS, width), bf16) for _, width in KINDS],
            *scratch(2, 4, 4),
            *scratch(6, 4),
            *scratch(6),
            *scratch(),
            pltpu.VMEM((128, 2 * ROWS), bf16),
            pltpu.VMEM((512, 2 * ROWS), bf16),
            pltpu.VMEM((7, 16, D), f32),
            pltpu.VMEM((6, 16, D), f32),
            pltpu.SemaphoreType.DMA((SCATTER_COPIES,)),
            pltpu.SemaphoreType.DMA((SCATTER_COPIES,)),
            pltpu.SemaphoreType.DMA((8,)),
        ],
        compiler_params=pltpu.CompilerParams(
            collective_id=2, has_side_effects=True, vmem_limit_bytes=60 * 2**20
        ),
        name="scatter_gradients",
    )(*lhs, *rhs, vec)


def body(
    tokens,
    positions,
    cotangent,
    w_qkv,
    b_query,
    b_value,
    w_out,
    b_out,
    w_up,
    b_up,
    w_down,
    b_down,
    gain_one,
    shift_one,
    gain_two,
    shift_two,
):
    small = (b_query, b_value, b_out, b_down, gain_one, shift_one, gain_two, shift_two)
    packed = jnp.concatenate([b_up, *small], axis=1)
    packed = jnp.pad(packed, ((0, 0), (0, 2048 - 192))).reshape(16, 128)
    ga, gb = gather(jnp.concatenate([w_qkv[0], w_out[0], w_up[0], packed], axis=1), w_down[0])
    ga, gb = ga.reshape(D, NA), gb.reshape(FF, D)
    vectors = ga[:, 8192:].reshape(64, 2048)[:, :192].astype(f32)
    bup_all = vectors[:, :64].reshape(1, FF)
    vec_all = vectors[:, 64:].reshape(64, 8, 16).transpose(1, 0, 2).reshape(8, D)
    slopes = 2.0 ** (-8.0 * jnp.arange(1, HEADS + 1, dtype=f32) / HEADS)
    results = layer(
        tokens.reshape(ROWS, D),
        positions.reshape(ROWS, 1),
        cotangent.reshape(ROWS, D),
        slopes,
        vec_all,
        jnp.broadcast_to(bup_all, (8, FF)),
        ga,
        gb,
    )
    layer_out, input_grad, n_t, a_t, n2_t, act_t, g_mixed, g_branch, g_up, g_y, g_vec = results

    def shards(value, rows):
        return value.reshape(2, 4, 4, 2, rows, ROWS)

    down, up, qkv, out, sums = scatter(
        (shards(act_t, 64), shards(n2_t, 16), shards(n_t, 16), shards(a_t, 16)),
        (g_y, g_up, g_mixed, g_branch),
        g_vec,
    )
    index = lax.axis_index(DP)
    rest = lax.dynamic_slice(sums, (0, index * 16), (8, 16))
    gbu = lax.dynamic_slice(sums, (8 + index // 16, index % 16 * 64), (1, 64))
    gv = [rest[k : k + 1] for k in range(8)]
    return (
        layer_out.reshape(1, 2, BLOCK, D),
        input_grad.reshape(1, 2, BLOCK, D),
        qkv[None],
        gv[B_QUERY],
        gv[B_VALUE],
        out[None],
        gv[B_OUT],
        up[None],
        gbu,
        down[None],
        gv[B_DOWN],
        gv[G_ONE],
        gv[S_ONE],
        gv[G_TWO],
        gv[S_TWO],
    )


def solution(mesh):
    torus = Mesh(mesh.devices.reshape(2, 2, 4, 4, 2), AXES)
    rows, matrix, vector = P(None, DP, None), P("section", DP, None), P("section", DP)
    of_layer = P("section", None, DP, None)
    return jax.shard_map(
        body,
        mesh=torus,
        in_specs=(
            rows,
            P(None, DP),
            rows,
            matrix,
            vector,
            vector,
            matrix,
            vector,
            matrix,
            vector,
            matrix,
            vector,
            vector,
            vector,
            vector,
            vector,
        ),
        out_specs=(
            of_layer,
            of_layer,
            matrix,
            vector,
            vector,
            matrix,
            vector,
            matrix,
            vector,
            matrix,
            vector,
            vector,
            vector,
            vector,
            vector,
        ),
        check_vma=False,
    )
```

```python
import jax
import jax.numpy as jnp
from jax import lax
from jax.experimental import pallas as pl
from jax.experimental.pallas import tpu as pltpu
from jax.sharding import Mesh
from jax.sharding import PartitionSpec as P

HEADS = 16
D = 1024
FF = 4096
ROWS = 256
BLOCK = 128
QKV0, OUT0, UP0, NA = 128, 3200, 4224, 8320
AXES = ("section", "dp_0", "dp_1", "dp_2", "dp_3")
DP = AXES[1:]
MESH = pl.DeviceIdType.MESH
EPSILON = 1e-05
FAR = 1e30
ANY = pl.BlockSpec(memory_space=pl.ANY)
VMEM = pl.BlockSpec(memory_space=pltpu.VMEM)
SMEM = pl.BlockSpec(memory_space=pltpu.SMEM)
bf16 = jnp.bfloat16
f32 = jnp.float32


class Place:
    def __init__(self):
        self.s, self.yh, self.z, self.x, self.c = [lax.axis_index(a) for a in AXES]
        self.p = jnp.where(self.c == 0, self.z, self.x)
        self.q = jnp.where(self.c == 0, self.x, self.z)

    def zx(self, dp, dq):
        pp, qq = lax.rem(self.p + (dp + 4), 4), lax.rem(self.q + (dq + 4), 4)
        return jnp.where(self.c == 0, pp, qq), jnp.where(self.c == 0, qq, pp)

    def at(self, dp, dq):
        z, x = self.zx(dp, dq)
        return (self.s, self.yh, z, x, self.c)

    def half(self, r):
        return lax.rem(self.yh + r, 2)

    def over_y(self):
        return (self.s, 1 - self.yh, self.z, self.x, self.c)

    def other_core(self):
        return (self.s, self.yh, self.z, self.x, 1 - self.c)

    def neighbours(self):
        return (
            self.over_y(),
            self.other_core(),
            self.at(1, 0),
            self.at(-1, 0),
            self.at(0, 1),
            self.at(0, -1),
        )


def greet(devices):
    barrier = pltpu.get_barrier_semaphore()
    for device in devices:
        pl.semaphore_signal(barrier, inc=1, device_id=device, device_id_type=MESH)
    pl.semaphore_wait(barrier, len(devices))


class Mail:
    def __init__(self, send, recv):
        self.send, self.recv, self.sent, self.number = send, recv, {}, {}

    def post(self, name, src, dst, device):
        self.number.setdefault(name, len(self.number))
        self.sent[name] = (src, dst, device)
        self.copy(name).start()

    def copy(self, name):
        src, dst, device = self.sent[name]
        k = self.number[name]
        return pltpu.make_async_remote_copy(
            src_ref=src() if callable(src) else src,
            dst_ref=dst() if callable(dst) else dst,
            send_sem=self.send.at[k],
            recv_sem=self.recv.at[k],
            device_id=device,
            device_id_type=MESH,
        )

    def take(self, name, dst, device):
        k = self.number[name]
        pltpu.make_async_remote_copy(
            src_ref=dst,
            dst_ref=dst,
            send_sem=self.send.at[k],
            recv_sem=self.recv.at[k],
            device_id=device,
            device_id_type=MESH,
        ).wait_recv()

    def finish(self, names):
        for name in names:
            self.copy(name).wait_send()


def dot(a, b, dims=((1,), (0,))):
    return lax.dot_general(a, b, (dims, ((), ())), preferred_element_type=f32)


NT = ((1,), (1,))
TN = ((0,), (0,))


def cols(j, width, base=0):
    return pl.ds(pl.multiple_of(base + j * width, 128), width)


B_QUERY, B_VALUE, B_OUT, B_DOWN, G_ONE, S_ONE, G_TWO, S_TWO = range(8)
DOWN, UP, QKV, OUT = range(4)
KINDS = ((64, D, None), (16, FF, UP0), (16, 3 * D, QKV0), (16, D, OUT0))
COPIES = 3 * 63 + 4 * (2 + 6 + 6 + 1) + 6 + 2
RING_P, RING_Q, LAST = 32, 56, 62


def step_kernel(
    tokens,
    positions,
    cotangent,
    vec_tile,
    in_qkv,
    in_out,
    in_up,
    in_down,
    layer_out,
    input_grad,
    out_down,
    out_up,
    out_qkv,
    out_out,
    vec_out,
    w1,
    w2,
    xin,
    gyin,
    vec,
    b_up,
    b_qkv,
    xhat1,
    rstd1,
    xhat2,
    rstd2,
    mixed,
    far,
    probs,
    middle,
    gprime,
    act,
    grad,
    act_t,
    n2_t,
    n_t,
    a_t,
    l_down,
    l_up,
    l_qkv,
    l_out,
    r_down,
    r_up,
    r_qkv,
    r_out,
    block,
    block_down,
    vec_sum,
    vec_got,
    send,
    recv,
    load,
    *credits,
):
    at = Place()
    mail = Mail(send, recv)
    section = at.s
    first_section, second_section = section == 0, section == 1
    over_section = (1 - at.s, at.yh, at.z, at.x, at.c)
    my_index = ((at.yh * 4 + at.z) * 4 + at.x) * 2 + at.c
    right_p, left_p, right_q, left_q = at.at(1, 0), at.at(-1, 0), at.at(0, 1), at.at(0, -1)

    def shard_rows(index, rows):
        return pl.ds(pl.multiple_of(index * rows, rows), rows)

    here = shard_rows(my_index, 16)
    placing = [
        pltpu.make_async_copy(vec_tile, w1.at[here, pl.ds(0, 128)], load.at[0]),
        pltpu.make_async_copy(in_qkv, w1.at[here, pl.ds(QKV0, 3 * D)], load.at[1]),
        pltpu.make_async_copy(in_out, w1.at[here, pl.ds(OUT0, D)], load.at[2]),
        pltpu.make_async_copy(in_up, w1.at[here, pl.ds(UP0, FF)], load.at[3]),
        pltpu.make_async_copy(in_down, w2.at[shard_rows(my_index, 64), :], load.at[4]),
    ]
    for copy in placing:
        copy.start()
    greet((*at.neighbours(), over_section))


    def view(t, r, dp, dq, core=None):
        z, x = at.zx(dp, dq)
        index = ((at.half(r) * 4 + z) * 4 + x) * 2 + (at.c if core is None else core)
        if t == 2:
            return w2.at[shard_rows(index, 64), :]
        return w1.at[shard_rows(index, 16), (pl.ds(0, OUT0), pl.ds(OUT0, NA - OUT0))[t]]

    def post(kind, t, r, dp, dq, device):
        v = view(t, r, dp, dq)
        mail.post((kind, t, r, dp, dq), v, v, device)

    def take(kind, t, sent, got):
        mail.take((kind, t, *sent), view(t, *got), right_p)

    def hand_over(t, r, dp, dq):
        post("C", t, r, dp, dq, at.other_core())

    def spread(t, r, dq):
        post("PR", t, r, 0, dq, right_p)
        post("PL", t, r, 0, dq, left_p)
        hand_over(t, r, 0, dq)

    def pass_on(t, dq):
        take("PR", t, (0, 0, dq), (0, -1, dq))
        post("PR2", t, 0, -1, dq, right_p)
        take("PL", t, (1, 0, dq), (1, 1, dq))
        post("PL2", t, 1, 1, dq, left_p)
        hand_over(t, 0, -1, dq)
        hand_over(t, 1, 1, dq)
        take("PL", t, (0, 0, dq), (0, 1, dq))
        take("PR", t, (1, 0, dq), (1, -1, dq))
        hand_over(t, 0, 1, dq)
        hand_over(t, 1, -1, dq)

    def gather_steps(t):
        def s0():
            for copy in {0: placing[:2], 1: placing[2:4], 2: placing[4:]}[t]:
                copy.wait()
            post("Y", t, 0, 0, 0, at.over_y())
            post("QR", t, 0, 0, 0, right_q)
            post("QL", t, 0, 0, 0, left_q)
            spread(t, 0, 0)

        def s1():
            take("Y", t, (0, 0, 0), (1, 0, 0))
            post("QR", t, 1, 0, 0, right_q)
            post("QL", t, 1, 0, 0, left_q)
            spread(t, 1, 0)

        def s2():
            take("QR", t, (0, 0, 0), (0, 0, -1))
            post("QR2", t, 0, 0, -1, right_q)
            spread(t, 0, -1)
            take("QL", t, (0, 0, 0), (0, 0, 1))
            spread(t, 0, 1)

        def s3():
            take("QL", t, (1, 0, 0), (1, 0, 1))
            post("QL2", t, 1, 0, 1, left_q)
            spread(t, 1, 1)
            take("QR", t, (1, 0, 0), (1, 0, -1))
            spread(t, 1, -1)

        def s4():
            pass_on(t, 0)

        def s5():
            take("QR2", t, (0, 0, -1), (0, 0, -2))
            spread(t, 0, 2)
            take("QL2", t, (1, 0, 1), (1, 0, 2))
            spread(t, 1, 2)

        def s9():
            for dq in (0, -1, 1, 2):
                take("PR2", t, (0, -1, dq), (0, -2, dq))
                take("PL2", t, (1, 1, dq), (1, 2, dq))
                hand_over(t, 0, 2, dq)
                hand_over(t, 1, 2, dq)

        def s10():
            for r in range(2):
                for dp in (0, -1, 1, 2):
                    for dq in (0, -1, 1, 2):
                        name = ("C", t, r, dp, dq)
                        mail.take(name, view(t, r, dq, dp, 1 - at.c), at.other_core())

        passing = [lambda dq=dq: pass_on(t, dq) for dq in (-1, 1, 2)]
        return [s0, s1, s2, s3, s4, s5, *passing, s9, s10]


    chunk = 32

    def rows_loop(body):
        @pl.loop(0, ROWS // chunk)
        def _(i):
            body(pl.ds(pl.multiple_of(i * chunk, chunk), chunk))

    g_y, g_branch = r_down.at[pl.ds(0, ROWS), :], r_out.at[pl.ds(0, ROWS), :]
    g_upward, g_mixed = r_up.at[pl.ds(0, ROWS), :], r_qkv.at[pl.ds(0, ROWS), :]
    normed, attended = g_branch, g_y

    row = lax.broadcasted_iota(jnp.int32, (BLOCK, BLOCK), 0)
    col = lax.broadcasted_iota(jnp.int32, (BLOCK, BLOCK), 1)
    low_lane = col < 64

    def make_far():
        distance = col - row
        for b in range(2):
            allowed = (distance >= 0) & (distance <= positions[pl.ds(b, 1), :])
            far[b] = jnp.where(allowed, distance.astype(f32), FAR).T

    def unpack_vectors():
        for j in range(8):
            tiles = [w1[pl.ds((8 * j + i) * 16, 16), pl.ds(0, 128)].astype(f32) for i in range(8)]
            pairs = [tiles[2 * i] + tiles[2 * i + 1] for i in range(4)]
            for i in range(4):
                b_up[:, pl.ds((4 * j + i) * 128, 128)] = pairs[i][8:16]
            vec[:, pl.ds(j * 128, 128)] = ((pairs[0] + pairs[1]) + (pairs[2] + pairs[3]))[0:8]
        b_qkv[pl.ds(0, 1), pl.ds(0, D)] = vec[pl.ds(B_QUERY, 1), :]
        b_qkv[pl.ds(0, 1), pl.ds(D, D)] = jnp.zeros((1, D), f32)
        b_qkv[pl.ds(0, 1), pl.ds(2 * D, D)] = vec[pl.ds(B_VALUE, 1), :]

    def norm_rows(rows, v, xhat, rstd, gain, shift):
        center = v - jnp.mean(v, axis=-1, keepdims=True)
        r = lax.rsqrt(jnp.mean(center * center, axis=-1, keepdims=True) + EPSILON)
        h = center * r
        xhat[rows, :] = h
        rstd[rows, :] = jnp.broadcast_to(r, (chunk, 128))
        return h * vec[pl.ds(gain, 1), :] + vec[pl.ds(shift, 1), :]

    def transpose_into(dst, src):
        @pl.loop(0, D // 256)
        def _(j):
            dst[pl.ds(j * 8, 8)] = src[:, cols(j, 256)].T.reshape(8, 2, 16, ROWS)

    def post_lhs(a):
        mail.post(("L", a), lhs_t[a].at[:, 1 - at.c], lhs_got[a], at.other_core())

    lhs_t, lhs_got = (act_t, n2_t, n_t, a_t), (l_down, l_up, l_qkv, l_out)
    rhs = (r_down, r_up, r_qkv, r_out)

    def norm_one():
        def one(rows):
            v = xin[rows, :].astype(f32)
            normed[rows, :] = norm_rows(rows, v, xhat1, rstd1, G_ONE, S_ONE).astype(bf16)

        rows_loop(one)

    def project(lo, hi):
        @pl.loop(0, hi - lo)
        def _(i):
            j = i + lo
            y = dot(normed[...], w1[:, cols(j, 512, QKV0)])
            mixed[:, cols(j, 512)] = (y + b_qkv[pl.ds(0, 1), cols(j, 512)]).astype(bf16)

    def pair(value):
        zero = jnp.zeros_like(value)
        return jnp.concatenate(
            [jnp.where(low_lane, value, zero), jnp.where(low_lane, zero, value)], axis=0
        )

    def unpair(value):
        return jnp.where(low_lane, value[:BLOCK], value[BLOCK:])

    def slope_rows(hp):
        first = lax.broadcasted_iota(jnp.int32, (2 * BLOCK, 1), 0) < BLOCK
        h = ((2 * hp + 2) - first.astype(jnp.int32)).astype(f32)
        return jnp.exp(h * (-0.5 * 0.6931471805599453))

    def heads(ref, b, part, hp):
        return ref[pl.ds(b * BLOCK, BLOCK), cols(hp, 128, part * D)]

    def attend(lo, hi):
        @pl.loop(0, hi - lo)
        def _(i):
            hp = i + lo
            slope = slope_rows(hp)
            for b in range(2):
                queries = pair(heads(mixed, b, 0, hp))
                scores = dot(queries, heads(mixed, b, 1, hp), NT) * 0.125
                gap = jnp.concatenate([far[b], far[b]], axis=0)
                scores = scores - slope * gap
                e = jnp.exp(scores - jnp.max(scores, axis=-1, keepdims=True))
                p = e * (1.0 / jnp.sum(e, axis=-1, keepdims=True))
                probs[2 * hp + b] = p
                out = unpair(dot(p.astype(bf16), heads(mixed, b, 2, hp)))
                attended[pl.ds(b * BLOCK, BLOCK), cols(hp, 128)] = out.astype(bf16)

    def branch():
        @pl.loop(0, 2)
        def _(j):
            y = dot(attended[...], w1[:, cols(j, 512, OUT0)])
            middle[:, cols(j, 512)] = (
                xin[:, cols(j, 512)].astype(f32) + y + vec[pl.ds(B_OUT, 1), cols(j, 512)]
            )

    def norm_two():
        def two(rows):
            v = middle[rows, :]
            normed[rows, :] = norm_rows(rows, v, xhat2, rstd2, G_TWO, S_TWO).astype(bf16)

        rows_loop(two)

    def rise(lo, hi):
        @pl.loop(0, hi - lo)
        def _(i):
            j = i + lo
            y = dot(normed[...], w1[:, cols(j, 512, UP0)])
            u = y + b_up[pl.ds(0, 1), cols(j, 512)]
            c = 0.7978845608028654
            uu = u * u
            t = jnp.tanh(c * (u + 0.044715 * u * uu))
            half = 0.5 * (1.0 + t)
            a = (u * half).astype(bf16)
            act[:, cols(j, 512)] = a
            act_t[pl.ds(j * 4, 4)] = a.T.reshape(4, 2, 64, ROWS)
            gprime[:, cols(j, 512)] = half + 0.5 * u * (1.0 - t * t) * (
                c * (1.0 + (3 * 0.044715) * uu)
            )

    def first_part():
        def start():
            norm_one()
            transpose_into(n_t, normed)

        def end():
            transpose_into(a_t, attended)

        return [
            start,
            *[lambda j=j: project(2 * j, 2 * j + 2) for j in range(3)],
            *[lambda j=j: attend(2 * j, 2 * j + 2) for j in range(4)],
            end,
        ]

    def second_part():
        def start():
            branch()

        def middle_piece():
            norm_two()
            transpose_into(n2_t, normed)

        return [start, middle_piece, *[lambda j=j: rise(2 * j, 2 * j + 2) for j in range(4)]]

    def weave(steps, pieces):
        done = 0
        for k, step in enumerate(steps):
            step()
            upto = (k + 1) * len(pieces) // len(steps)
            if upto > done:

                @pl.when(first_section)
                def _(todo=tuple(pieces[done:upto])):
                    for piece in todo:
                        piece()

            done = upto

    forth = pltpu.make_async_remote_copy(
        src_ref=layer_out,
        dst_ref=xin,
        send_sem=send.at[COPIES - 2],
        recv_sem=recv.at[COPIES - 2],
        device_id=over_section,
        device_id_type=MESH,
    )
    back = pltpu.make_async_remote_copy(
        src_ref=input_grad,
        dst_ref=gyin,
        send_sem=send.at[COPIES - 1],
        recv_sem=recv.at[COPIES - 1],
        device_id=over_section,
        device_id_type=MESH,
    )

    g0, g1, g2 = gather_steps(0), gather_steps(1), gather_steps(2)
    for step in g0[:6]:
        step()
    make_far()

    @pl.when(first_section)
    def _():
        xin[...] = tokens[...]

    for step in (g1[0], *g0[6:8], g1[1], g0[8], g1[2], g0[9], g1[3], g0[10]):
        step()
    unpack_vectors()
    rest1 = [*g1[4:6], g2[0], g1[6], g2[1], g1[7], g2[2], g1[8], g2[3], g1[9], g1[10]]
    weave(rest1, first_part())
    weave(g2[4:], second_part())

    gathered = list(mail.sent)

    @pl.when(second_section)
    def _():
        mail.finish(gathered)
        forth.wait_recv()
        norm_one()
        transpose_into(n_t, normed)
        project(0, 6)
        attend(0, 8)
        transpose_into(a_t, attended)
        branch()
        norm_two()
        transpose_into(n2_t, normed)
        rise(0, 8)

    for a in (DOWN, UP, QKV, OUT):
        post_lhs(a)

    @pl.loop(0, 2)
    def _(j):
        y = dot(act[...], w2[:, cols(j, 512)])
        y = middle[:, cols(j, 512)] + y + vec[pl.ds(B_DOWN, 1), cols(j, 512)]
        layer_out[:, cols(j, 512)] = y.astype(bf16)

    @pl.when(first_section)
    def _():
        forth.start()
        mail.finish(gathered)
        back.wait_recv()
        g_y[...] = gyin[...]

    @pl.when(second_section)
    def _():
        g_y[...] = cotangent[...]


    def post_rhs(a):
        mine, other = pl.ds(0, ROWS), pl.ds(ROWS, ROWS)
        mail.post(("R", a), rhs[a].at[mine, :], rhs[a].at[other, :], at.other_core())

    sum_neighbours = (right_p, left_p, right_q, left_q, at.over_y())

    def give_room(a):
        for device in sum_neighbours:
            pl.semaphore_signal(credits[a], inc=1, device_id=device, device_id_type=MESH)

    def ready(a):
        mail.take(("L", a), lhs_got[a], at.other_core())
        mail.take(("R", a), rhs[a].at[pl.ds(ROWS, ROWS), :], at.other_core())
        pl.semaphore_wait(credits[a], len(sum_neighbours))

    def room(a, place, count=1):
        rows, width, base = KINDS[a]
        span = pl.ds(place * rows, count * rows)
        return w2.at[span, :] if base is None else w1.at[span, pl.ds(base, width)]

    def own(r, d, e=0):
        return (r * 4 + d) * 4 + e

    def products(a, d):
        rows, width, base = KINDS[a]
        buffer = block_down if rows == 64 else block
        for r in range(2):
            for e in range(4):
                z, x = at.zx(d, e)
                index = (at.half(r) * 4 + z) * 4 + x
                spot = pl.ds((r * 4 + e) * rows, rows)
                buffer[spot, pl.ds(0, ROWS)] = lhs_t[a][index, at.c]
                buffer[spot, pl.ds(ROWS, ROWS)] = lhs_got[a][index]

        @pl.loop(0, width // 512)
        def _(j):
            y = dot(buffer[...], rhs[a][:, cols(j, 512)]).astype(bf16)
            for r in range(2):
                span = pl.ds(own(r, d) * rows, 4 * rows)
                part = y[r * 4 * rows : (r + 1) * 4 * rows]
                if base is None:
                    w2[span, cols(j, 512)] = part
                else:
                    w1[span, cols(j, 512, base)] = part

    def total(a, dst, terms):
        @pl.loop(0, KINDS[a][1] // 512)
        def _(j):
            value = None
            for term in terms:
                piece = term[:, cols(j, 512)].astype(f32)
                value = piece if value is None else value + piece
            dst[:, cols(j, 512)] = value.astype(dst.dtype)

    def sum_p(a, r, d, *ks):
        dst = room(a, own(r, d), 4)
        total(a, dst, (dst, *[room(a, RING_P + 4 * k, 4) for k in ks]))

    def sum_q(a, r, e, *ks):
        dst = room(a, own(r, 0, e))
        total(a, dst, (dst, *[room(a, RING_Q + k) for k in ks]))

    def post_p(a, k, r, d, device):
        src, dst = lambda: room(a, own(r, d), 4), lambda: room(a, RING_P + 4 * k, 4)
        mail.post(("P", a, k), src, dst, device)

    def take_p(a, *ks):
        for k in ks:
            mail.take(("P", a, k), room(a, RING_P + 4 * k, 4), right_p)

    def post_q(a, k, r, e, device):
        mail.post(("Q", a, k), room(a, own(r, 0, e)), room(a, RING_Q + k), device)

    def take_q(a, *ks):
        for k in ks:
            mail.take(("Q", a, k), room(a, RING_Q + k), right_q)

    def a1(a):
        ready(a)
        products(a, 2)
        post_p(a, 0, 0, 2, right_p)
        post_p(a, 1, 1, 2, left_p)

    def a2(a):
        products(a, 1)
        post_p(a, 2, 1, 1, right_p)
        products(a, 3)
        post_p(a, 3, 0, 3, left_p)

    def a3(a):
        take_p(a, 0)
        sum_p(a, 0, 1, 0)
        post_p(a, 4, 0, 1, right_p)
        take_p(a, 1)
        sum_p(a, 1, 3, 1)
        post_p(a, 5, 1, 3, left_p)
        products(a, 0)

    def a4(a):
        take_p(a, 2, 3, 4, 5)
        sum_p(a, 0, 0, 4, 3)
        sum_p(a, 1, 0, 2, 5)
        post_q(a, 0, 0, 2, right_q)
        post_q(a, 1, 1, 2, left_q)
        post_q(a, 2, 1, 1, right_q)
        post_q(a, 3, 0, 3, left_q)

    def a5(a):
        take_q(a, 0)
        sum_q(a, 0, 1, 0)
        post_q(a, 4, 0, 1, right_q)
        take_q(a, 1)
        sum_q(a, 1, 3, 1)
        post_q(a, 5, 1, 3, left_q)

    def a6(a):
        take_q(a, 2, 3, 4, 5)
        sum_q(a, 1, 0, 2, 5)
        mail.post(("Y", a), room(a, own(1, 0)), room(a, LAST), at.over_y())

    outs = (out_down, out_up, out_qkv, out_out)

    def a7(a):
        mail.take(("Y", a), room(a, LAST), right_p)
        terms = (room(a, own(0, 0)), room(a, RING_Q + 4), room(a, RING_Q + 3), room(a, LAST))
        total(a, outs[a], terms)

    def when_first(*steps):
        @pl.when(first_section)
        def _():
            for step, a in steps:
                step(a)

    even_p, even_q = 1 - 2 * lax.rem(at.p, 2), 1 - 2 * lax.rem(at.q, 2)
    partners = (
        at.other_core(),
        at.at(even_p, 0),
        at.at(-even_p, 0),
        at.at(0, even_q),
        at.at(0, -even_q),
        at.over_y(),
    )

    def post_vec(k):
        mail.post(("V", k), vec_sum.at[k], vec_got.at[k], partners[k])

    def take_vec(k):
        mail.take(("V", k), vec_got.at[k], partners[k])
        vec_sum[k + 1] = vec_sum[k] + vec_got[k]


    g_vec = vec_sum.at[0]
    post_rhs(DOWN)
    g_vec[...] = jnp.zeros((16, D), f32)

    @pl.loop(0, 8)
    def _(j):
        g = dot(g_y[...], w2[cols(j, 512), :], NT)
        g = (g * gprime[:, cols(j, 512)]).astype(bf16)
        g_upward[:, cols(j, 512)] = g
        g_vec[pl.ds(8 + j // 2, 1), cols(j % 2, 512)] = jnp.sum(
            g.astype(f32), axis=0, keepdims=True
        )

    post_rhs(UP)
    give_room(DOWN)
    when_first((a1, DOWN))

    @pl.loop(0, 4)
    def _(j):
        grad[:, cols(j, 256)] = dot(g_upward[...], w1[cols(j, 256), pl.ds(UP0, FF)], NT)

    give_room(UP)
    when_first((a2, DOWN))

    def add(index, value):
        g_vec[pl.ds(index, 1), :] = g_vec[pl.ds(index, 1), :] + jnp.sum(
            value, axis=0, keepdims=True
        )

    def norm_back(rows, xhat, rstd, gain, shift):
        dy = grad[rows, :]
        h = xhat[rows, :]
        add(gain, dy * h)
        add(shift, dy)
        dh = dy * vec[pl.ds(gain, 1), :]
        m1 = jnp.mean(dh, axis=-1, keepdims=True)
        m2 = jnp.mean(dh * h, axis=-1, keepdims=True)
        return rstd[rows, pl.ds(0, 1)] * (dh - m1 - h * m2)

    def three(rows):
        gy = g_y[rows, :].astype(f32)
        gm = gy + norm_back(rows, xhat2, rstd2, G_TWO, S_TWO)
        add(B_DOWN, gy)
        middle[rows, :] = gm
        low = gm.astype(bf16)
        g_branch[rows, :] = low
        add(B_OUT, low.astype(f32))

    rows_loop(three)
    post_rhs(OUT)
    when_first((a1, UP))

    @pl.loop(0, 4)
    def _(j):
        y = dot(g_branch[...], w1[cols(j, 256), pl.ds(OUT0, D)], NT)
        act[:, cols(j, 256)] = y.astype(bf16)

    give_room(OUT)

    def attend_back(lo, hi):
        @pl.loop(0, hi - lo)
        def _(i):
            hp = i + lo
            for b in range(2):
                queries = pair(heads(mixed, b, 0, hp))
                keys, values = heads(mixed, b, 1, hp), heads(mixed, b, 2, hp)
                da = pair(heads(act, b, 0, hp))
                p = probs[2 * hp + b]
                dv = dot(p.astype(bf16), da, TN)
                dp = dot(da, values, NT)
                delta = jnp.sum(p * dp, axis=-1, keepdims=True)
                ds = (p * (dp - delta)).astype(bf16)
                dq = unpair(dot(ds, keys)) * 0.125
                dk = dot(ds, queries, TN) * 0.125
                for part, value in enumerate((dq, dk, dv)):
                    span = (pl.ds(b * BLOCK, BLOCK), cols(hp, 128, part * D))
                    g_mixed[span] = value.astype(bf16)

    attend_back(0, 8)
    post_rhs(QKV)
    when_first((a3, DOWN), (a2, UP))

    @pl.loop(0, 4)
    def _(j):
        grad[:, cols(j, 256)] = dot(g_mixed[...], w1[cols(j, 256), pl.ds(QKV0, 3 * D)], NT)

    give_room(QKV)

    def four(rows):
        gx = middle[rows, :] + norm_back(rows, xhat1, rstd1, G_ONE, S_ONE)
        input_grad[rows, :] = gx.astype(bf16)
        add(B_QUERY, g_mixed[rows, pl.ds(0, D)].astype(f32))
        add(B_VALUE, g_mixed[rows, pl.ds(2 * D, D)].astype(f32))

    rows_loop(four)

    @pl.when(second_section)
    def _():
        back.start()
        for step, a in ((a1, DOWN), (a2, DOWN), (a1, UP), (a3, DOWN), (a2, UP)):
            step(a)

    post_vec(0)
    a1(QKV)
    a2(QKV)
    a3(UP)
    take_vec(0)
    post_vec(1)
    a1(OUT)
    a2(OUT)
    a4(DOWN)
    a3(QKV)
    take_vec(1)
    post_vec(2)
    a3(OUT)
    a5(DOWN)
    a4(UP)
    take_vec(2)
    post_vec(3)
    a6(DOWN)
    a5(UP)
    a4(QKV)
    take_vec(3)
    post_vec(4)
    a4(OUT)
    a6(UP)
    a7(DOWN)
    a5(QKV)
    a5(OUT)
    take_vec(4)
    post_vec(5)
    a7(UP)
    a6(QKV)
    a6(OUT)
    take_vec(5)
    vec_out[...] = vec_sum[6]
    a7(QKV)
    a7(OUT)

    @pl.when(first_section)
    def _():
        forth.wait_send()

    @pl.when(second_section)
    def _():
        back.wait_send()

    mail.finish([name for name in mail.sent if name not in gathered])


def step(*args):
    def out(rows, columns, kind=bf16):
        return jax.ShapeDtypeStruct((rows, columns), kind)

    return pl.pallas_call(
        step_kernel,
        out_shape=(
            out(ROWS, D),
            out(ROWS, D),
            *[out(rows, width, f32) for rows, width, _ in KINDS],
            out(16, D, f32),
        ),
        in_specs=[VMEM, VMEM, VMEM, *[ANY] * 5],
        out_specs=(VMEM,) * 7,
        scratch_shapes=[
            pltpu.VMEM((D, NA), bf16),
            pltpu.VMEM((FF, D), bf16),
            pltpu.VMEM((ROWS, D), bf16),
            pltpu.VMEM((ROWS, D), bf16),
            pltpu.VMEM((8, D), f32),
            pltpu.VMEM((8, FF), f32),
            pltpu.VMEM((8, 3 * D), f32),
            pltpu.VMEM((ROWS, D), f32),
            pltpu.VMEM((ROWS, 128), f32),
            pltpu.VMEM((ROWS, D), f32),
            pltpu.VMEM((ROWS, 128), f32),
            pltpu.VMEM((ROWS, 3 * D), bf16),
            pltpu.VMEM((2, BLOCK, BLOCK), f32),
            pltpu.VMEM((16, 2 * BLOCK, BLOCK), f32),
            pltpu.VMEM((ROWS, D), f32),
            pltpu.VMEM((ROWS, FF), f32),
            pltpu.VMEM((ROWS, FF), bf16),
            pltpu.VMEM((ROWS, D), f32),
            *[pltpu.VMEM((32, 2, rows, ROWS), bf16) for rows, _, _ in KINDS],
            *[pltpu.VMEM((32, rows, ROWS), bf16) for rows, _, _ in KINDS],
            *[pltpu.VMEM((2 * ROWS, width), bf16) for _, width, _ in KINDS],
            pltpu.VMEM((128, 2 * ROWS), bf16),
            pltpu.VMEM((512, 2 * ROWS), bf16),
            pltpu.VMEM((7, 16, D), f32),
            pltpu.VMEM((6, 16, D), f32),
            pltpu.SemaphoreType.DMA((COPIES,)),
            pltpu.SemaphoreType.DMA((COPIES,)),
            pltpu.SemaphoreType.DMA((5,)),
            *[pltpu.SemaphoreType.REGULAR] * 4,
        ],
        compiler_params=pltpu.CompilerParams(
            collective_id=0, has_side_effects=True, vmem_limit_bytes=62 * 2**20
        ),
        name="step",
    )(*args)


def lay_out_kernel(index, *refs):
    big_in, sums, big_out, vectors = refs[:6], refs[6], refs[7:13], refs[13:]
    for src, dst in zip(big_in, big_out):
        dst[...] = src[...]
    i = index[0]
    own = sums[pl.ds(0, 8), cols(i // 8, 128)]
    own = pltpu.roll(own, lax.rem(128 - lax.rem(i, 8) * 16, 128), 1)
    for k in range(8):
        vectors[k][...] = own[k : k + 1, 0:16]
    rows = sums[pl.ds(8, 8), cols(lax.rem(i, 16) // 2, 128)]
    rows = pltpu.roll(rows, lax.rem(128 - lax.rem(i, 2) * 64, 128), 1)
    row = lax.broadcasted_iota(jnp.int32, (8, 128), 0) == i // 16
    vectors[8][...] = jnp.sum(jnp.where(row, rows, 0.0), axis=0, keepdims=True)[:, 0:64]


def lay_out(index, big, sums):
    return pl.pallas_call(
        lay_out_kernel,
        out_shape=(
            *[jax.ShapeDtypeStruct(v.shape, v.dtype) for v in big],
            *[jax.ShapeDtypeStruct((1, 16), f32)] * 8,
            jax.ShapeDtypeStruct((1, 64), f32),
        ),
        in_specs=[SMEM, *[VMEM] * 7],
        out_specs=(VMEM,) * 15,
        compiler_params=pltpu.CompilerParams(vmem_limit_bytes=32 * 2**20),
        name="lay_out",
    )(index, *big, sums)


def body(
    tokens,
    positions,
    cotangent,
    w_qkv,
    b_query,
    b_value,
    w_out,
    b_out,
    w_up,
    b_up,
    w_down,
    b_down,
    gain_one,
    shift_one,
    gain_two,
    shift_two,
):
    index = lax.axis_index(DP)
    small = (b_query, b_value, b_out, b_down, gain_one, shift_one, gain_two, shift_two)
    lane = jnp.arange(128)[None]
    rows = jnp.tile(jnp.concatenate(small, axis=0), (1, 8))
    rows = jnp.where(lane // 16 == index % 8, rows, jnp.zeros_like(rows))
    wide = jnp.tile(b_up, (8, 2))
    wide = jnp.where(lane // 64 == index % 2, wide, jnp.zeros_like(wide))
    *big, sums = step(
        tokens.reshape(ROWS, D),
        positions,
        cotangent.reshape(ROWS, D),
        jnp.concatenate([rows, wide], axis=0),
        w_qkv[0],
        w_out[0],
        w_up[0],
        w_down[0],
    )
    layer_out, input_grad, down, up, qkv, out, *vectors = lay_out(
        jnp.reshape(index, (1,)).astype(jnp.int32), big, sums
    )
    return (
        layer_out.reshape(1, 2, BLOCK, D),
        input_grad.reshape(1, 2, BLOCK, D),
        qkv[None],
        vectors[B_QUERY],
        vectors[B_VALUE],
        out[None],
        vectors[B_OUT],
        up[None],
        vectors[8],
        down[None],
        vectors[B_DOWN],
        vectors[G_ONE],
        vectors[S_ONE],
        vectors[G_TWO],
        vectors[S_TWO],
    )


def solution(mesh):
    torus = Mesh(mesh.devices.reshape(2, 2, 4, 4, 2), AXES)
    rows, matrix, vector = P(None, DP, None), P("section", DP, None), P("section", DP)
    of_layer = P("section", None, DP, None)
    return jax.shard_map(
        body,
        mesh=torus,
        in_specs=(
            rows,
            P(None, DP),
            rows,
            matrix,
            vector,
            vector,
            matrix,
            vector,
            matrix,
            vector,
            matrix,
            vector,
            vector,
            vector,
            vector,
            vector,
        ),
        out_specs=(
            of_layer,
            of_layer,
            matrix,
            vector,
            vector,
            matrix,
            vector,
            matrix,
            vector,
            matrix,
            vector,
            vector,
            vector,
            vector,
            vector,
        ),
        check_vma=False,
    )
```

```python
import jax
import jax.numpy as jnp
from jax import lax
from jax.experimental import pallas as pl
from jax.experimental.pallas import tpu as pltpu
from jax.sharding import Mesh
from jax.sharding import PartitionSpec as P

HEADS = 16
D = 1024
FF = 4096
ROWS = 256
BLOCK = 128
QKV0, OUT0, UP0, NA = 128, 3200, 4224, 8320
HALF = 1664
AXES = ("section", "dp_0", "dp_1", "dp_2", "dp_3")
DP = AXES[1:]
MESH = pl.DeviceIdType.MESH
EPSILON = 1e-05
FAR = 1e30
ANY = pl.BlockSpec(memory_space=pl.ANY)
VMEM = pl.BlockSpec(memory_space=pltpu.VMEM)
SMEM = pl.BlockSpec(memory_space=pltpu.SMEM)
bf16 = jnp.bfloat16
f32 = jnp.float32


class Place:
    def __init__(self):
        self.s, self.yh, self.z, self.x, self.c = [lax.axis_index(a) for a in AXES]
        self.p = jnp.where(self.c == 0, self.z, self.x)
        self.q = jnp.where(self.c == 0, self.x, self.z)

    def zx(self, dp, dq):
        pp, qq = lax.rem(self.p + (dp + 4), 4), lax.rem(self.q + (dq + 4), 4)
        return jnp.where(self.c == 0, pp, qq), jnp.where(self.c == 0, qq, pp)

    def at(self, dp, dq):
        z, x = self.zx(dp, dq)
        return (self.s, self.yh, z, x, self.c)

    def half(self, r):
        return lax.rem(self.yh + r, 2)

    def over_y(self):
        return (self.s, 1 - self.yh, self.z, self.x, self.c)

    def other_core(self):
        return (self.s, self.yh, self.z, self.x, 1 - self.c)

    def neighbours(self):
        return (
            self.over_y(),
            self.other_core(),
            self.at(1, 0),
            self.at(-1, 0),
            self.at(0, 1),
            self.at(0, -1),
        )


def greet(devices):
    barrier = pltpu.get_barrier_semaphore()
    for device in devices:
        pl.semaphore_signal(barrier, inc=1, device_id=device, device_id_type=MESH)
    pl.semaphore_wait(barrier, len(devices))


class Mail:
    def __init__(self, send, recv):
        self.send, self.recv, self.sent, self.number = send, recv, {}, {}

    def post(self, name, src, dst, device):
        self.number.setdefault(name, len(self.number))
        self.sent[name] = (src, dst, device)
        self.copy(name).start()

    def copy(self, name):
        src, dst, device = self.sent[name]
        k = self.number[name]
        return pltpu.make_async_remote_copy(
            src_ref=src() if callable(src) else src,
            dst_ref=dst() if callable(dst) else dst,
            send_sem=self.send.at[k],
            recv_sem=self.recv.at[k],
            device_id=device,
            device_id_type=MESH,
        )

    def take(self, name, dst, device):
        k = self.number[name]
        pltpu.make_async_remote_copy(
            src_ref=dst,
            dst_ref=dst,
            send_sem=self.send.at[k],
            recv_sem=self.recv.at[k],
            device_id=device,
            device_id_type=MESH,
        ).wait_recv()

    def finish(self, names):
        for name in names:
            self.copy(name).wait_send()


def dot(a, b, dims=((1,), (0,))):
    return lax.dot_general(a, b, (dims, ((), ())), preferred_element_type=f32)


NT = ((1,), (1,))
TN = ((0,), (0,))


def cols(j, width, base=0):
    return pl.ds(pl.multiple_of(base + j * width, 128), width)


B_QUERY, B_VALUE, B_OUT, B_DOWN, G_ONE, S_ONE, G_TWO, S_TWO = range(8)
DOWN, UP, QKV, OUT = range(4)
KINDS = ((64, D, None), (16, FF, UP0), (16, 3 * D, QKV0), (16, D, OUT0))
COPIES = 68 + 2 * 63 + 4 * (2 + 6 + 6) + 3 + 4 + 6 + 2
RING_P, RING_Q, LAST = 32, 56, 62


def step_kernel(
    tokens,
    positions,
    cotangent,
    vec_tile,
    in_qkv,
    in_out,
    in_up,
    in_down,
    layer_out,
    input_grad,
    out_down,
    out_up,
    out_qkv,
    out_out,
    vec_out,
    w1,
    w2,
    xin,
    gyin,
    vec,
    b_up,
    b_qkv,
    xhat1,
    rstd1,
    xhat2,
    rstd2,
    mixed,
    far,
    probs,
    middle,
    gprime,
    act,
    grad,
    act_t,
    n2_t,
    n_t,
    a_t,
    l_down,
    l_up,
    l_qkv,
    l_out,
    r_down,
    r_up,
    r_qkv,
    r_out,
    block,
    block_down,
    vec_sum,
    vec_got,
    send,
    recv,
    load,
    *credits,
):
    at = Place()
    mail = Mail(send, recv)
    section = at.s
    first_section, second_section = section == 0, section == 1
    over_section = (1 - at.s, at.yh, at.z, at.x, at.c)
    my_index = ((at.yh * 4 + at.z) * 4 + at.x) * 2 + at.c
    right_p, left_p, right_q, left_q = at.at(1, 0), at.at(-1, 0), at.at(0, 1), at.at(0, -1)

    def shard_rows(index, rows):
        return pl.ds(pl.multiple_of(index * rows, rows), rows)

    here = shard_rows(my_index, 16)
    placing = [
        pltpu.make_async_copy(vec_tile, w1.at[here, pl.ds(0, 128)], load.at[0]),
        pltpu.make_async_copy(in_qkv, w1.at[here, pl.ds(QKV0, 3 * D)], load.at[1]),
        pltpu.make_async_copy(in_out, w1.at[here, pl.ds(OUT0, D)], load.at[2]),
        pltpu.make_async_copy(in_up, w1.at[here, pl.ds(UP0, FF)], load.at[3]),
        pltpu.make_async_copy(in_down, w2.at[shard_rows(my_index, 64), :], load.at[4]),
    ]
    for copy in placing:
        copy.start()
    greet((*at.neighbours(), over_section))


    def view(t, r, dp, dq, core=None, part=None):
        z, x = at.zx(dp, dq)
        index = ((at.half(r) * 4 + z) * 4 + x) * 2 + (at.c if core is None else core)
        if t == 2:
            return w2.at[shard_rows(index, 64), :]
        span = (pl.ds(0, OUT0), pl.ds(OUT0, NA - OUT0))[t]
        if part is not None:
            span = (pl.ds(0, HALF), pl.ds(HALF, OUT0 - HALF))[part]
        return w1.at[shard_rows(index, 16), span]

    def post(kind, t, r, dp, dq, device):
        v = view(t, r, dp, dq)
        mail.post((kind, t, r, dp, dq), v, v, device)

    def take(kind, t, sent, got):
        mail.take((kind, t, *sent), view(t, *got), right_p)

    def hand_over(t, r, dp, dq):
        post("C", t, r, dp, dq, at.other_core())

    def spread(t, r, dq):
        post("PR", t, r, 0, dq, right_p)
        post("PL", t, r, 0, dq, left_p)
        hand_over(t, r, 0, dq)

    def pass_on(t, dq):
        take("PR", t, (0, 0, dq), (0, -1, dq))
        post("PR2", t, 0, -1, dq, right_p)
        take("PL", t, (1, 0, dq), (1, 1, dq))
        post("PL2", t, 1, 1, dq, left_p)
        hand_over(t, 0, -1, dq)
        hand_over(t, 1, 1, dq)
        take("PL", t, (0, 0, dq), (0, 1, dq))
        take("PR", t, (1, 0, dq), (1, -1, dq))
        hand_over(t, 0, 1, dq)
        hand_over(t, 1, -1, dq)

    def gather_y_last():
        around = (0, -1, 1, 2)

        def post_half(kind, part, dp, dq, device):
            v = view(0, 0, dp, dq, part=part)
            mail.post((kind, dp, dq), v, v, device)

        def take_half(kind, part, sent, got):
            mail.take((kind, *sent), view(0, 0, *got, part=part), right_p)

        def onward(dp, dq):
            post("Y", 0, 0, dp, dq, at.over_y())
            hand_over(0, 0, dp, dq)

        def here(dq):
            post("PR", 0, 0, 0, dq, right_p)
            post("PL", 0, 0, 0, dq, left_p)
            onward(0, dq)

        def s0():
            post("QR", 0, 0, 0, 0, right_q)
            post("QL", 0, 0, 0, 0, left_q)
            here(0)

        def s1():
            take("QR", 0, (0, 0, 0), (0, 0, -1))
            post_half("QH", 0, 0, -1, right_q)
            here(-1)
            take("QL", 0, (0, 0, 0), (0, 0, 1))
            post_half("QG", 1, 0, 1, left_q)
            here(1)

        def s2():
            take_half("QH", 0, (0, -1), (0, -2))
            take_half("QG", 1, (0, 1), (0, 2))
            here(2)

        def s3(dq):
            take("PR", 0, (0, 0, dq), (0, -1, dq))
            post_half("PH", 0, -1, dq, right_p)
            onward(-1, dq)
            take("PL", 0, (0, 0, dq), (0, 1, dq))
            post_half("PG", 1, 1, dq, left_p)
            onward(1, dq)

        def s4():
            for dq in around:
                take_half("PH", 0, (-1, dq), (-2, dq))
                take_half("PG", 1, (1, dq), (2, dq))
                onward(2, dq)

        def from_y(dp, dqs):
            for dq in dqs:
                take("Y", 0, (0, dp, dq), (1, dp, dq))
                hand_over(0, 1, dp, dq)

        def over_y():
            from_y(0, around)
            from_y(-1, (0,))
            from_y(1, (0,))

        def over_y_too():
            for dq in (-1, 1, 2):
                from_y(-1, (dq,))
                from_y(1, (dq,))
            from_y(2, around)

        def s10():
            for r in range(2):
                for dp in around:
                    for dq in around:
                        name = ("C", 0, r, dp, dq)
                        mail.take(name, view(0, r, dq, dp, 1 - at.c), at.other_core())

        return [s0, s1, s2, *[lambda dq=dq: s3(dq) for dq in around], s4, over_y, over_y_too, s10]

    def gather_steps(t):
        def s0():
            post("QR", t, 0, 0, 0, right_q)
            post("QL", t, 0, 0, 0, left_q)
            spread(t, 0, 0)

        def s1():
            take("Y", t, (0, 0, 0), (1, 0, 0))
            post("QR", t, 1, 0, 0, right_q)
            post("QL", t, 1, 0, 0, left_q)
            spread(t, 1, 0)

        def s2():
            take("QR", t, (0, 0, 0), (0, 0, -1))
            post("QR2", t, 0, 0, -1, right_q)
            spread(t, 0, -1)
            take("QL", t, (0, 0, 0), (0, 0, 1))
            spread(t, 0, 1)

        def s3():
            take("QL", t, (1, 0, 0), (1, 0, 1))
            post("QL2", t, 1, 0, 1, left_q)
            spread(t, 1, 1)
            take("QR", t, (1, 0, 0), (1, 0, -1))
            spread(t, 1, -1)

        def s4():
            pass_on(t, 0)

        def s5():
            take("QR2", t, (0, 0, -1), (0, 0, -2))
            spread(t, 0, 2)
            take("QL2", t, (1, 0, 1), (1, 0, 2))
            spread(t, 1, 2)

        def s9():
            for dq in (0, -1, 1, 2):
                take("PR2", t, (0, -1, dq), (0, -2, dq))
                take("PL2", t, (1, 1, dq), (1, 2, dq))
                hand_over(t, 0, 2, dq)
                hand_over(t, 1, 2, dq)

        def s10():
            for r in range(2):
                for dp in (0, -1, 1, 2):
                    for dq in (0, -1, 1, 2):
                        name = ("C", t, r, dp, dq)
                        mail.take(name, view(t, r, dq, dp, 1 - at.c), at.other_core())

        passing = [lambda dq=dq: pass_on(t, dq) for dq in (-1, 1, 2)]
        return [s0, s1, s2, s3, s4, s5, *passing, s9, s10]


    chunk = 128

    def rows_loop(body):
        @pl.loop(0, ROWS // chunk)
        def _(i):
            body(pl.ds(pl.multiple_of(i * chunk, chunk), chunk))

    g_y, g_branch = r_down.at[pl.ds(0, ROWS), :], r_out.at[pl.ds(0, ROWS), :]
    g_upward, g_mixed = r_up.at[pl.ds(0, ROWS), :], r_qkv.at[pl.ds(0, ROWS), :]
    normed, attended = g_branch, g_y

    row = lax.broadcasted_iota(jnp.int32, (BLOCK, BLOCK), 0)
    col = lax.broadcasted_iota(jnp.int32, (BLOCK, BLOCK), 1)
    low_lane = col < 64

    def make_far():
        distance = col - row
        for b in range(2):
            allowed = (distance >= 0) & (distance <= positions[pl.ds(b, 1), :])
            far[b] = jnp.where(allowed, distance.astype(f32), FAR).T

    def unpack_vectors():
        for j in range(8):
            tiles = [w1[pl.ds((8 * j + i) * 16, 16), pl.ds(0, 128)].astype(f32) for i in range(8)]
            pairs = [tiles[2 * i] + tiles[2 * i + 1] for i in range(4)]
            for i in range(4):
                b_up[:, pl.ds((4 * j + i) * 128, 128)] = pairs[i][8:16]
            vec[:, pl.ds(j * 128, 128)] = ((pairs[0] + pairs[1]) + (pairs[2] + pairs[3]))[0:8]
        b_qkv[pl.ds(0, 1), pl.ds(0, D)] = vec[pl.ds(B_QUERY, 1), :]
        b_qkv[pl.ds(0, 1), pl.ds(D, D)] = jnp.zeros((1, D), f32)
        b_qkv[pl.ds(0, 1), pl.ds(2 * D, D)] = vec[pl.ds(B_VALUE, 1), :]

    def norm_rows(rows, v, xhat, rstd, gain, shift):
        center = v - jnp.mean(v, axis=-1, keepdims=True)
        r = lax.rsqrt(jnp.mean(center * center, axis=-1, keepdims=True) + EPSILON)
        h = center * r
        xhat[rows, :] = h
        rstd[rows, :] = jnp.broadcast_to(r, (chunk, 128))
        return h * vec[pl.ds(gain, 1), :] + vec[pl.ds(shift, 1), :]

    def transpose_into(dst, src):
        @pl.loop(0, D // 256, unroll=True)
        def _(j):
            dst[pl.ds(j * 8, 8)] = src[:, cols(j, 256)].T.reshape(8, 2, 16, ROWS)

    def post_lhs(a):
        mail.post(("L", a), lhs_t[a].at[:, 1 - at.c], lhs_got[a], at.other_core())

    lhs_t, lhs_got = (act_t, n2_t, n_t, a_t), (l_down, l_up, l_qkv, l_out)
    rhs = (r_down, r_up, r_qkv, r_out)

    def norm_one():
        def one(rows):
            v = xin[rows, :].astype(f32)
            normed[rows, :] = norm_rows(rows, v, xhat1, rstd1, G_ONE, S_ONE).astype(bf16)

        rows_loop(one)

    def project(lo, hi):
        @pl.loop(0, hi - lo, unroll=True)
        def _(i):
            j = i + lo
            y = dot(normed[...], w1[:, cols(j, 512, QKV0)])
            mixed[:, cols(j, 512)] = (y + b_qkv[pl.ds(0, 1), cols(j, 512)]).astype(bf16)

    def pair(value):
        zero = jnp.zeros_like(value)
        return jnp.concatenate(
            [jnp.where(low_lane, value, zero), jnp.where(low_lane, zero, value)], axis=0
        )

    def unpair(value):
        return jnp.where(low_lane, value[:BLOCK], value[BLOCK:])

    def slope_rows(hp):
        first = lax.broadcasted_iota(jnp.int32, (2 * BLOCK, 1), 0) < BLOCK
        h = ((2 * hp + 2) - first.astype(jnp.int32)).astype(f32)
        return jnp.exp(h * (-0.5 * 0.6931471805599453))

    def heads(ref, b, part, hp):
        return ref[pl.ds(b * BLOCK, BLOCK), cols(hp, 128, part * D)]

    def attend(lo, hi):
        @pl.loop(0, hi - lo, unroll=True)
        def _(i):
            hp = i + lo
            slope = slope_rows(hp)
            for b in range(2):
                queries = pair(heads(mixed, b, 0, hp))
                scores = dot(queries, heads(mixed, b, 1, hp), NT) * 0.125
                gap = jnp.concatenate([far[b], far[b]], axis=0)
                scores = scores - slope * gap
                e = jnp.exp(scores - jnp.max(scores, axis=-1, keepdims=True))
                p = e * (1.0 / jnp.sum(e, axis=-1, keepdims=True))
                probs[2 * hp + b] = p
                out = unpair(dot(p.astype(bf16), heads(mixed, b, 2, hp)))
                attended[pl.ds(b * BLOCK, BLOCK), cols(hp, 128)] = out.astype(bf16)

    def branch():
        @pl.loop(0, 2, unroll=True)
        def _(j):
            y = dot(attended[...], w1[:, cols(j, 512, OUT0)])
            middle[:, cols(j, 512)] = (
                xin[:, cols(j, 512)].astype(f32) + y + vec[pl.ds(B_OUT, 1), cols(j, 512)]
            )

    def norm_two():
        def two(rows):
            v = middle[rows, :]
            normed[rows, :] = norm_rows(rows, v, xhat2, rstd2, G_TWO, S_TWO).astype(bf16)

        rows_loop(two)

    def rise(lo, hi):
        @pl.loop(0, hi - lo, unroll=True)
        def _(i):
            j = i + lo
            y = dot(normed[...], w1[:, cols(j, 512, UP0)])
            u = y + b_up[pl.ds(0, 1), cols(j, 512)]
            c = 0.7978845608028654
            uu = u * u
            t = jnp.tanh(c * (u + 0.044715 * u * uu))
            half = 0.5 * (1.0 + t)
            a = (u * half).astype(bf16)
            act[:, cols(j, 512)] = a
            act_t[pl.ds(j * 4, 4)] = a.T.reshape(4, 2, 64, ROWS)
            gprime[:, cols(j, 512)] = half + 0.5 * u * (1.0 - t * t) * (
                c * (1.0 + (3 * 0.044715) * uu)
            )

    def first_part():
        def start():
            norm_one()
            transpose_into(n_t, normed)

        def end():
            transpose_into(a_t, attended)

        return [
            start,
            *[lambda j=j: project(2 * j, 2 * j + 2) for j in range(3)],
            *[lambda j=j: attend(2 * j, 2 * j + 2) for j in range(4)],
            end,
        ]

    def second_part():
        def start():
            branch()

        def middle_piece():
            norm_two()
            transpose_into(n2_t, normed)

        return [start, middle_piece, *[lambda j=j: rise(2 * j, 2 * j + 2) for j in range(4)]]

    def weave(steps, pieces):
        done = 0
        for k, step in enumerate(steps):
            step()
            upto = (k + 1) * len(pieces) // len(steps)
            if upto > done:

                @pl.when(first_section)
                def _(todo=tuple(pieces[done:upto])):
                    for piece in todo:
                        piece()

            done = upto

    forth = pltpu.make_async_remote_copy(
        src_ref=layer_out,
        dst_ref=xin,
        send_sem=send.at[COPIES - 2],
        recv_sem=recv.at[COPIES - 2],
        device_id=over_section,
        device_id_type=MESH,
    )
    back = pltpu.make_async_remote_copy(
        src_ref=input_grad,
        dst_ref=gyin,
        send_sem=send.at[COPIES - 1],
        recv_sem=recv.at[COPIES - 1],
        device_id=over_section,
        device_id_type=MESH,
    )

    g0, g1, g2 = gather_y_last(), gather_steps(1), gather_steps(2)
    for copy in placing:
        copy.wait()
    for t in (1, 2):
        post("Y", t, 0, 0, 0, at.over_y())
    for step in (g0[0], g1[0], g2[0]):
        step()
    make_far()

    @pl.when(first_section)
    def _():
        xin[...] = tokens[...]

    for step in (g0[1], g0[2], g1[1], g0[3], g0[4], g2[1], g0[5], g0[6], g1[2], g0[7]):
        step()
    for step in (g1[3], g2[2], g1[4], g0[8], g1[5], g2[3], g1[6], g1[7], g2[4], g0[9]):
        step()
    for step in (g1[8], g2[5], g0[10]):
        step()
    unpack_vectors()
    weave([g1[9], g2[6], g1[10], g2[7], g2[8]], first_part())
    weave(g2[9:], second_part())

    gathered = list(mail.sent)

    @pl.when(second_section)
    def _():
        mail.finish(gathered)
        forth.wait_recv()
        norm_one()
        transpose_into(n_t, normed)
        project(0, 6)
        attend(0, 8)
        transpose_into(a_t, attended)
        branch()
        norm_two()
        transpose_into(n2_t, normed)
        rise(0, 8)

    for a in (DOWN, UP, QKV, OUT):
        post_lhs(a)

    @pl.loop(0, 2, unroll=True)
    def _(j):
        y = dot(act[...], w2[:, cols(j, 512)])
        y = middle[:, cols(j, 512)] + y + vec[pl.ds(B_DOWN, 1), cols(j, 512)]
        layer_out[:, cols(j, 512)] = y.astype(bf16)

    @pl.when(first_section)
    def _():
        forth.start()
        mail.finish(gathered)
        back.wait_recv()
        g_y[...] = gyin[...]

    @pl.when(second_section)
    def _():
        g_y[...] = cotangent[...]


    def post_rhs(a):
        mine, other = pl.ds(0, ROWS), pl.ds(ROWS, ROWS)
        mail.post(("R", a), rhs[a].at[mine, :], rhs[a].at[other, :], at.other_core())

    sum_neighbours = (right_p, left_p, right_q, left_q, at.over_y())

    def give_room(a):
        for device in sum_neighbours:
            pl.semaphore_signal(credits[a], inc=1, device_id=device, device_id_type=MESH)

    def ready(a):
        mail.take(("L", a), lhs_got[a], at.other_core())
        mail.take(("R", a), rhs[a].at[pl.ds(ROWS, ROWS), :], at.other_core())
        pl.semaphore_wait(credits[a], len(sum_neighbours))

    def room(a, place, count=1):
        rows, width, base = KINDS[a]
        span = pl.ds(place * rows, count * rows)
        return w2.at[span, :] if base is None else w1.at[span, pl.ds(base, width)]

    def own(r, d, e=0):
        return (r * 4 + d) * 4 + e

    def products(a, d):
        rows, width, base = KINDS[a]
        buffer = block_down if rows == 64 else block
        for r in range(2):
            for e in range(4):
                z, x = at.zx(d, e)
                index = (at.half(r) * 4 + z) * 4 + x
                spot = pl.ds((r * 4 + e) * rows, rows)
                buffer[spot, pl.ds(0, ROWS)] = lhs_t[a][index, at.c]
                buffer[spot, pl.ds(ROWS, ROWS)] = lhs_got[a][index]

        @pl.loop(0, width // 512)
        def _(j):
            y = dot(buffer[...], rhs[a][:, cols(j, 512)]).astype(bf16)
            for r in range(2):
                span = pl.ds(own(r, d) * rows, 4 * rows)
                part = y[r * 4 * rows : (r + 1) * 4 * rows]
                if base is None:
                    w2[span, cols(j, 512)] = part
                else:
                    w1[span, cols(j, 512, base)] = part

    def total(a, dst, terms):
        @pl.loop(0, KINDS[a][1] // 512, unroll=True)
        def _(j):
            value = None
            for term in terms:
                piece = term[:, cols(j, 512)].astype(f32)
                value = piece if value is None else value + piece
            dst[:, cols(j, 512)] = value.astype(dst.dtype)

    def sum_p(a, r, d, *ks):
        dst = room(a, own(r, d), 4)
        total(a, dst, (dst, *[room(a, RING_P + 4 * k, 4) for k in ks]))

    def sum_q(a, r, e, *ks):
        dst = room(a, own(r, 0, e))
        total(a, dst, (dst, *[room(a, RING_Q + k) for k in ks]))

    def post_p(a, k, r, d, device):
        src, dst = lambda: room(a, own(r, d), 4), lambda: room(a, RING_P + 4 * k, 4)
        mail.post(("P", a, k), src, dst, device)

    def take_p(a, *ks):
        for k in ks:
            mail.take(("P", a, k), room(a, RING_P + 4 * k, 4), right_p)

    def post_q(a, k, r, e, device):
        mail.post(("Q", a, k), room(a, own(r, 0, e)), room(a, RING_Q + k), device)

    def take_q(a, *ks):
        for k in ks:
            mail.take(("Q", a, k), room(a, RING_Q + k), right_q)

    over_y = at.over_y()

    def post_y(d):
        src, dst = lambda: room(DOWN, own(1, d), 4), lambda: room(DOWN, 32 + 4 * d, 4)
        mail.post(("Z", d), src, dst, over_y)

    def take_y(d):
        mail.take(("Z", d), room(DOWN, 32 + 4 * d, 4), right_p)
        dst = room(DOWN, own(0, d), 4)
        total(DOWN, dst, (dst, room(DOWN, 32 + 4 * d, 4)))

    def down_p(d, e):
        return room(DOWN, own(0, d, e), 2)

    def down_ring_p(k):
        return room(DOWN, 48 + 2 * k, 2)

    def down_rows(e, half):
        return w2.at[pl.ds(own(0, 0, e) * 64 + 32 * half, 32), :]

    def down_ring_q(k):
        return w2.at[pl.ds(60 * 64 + 32 * k, 32), :]

    def down1(a):
        ready(DOWN)
        products(DOWN, 2)
        post_y(2)

    def down2(a):
        for d in (1, 3, 0):
            products(DOWN, d)
            post_y(d)

    def down_post(k, d, e, device):
        mail.post(("P", DOWN, k), down_p(d, e), down_ring_p(k), device)

    def down_take(*ks):
        for k in ks:
            mail.take(("P", DOWN, k), down_ring_p(k), right_p)

    def down3():
        take_y(2)
        down_post(0, 2, 0, right_p)
        down_post(1, 2, 2, left_p)

    def down4():
        take_y(1)
        down_post(2, 1, 2, right_p)

    def down5():
        take_y(3)
        down_post(3, 3, 0, left_p)

    def down6():
        down_take(0)
        total(DOWN, down_p(1, 0), (down_p(1, 0), down_ring_p(0)))
        down_post(4, 1, 0, right_p)
        down_take(1)
        total(DOWN, down_p(3, 2), (down_p(3, 2), down_ring_p(1)))
        down_post(5, 3, 2, left_p)

    def down_post_q(k, e, half, device):
        mail.post(("Q", DOWN, k), down_rows(e, half), down_ring_q(k), device)

    def down_take_q(*ks):
        for k in ks:
            mail.take(("Q", DOWN, k), down_ring_q(k), right_q)

    def down7():
        take_y(0)
        down_take(2, 3, 4, 5)
        total(DOWN, down_p(0, 2), (down_p(0, 2), down_ring_p(2), down_ring_p(5)))
        down_post_q(0, 2, 0, right_q)
        down_post_q(1, 2, 1, left_q)
        down_post_q(3, 3, 0, left_q)
        total(DOWN, down_p(0, 0), (down_p(0, 0), down_ring_p(4), down_ring_p(3)))
        down_post_q(2, 1, 1, right_q)

    def down8():
        down_take_q(0)
        total(DOWN, down_rows(1, 0), (down_rows(1, 0), down_ring_q(0)))
        down_post_q(4, 1, 0, right_q)
        down_take_q(1)
        total(DOWN, down_rows(3, 1), (down_rows(3, 1), down_ring_q(1)))
        down_post_q(5, 3, 1, left_q)

    def down9():
        down_take_q(2, 3, 4, 5)
        for half, k, m in ((0, 4, 3), (1, 2, 5)):
            terms = (down_rows(0, half), down_ring_q(k), down_ring_q(m))
            total(DOWN, out_down.at[pl.ds(32 * half, 32), :], terms)

    def a1(a):
        ready(a)
        products(a, 2)
        post_p(a, 0, 0, 2, right_p)
        post_p(a, 1, 1, 2, left_p)

    def a2(a):
        products(a, 1)
        post_p(a, 2, 1, 1, right_p)
        products(a, 3)
        post_p(a, 3, 0, 3, left_p)

    def a3(a):
        take_p(a, 0)
        sum_p(a, 0, 1, 0)
        post_p(a, 4, 0, 1, right_p)
        take_p(a, 1)
        sum_p(a, 1, 3, 1)
        post_p(a, 5, 1, 3, left_p)
        products(a, 0)

    def a4(a):
        take_p(a, 2, 3, 4, 5)
        sum_p(a, 0, 0, 4, 3)
        sum_p(a, 1, 0, 2, 5)
        post_q(a, 0, 0, 2, right_q)
        post_q(a, 1, 1, 2, left_q)
        post_q(a, 2, 1, 1, right_q)
        post_q(a, 3, 0, 3, left_q)

    def a5(a):
        take_q(a, 0)
        sum_q(a, 0, 1, 0)
        post_q(a, 4, 0, 1, right_q)
        take_q(a, 1)
        sum_q(a, 1, 3, 1)
        post_q(a, 5, 1, 3, left_q)

    def a6(a):
        take_q(a, 2, 3, 4, 5)
        sum_q(a, 1, 0, 2, 5)
        mail.post(("Y", a), room(a, own(1, 0)), room(a, LAST), at.over_y())

    outs = (out_down, out_up, out_qkv, out_out)

    def a7(a):
        mail.take(("Y", a), room(a, LAST), right_p)
        terms = (room(a, own(0, 0)), room(a, RING_Q + 4), room(a, RING_Q + 3), room(a, LAST))
        total(a, outs[a], terms)

    def when_first(*steps):
        @pl.when(first_section)
        def _():
            for step, a in steps:
                step(a)

    even_p, even_q = 1 - 2 * lax.rem(at.p, 2), 1 - 2 * lax.rem(at.q, 2)
    partners = (
        at.other_core(),
        at.at(even_p, 0),
        at.at(-even_p, 0),
        at.at(0, even_q),
        at.at(0, -even_q),
        at.over_y(),
    )

    def post_vec(k):
        mail.post(("V", k), vec_sum.at[k], vec_got.at[k], partners[k])

    def take_vec(k):
        mail.take(("V", k), vec_got.at[k], partners[k])
        vec_sum[k + 1] = vec_sum[k] + vec_got[k]


    g_vec = vec_sum.at[0]
    post_rhs(DOWN)
    g_vec[...] = jnp.zeros((16, D), f32)

    @pl.loop(0, 8, unroll=True)
    def _(j):
        g = dot(g_y[...], w2[cols(j, 512), :], NT)
        g = (g * gprime[:, cols(j, 512)]).astype(bf16)
        g_upward[:, cols(j, 512)] = g
        g_vec[pl.ds(8 + j // 2, 1), cols(j % 2, 512)] = jnp.sum(
            g.astype(f32), axis=0, keepdims=True
        )

    post_rhs(UP)
    give_room(DOWN)
    when_first((down1, DOWN))

    @pl.loop(0, 4, unroll=True)
    def _(j):
        grad[:, cols(j, 256)] = dot(g_upward[...], w1[cols(j, 256), pl.ds(UP0, FF)], NT)

    give_room(UP)
    when_first((down2, DOWN))

    def add(index, value):
        g_vec[pl.ds(index, 1), :] = g_vec[pl.ds(index, 1), :] + jnp.sum(
            value, axis=0, keepdims=True
        )

    def norm_back(rows, xhat, rstd, gain, shift):
        dy = grad[rows, :]
        h = xhat[rows, :]
        add(gain, dy * h)
        add(shift, dy)
        dh = dy * vec[pl.ds(gain, 1), :]
        m1 = jnp.mean(dh, axis=-1, keepdims=True)
        m2 = jnp.mean(dh * h, axis=-1, keepdims=True)
        return rstd[rows, pl.ds(0, 1)] * (dh - m1 - h * m2)

    def three(rows):
        gy = g_y[rows, :].astype(f32)
        gm = gy + norm_back(rows, xhat2, rstd2, G_TWO, S_TWO)
        add(B_DOWN, gy)
        middle[rows, :] = gm
        low = gm.astype(bf16)
        g_branch[rows, :] = low
        add(B_OUT, low.astype(f32))

    rows_loop(three)
    post_rhs(OUT)
    when_first((a1, UP))

    @pl.loop(0, 4, unroll=True)
    def _(j):
        y = dot(g_branch[...], w1[cols(j, 256), pl.ds(OUT0, D)], NT)
        act[:, cols(j, 256)] = y.astype(bf16)

    give_room(OUT)

    def attend_back(lo, hi):
        @pl.loop(0, hi - lo, unroll=True)
        def _(i):
            hp = i + lo
            for b in range(2):
                queries = pair(heads(mixed, b, 0, hp))
                keys, values = heads(mixed, b, 1, hp), heads(mixed, b, 2, hp)
                da = pair(heads(act, b, 0, hp))
                p = probs[2 * hp + b]
                dv = dot(p.astype(bf16), da, TN)
                dp = dot(da, values, NT)
                delta = jnp.sum(p * dp, axis=-1, keepdims=True)
                ds = (p * (dp - delta)).astype(bf16)
                dq = unpair(dot(ds, keys)) * 0.125
                dk = dot(ds, queries, TN) * 0.125
                for part, value in enumerate((dq, dk, dv)):
                    span = (pl.ds(b * BLOCK, BLOCK), cols(hp, 128, part * D))
                    g_mixed[span] = value.astype(bf16)

    attend_back(0, 8)
    post_rhs(QKV)
    when_first((a2, UP))

    @pl.loop(0, 4, unroll=True)
    def _(j):
        grad[:, cols(j, 256)] = dot(g_mixed[...], w1[cols(j, 256), pl.ds(QKV0, 3 * D)], NT)

    give_room(QKV)

    def four(rows):
        gx = middle[rows, :] + norm_back(rows, xhat1, rstd1, G_ONE, S_ONE)
        input_grad[rows, :] = gx.astype(bf16)
        add(B_QUERY, g_mixed[rows, pl.ds(0, D)].astype(f32))
        add(B_VALUE, g_mixed[rows, pl.ds(2 * D, D)].astype(f32))

    rows_loop(four)

    @pl.when(second_section)
    def _():
        back.start()
        for step, a in ((down1, DOWN), (down2, DOWN), (a1, UP), (a2, UP)):
            step(a)

    post_vec(0)
    a1(QKV)
    a2(QKV)
    a1(OUT)
    a2(OUT)
    a3(UP)
    take_vec(0)
    post_vec(1)
    down3()
    a3(QKV)
    take_vec(1)
    post_vec(2)
    a3(OUT)
    down4()
    a4(UP)
    take_vec(2)
    post_vec(3)
    a4(QKV)
    a5(UP)
    a4(OUT)
    take_vec(3)
    post_vec(4)
    down5()
    down6()
    a6(UP)
    a5(QKV)
    a5(OUT)
    take_vec(4)
    post_vec(5)
    a6(QKV)
    a6(OUT)
    down7()
    a7(UP)
    take_vec(5)
    vec_out[...] = vec_sum[6]
    down8()
    a7(QKV)
    a7(OUT)
    down9()

    @pl.when(first_section)
    def _():
        forth.wait_send()

    @pl.when(second_section)
    def _():
        back.wait_send()

    mail.finish([name for name in mail.sent if name not in gathered])


def step(*args):
    def out(rows, columns, kind=bf16):
        return jax.ShapeDtypeStruct((rows, columns), kind)

    return pl.pallas_call(
        step_kernel,
        out_shape=(
            out(ROWS, D),
            out(ROWS, D),
            *[out(rows, width, f32) for rows, width, _ in KINDS],
            out(16, D, f32),
        ),
        in_specs=[VMEM, VMEM, VMEM, *[ANY] * 5],
        out_specs=(VMEM,) * 7,
        scratch_shapes=[
            pltpu.VMEM((D, NA), bf16),
            pltpu.VMEM((FF, D), bf16),
            pltpu.VMEM((ROWS, D), bf16),
            pltpu.VMEM((ROWS, D), bf16),
            pltpu.VMEM((8, D), f32),
            pltpu.VMEM((8, FF), f32),
            pltpu.VMEM((8, 3 * D), f32),
            pltpu.VMEM((ROWS, D), f32),
            pltpu.VMEM((ROWS, 128), f32),
            pltpu.VMEM((ROWS, D), f32),
            pltpu.VMEM((ROWS, 128), f32),
            pltpu.VMEM((ROWS, 3 * D), bf16),
            pltpu.VMEM((2, BLOCK, BLOCK), f32),
            pltpu.VMEM((16, 2 * BLOCK, BLOCK), f32),
            pltpu.VMEM((ROWS, D), f32),
            pltpu.VMEM((ROWS, FF), f32),
            pltpu.VMEM((ROWS, FF), bf16),
            pltpu.VMEM((ROWS, D), f32),
            *[pltpu.VMEM((32, 2, rows, ROWS), bf16) for rows, _, _ in KINDS],
            *[pltpu.VMEM((32, rows, ROWS), bf16) for rows, _, _ in KINDS],
            *[pltpu.VMEM((2 * ROWS, width), bf16) for _, width, _ in KINDS],
            pltpu.VMEM((128, 2 * ROWS), bf16),
            pltpu.VMEM((512, 2 * ROWS), bf16),
            pltpu.VMEM((7, 16, D), f32),
            pltpu.VMEM((6, 16, D), f32),
            pltpu.SemaphoreType.DMA((COPIES,)),
            pltpu.SemaphoreType.DMA((COPIES,)),
            pltpu.SemaphoreType.DMA((5,)),
            *[pltpu.SemaphoreType.REGULAR] * 4,
        ],
        compiler_params=pltpu.CompilerParams(
            collective_id=0, has_side_effects=True, vmem_limit_bytes=62 * 2**20
        ),
        name="step",
    )(*args)


def lay_out_kernel(index, *refs):
    big_in, sums_in, big_out, vectors = refs[:6], refs[6], refs[7:13], refs[13:22]
    held, (sums, came, left) = refs[22:28], refs[28:]
    first = pltpu.make_async_copy(sums_in, sums, came.at[6])
    first.start()
    come = [pltpu.make_async_copy(big_in[k], held[k], came.at[k]) for k in range(6)]
    leave = [pltpu.make_async_copy(held[k], big_out[k], left.at[k]) for k in range(6)]
    for copy in come:
        copy.start()
    for k in range(6):
        come[k].wait()
        leave[k].start()
    first.wait()
    i = index[0]
    own = sums[pl.ds(0, 8), cols(i // 8, 128)]
    own = pltpu.roll(own, lax.rem(128 - lax.rem(i, 8) * 16, 128), 1)
    for k in range(8):
        vectors[k][...] = own[k : k + 1, 0:16]
    rows = sums[pl.ds(8, 8), cols(lax.rem(i, 16) // 2, 128)]
    rows = pltpu.roll(rows, lax.rem(128 - lax.rem(i, 2) * 64, 128), 1)
    row = lax.broadcasted_iota(jnp.int32, (8, 128), 0) == i // 16
    vectors[8][...] = jnp.sum(jnp.where(row, rows, 0.0), axis=0, keepdims=True)[:, 0:64]
    for copy in leave:
        copy.wait()


def lay_out(index, big, sums):
    return pl.pallas_call(
        lay_out_kernel,
        out_shape=(
            *[jax.ShapeDtypeStruct(v.shape, v.dtype) for v in big],
            *[jax.ShapeDtypeStruct((1, 16), f32)] * 8,
            jax.ShapeDtypeStruct((1, 64), f32),
        ),
        in_specs=[SMEM, *[ANY] * 7],
        out_specs=(*[ANY] * 6, *[VMEM] * 9),
        scratch_shapes=[
            *[pltpu.VMEM(v.shape, v.dtype) for v in big],
            pltpu.VMEM((16, D), f32),
            pltpu.SemaphoreType.DMA((7,)),
            pltpu.SemaphoreType.DMA((6,)),
        ],
        compiler_params=pltpu.CompilerParams(vmem_limit_bytes=62 * 2**20),
        name="lay_out",
    )(index, *big, sums)


def body(
    tokens,
    positions,
    cotangent,
    w_qkv,
    b_query,
    b_value,
    w_out,
    b_out,
    w_up,
    b_up,
    w_down,
    b_down,
    gain_one,
    shift_one,
    gain_two,
    shift_two,
):
    index = lax.axis_index(DP)
    small = (b_query, b_value, b_out, b_down, gain_one, shift_one, gain_two, shift_two)
    lane = jnp.arange(128)[None]
    rows = jnp.tile(jnp.concatenate(small, axis=0), (1, 8))
    rows = jnp.where(lane // 16 == index % 8, rows, jnp.zeros_like(rows))
    wide = jnp.tile(b_up, (8, 2))
    wide = jnp.where(lane // 64 == index % 2, wide, jnp.zeros_like(wide))
    *big, sums = step(
        tokens.reshape(ROWS, D),
        positions,
        cotangent.reshape(ROWS, D),
        jnp.concatenate([rows, wide], axis=0),
        w_qkv[0],
        w_out[0],
        w_up[0],
        w_down[0],
    )
    layer_out, input_grad, down, up, qkv, out, *vectors = lay_out(
        jnp.reshape(index, (1,)).astype(jnp.int32), big, sums
    )
    return (
        layer_out.reshape(1, 2, BLOCK, D),
        input_grad.reshape(1, 2, BLOCK, D),
        qkv[None],
        vectors[B_QUERY],
        vectors[B_VALUE],
        out[None],
        vectors[B_OUT],
        up[None],
        vectors[8],
        down[None],
        vectors[B_DOWN],
        vectors[G_ONE],
        vectors[S_ONE],
        vectors[G_TWO],
        vectors[S_TWO],
    )


def solution(mesh):
    torus = Mesh(mesh.devices.reshape(2, 2, 4, 4, 2), AXES)
    rows, matrix, vector = P(None, DP, None), P("section", DP, None), P("section", DP)
    of_layer = P("section", None, DP, None)
    return jax.shard_map(
        body,
        mesh=torus,
        in_specs=(
            rows,
            P(None, DP),
            rows,
            matrix,
            vector,
            vector,
            matrix,
            vector,
            matrix,
            vector,
            matrix,
            vector,
            vector,
            vector,
            vector,
            vector,
        ),
        out_specs=(
            of_layer,
            of_layer,
            matrix,
            vector,
            vector,
            matrix,
            vector,
            matrix,
            vector,
            matrix,
            vector,
            vector,
            vector,
            vector,
            vector,
        ),
        check_vma=False,
    )
```

```python
import jax
import jax.numpy as jnp
from jax import lax
from jax.experimental import pallas as pl
from jax.experimental.pallas import tpu as pltpu
from jax.sharding import Mesh
from jax.sharding import PartitionSpec as P

HEADS = 16
D = 1024
FF = 4096
ROWS = 256
BLOCK = 128
QKV0, OUT0, UP0, NA = 128, 3200, 4224, 8320
HALF = 1664
AXES = ("section", "dp_0", "dp_1", "dp_2", "dp_3")
DP = AXES[1:]
MESH = pl.DeviceIdType.MESH
EPSILON = 1e-05
FAR = 1e30
ANY = pl.BlockSpec(memory_space=pl.ANY)
VMEM = pl.BlockSpec(memory_space=pltpu.VMEM)
SMEM = pl.BlockSpec(memory_space=pltpu.SMEM)
bf16 = jnp.bfloat16
f32 = jnp.float32


class Place:
    def __init__(self):
        self.s, self.yh, self.z, self.x, self.c = [lax.axis_index(a) for a in AXES]
        self.p = jnp.where(self.c == 0, self.z, self.x)
        self.q = jnp.where(self.c == 0, self.x, self.z)

    def zx(self, dp, dq):
        pp, qq = lax.rem(self.p + (dp + 4), 4), lax.rem(self.q + (dq + 4), 4)
        return jnp.where(self.c == 0, pp, qq), jnp.where(self.c == 0, qq, pp)

    def at(self, dp, dq):
        z, x = self.zx(dp, dq)
        return (self.s, self.yh, z, x, self.c)

    def half(self, r):
        return lax.rem(self.yh + r, 2)

    def over_y(self):
        return (self.s, 1 - self.yh, self.z, self.x, self.c)

    def other_core(self):
        return (self.s, self.yh, self.z, self.x, 1 - self.c)

    def neighbours(self):
        return (
            self.over_y(),
            self.other_core(),
            self.at(1, 0),
            self.at(-1, 0),
            self.at(0, 1),
            self.at(0, -1),
        )


def greet(devices):
    barrier = pltpu.get_barrier_semaphore()
    for device in devices:
        pl.semaphore_signal(barrier, inc=1, device_id=device, device_id_type=MESH)
    pl.semaphore_wait(barrier, len(devices))


class Mail:
    def __init__(self, send, recv):
        self.send, self.recv, self.sent, self.number = send, recv, {}, {}

    def post(self, name, src, dst, device):
        self.number.setdefault(name, len(self.number))
        self.sent[name] = (src, dst, device)
        self.copy(name).start()

    def copy(self, name):
        src, dst, device = self.sent[name]
        k = self.number[name]
        return pltpu.make_async_remote_copy(
            src_ref=src() if callable(src) else src,
            dst_ref=dst() if callable(dst) else dst,
            send_sem=self.send.at[k],
            recv_sem=self.recv.at[k],
            device_id=device,
            device_id_type=MESH,
        )

    def take(self, name, dst, device):
        k = self.number[name]
        pltpu.make_async_remote_copy(
            src_ref=dst,
            dst_ref=dst,
            send_sem=self.send.at[k],
            recv_sem=self.recv.at[k],
            device_id=device,
            device_id_type=MESH,
        ).wait_recv()

    def finish(self, names):
        for name in names:
            self.copy(name).wait_send()


def dot(a, b, dims=((1,), (0,))):
    return lax.dot_general(a, b, (dims, ((), ())), preferred_element_type=f32)


NT = ((1,), (1,))
TN = ((0,), (0,))


def cols(j, width, base=0):
    return pl.ds(pl.multiple_of(base + j * width, 128), width)


B_QUERY, B_VALUE, B_OUT, B_DOWN, G_ONE, S_ONE, G_TWO, S_TWO = range(8)
DOWN, UP, QKV, OUT = range(4)
KINDS = ((64, D, None), (16, FF, UP0), (16, 3 * D, QKV0), (16, D, OUT0))
COPIES = 68 + 2 * 63 + 4 * (2 + 6 + 6) + 3 + 4 + 6 + 4
RING_P, RING_Q, LAST = 32, 56, 62


def step_kernel(
    tokens,
    positions,
    cotangent,
    vec_tile,
    in_qkv,
    in_out,
    in_up,
    in_down,
    layer_out,
    input_grad,
    out_down,
    out_up,
    out_qkv,
    out_out,
    vec_out,
    w1,
    w2,
    xin,
    gyin,
    vec,
    b_up,
    b_qkv,
    xhat1,
    rstd1,
    xhat2,
    rstd2,
    mixed,
    far,
    probs,
    middle,
    gprime,
    act,
    grad,
    act_t,
    n2_t,
    n_t,
    a_t,
    l_down,
    l_up,
    l_qkv,
    l_out,
    r_down,
    r_up,
    r_qkv,
    r_out,
    block,
    block_down,
    vec_sum,
    vec_got,
    send,
    recv,
    load,
    *credits,
):
    at = Place()
    mail = Mail(send, recv)
    section = at.s
    first_section, second_section = section == 0, section == 1
    over_section = (1 - at.s, at.yh, at.z, at.x, at.c)
    my_index = ((at.yh * 4 + at.z) * 4 + at.x) * 2 + at.c
    right_p, left_p, right_q, left_q = at.at(1, 0), at.at(-1, 0), at.at(0, 1), at.at(0, -1)

    def shard_rows(index, rows):
        return pl.ds(pl.multiple_of(index * rows, rows), rows)

    here = shard_rows(my_index, 16)
    placing = [
        pltpu.make_async_copy(vec_tile, w1.at[here, pl.ds(0, 128)], load.at[0]),
        pltpu.make_async_copy(in_qkv, w1.at[here, pl.ds(QKV0, 3 * D)], load.at[1]),
        pltpu.make_async_copy(in_out, w1.at[here, pl.ds(OUT0, D)], load.at[2]),
        pltpu.make_async_copy(in_up, w1.at[here, pl.ds(UP0, FF)], load.at[3]),
        pltpu.make_async_copy(in_down, w2.at[shard_rows(my_index, 64), :], load.at[4]),
    ]
    for copy in placing:
        copy.start()
    greet((*at.neighbours(), over_section))


    def view(t, r, dp, dq, core=None, part=None):
        z, x = at.zx(dp, dq)
        index = ((at.half(r) * 4 + z) * 4 + x) * 2 + (at.c if core is None else core)
        if t == 2:
            return w2.at[shard_rows(index, 64), :]
        span = (pl.ds(0, OUT0), pl.ds(OUT0, NA - OUT0))[t]
        if part is not None:
            span = (pl.ds(0, HALF), pl.ds(HALF, OUT0 - HALF))[part]
        return w1.at[shard_rows(index, 16), span]

    def post(kind, t, r, dp, dq, device):
        v = view(t, r, dp, dq)
        mail.post((kind, t, r, dp, dq), v, v, device)

    def take(kind, t, sent, got):
        mail.take((kind, t, *sent), view(t, *got), right_p)

    def hand_over(t, r, dp, dq):
        post("C", t, r, dp, dq, at.other_core())

    def spread(t, r, dq):
        post("PR", t, r, 0, dq, right_p)
        post("PL", t, r, 0, dq, left_p)
        hand_over(t, r, 0, dq)

    def pass_on(t, dq):
        take("PR", t, (0, 0, dq), (0, -1, dq))
        post("PR2", t, 0, -1, dq, right_p)
        take("PL", t, (1, 0, dq), (1, 1, dq))
        post("PL2", t, 1, 1, dq, left_p)
        hand_over(t, 0, -1, dq)
        hand_over(t, 1, 1, dq)
        take("PL", t, (0, 0, dq), (0, 1, dq))
        take("PR", t, (1, 0, dq), (1, -1, dq))
        hand_over(t, 0, 1, dq)
        hand_over(t, 1, -1, dq)

    def gather_y_last():
        around = (0, -1, 1, 2)

        def post_half(kind, part, dp, dq, device):
            v = view(0, 0, dp, dq, part=part)
            mail.post((kind, dp, dq), v, v, device)

        def take_half(kind, part, sent, got):
            mail.take((kind, *sent), view(0, 0, *got, part=part), right_p)

        def onward(dp, dq):
            post("Y", 0, 0, dp, dq, at.over_y())
            hand_over(0, 0, dp, dq)

        def here(dq):
            post("PR", 0, 0, 0, dq, right_p)
            post("PL", 0, 0, 0, dq, left_p)
            onward(0, dq)

        def s0():
            post("QR", 0, 0, 0, 0, right_q)
            post("QL", 0, 0, 0, 0, left_q)
            here(0)

        def s1():
            take("QR", 0, (0, 0, 0), (0, 0, -1))
            post_half("QH", 0, 0, -1, right_q)
            here(-1)
            take("QL", 0, (0, 0, 0), (0, 0, 1))
            post_half("QG", 1, 0, 1, left_q)
            here(1)

        def s2():
            take_half("QH", 0, (0, -1), (0, -2))
            take_half("QG", 1, (0, 1), (0, 2))
            here(2)

        def s3(dq):
            take("PR", 0, (0, 0, dq), (0, -1, dq))
            post_half("PH", 0, -1, dq, right_p)
            onward(-1, dq)
            take("PL", 0, (0, 0, dq), (0, 1, dq))
            post_half("PG", 1, 1, dq, left_p)
            onward(1, dq)

        def s4():
            for dq in around:
                take_half("PH", 0, (-1, dq), (-2, dq))
                take_half("PG", 1, (1, dq), (2, dq))
                onward(2, dq)

        def from_y(dp, dqs):
            for dq in dqs:
                take("Y", 0, (0, dp, dq), (1, dp, dq))
                hand_over(0, 1, dp, dq)

        def over_y():
            from_y(0, around)
            from_y(-1, (0,))
            from_y(1, (0,))

        def over_y_too():
            for dq in (-1, 1, 2):
                from_y(-1, (dq,))
                from_y(1, (dq,))
            from_y(2, around)

        def s10():
            for r in range(2):
                for dp in around:
                    for dq in around:
                        name = ("C", 0, r, dp, dq)
                        mail.take(name, view(0, r, dq, dp, 1 - at.c), at.other_core())

        return [s0, s1, s2, *[lambda dq=dq: s3(dq) for dq in around], s4, over_y, over_y_too, s10]

    def gather_steps(t):
        def s0():
            post("QR", t, 0, 0, 0, right_q)
            post("QL", t, 0, 0, 0, left_q)
            spread(t, 0, 0)

        def s1():
            take("Y", t, (0, 0, 0), (1, 0, 0))
            post("QR", t, 1, 0, 0, right_q)
            post("QL", t, 1, 0, 0, left_q)
            spread(t, 1, 0)

        def s2():
            take("QR", t, (0, 0, 0), (0, 0, -1))
            post("QR2", t, 0, 0, -1, right_q)
            spread(t, 0, -1)
            take("QL", t, (0, 0, 0), (0, 0, 1))
            spread(t, 0, 1)

        def s3():
            take("QL", t, (1, 0, 0), (1, 0, 1))
            post("QL2", t, 1, 0, 1, left_q)
            spread(t, 1, 1)
            take("QR", t, (1, 0, 0), (1, 0, -1))
            spread(t, 1, -1)

        def s4():
            pass_on(t, 0)

        def s5():
            take("QR2", t, (0, 0, -1), (0, 0, -2))
            spread(t, 0, 2)
            take("QL2", t, (1, 0, 1), (1, 0, 2))
            spread(t, 1, 2)

        def s9():
            for dq in (0, -1, 1, 2):
                take("PR2", t, (0, -1, dq), (0, -2, dq))
                take("PL2", t, (1, 1, dq), (1, 2, dq))
                hand_over(t, 0, 2, dq)
                hand_over(t, 1, 2, dq)

        def s10():
            for r in range(2):
                for dp in (0, -1, 1, 2):
                    for dq in (0, -1, 1, 2):
                        name = ("C", t, r, dp, dq)
                        mail.take(name, view(t, r, dq, dp, 1 - at.c), at.other_core())

        passing = [lambda dq=dq: pass_on(t, dq) for dq in (-1, 1, 2)]
        return [s0, s1, s2, s3, s4, s5, *passing, s9, s10]


    chunk = BLOCK
    halves = (pl.ds(0, BLOCK), pl.ds(BLOCK, BLOCK))
    whole = pl.ds(0, ROWS)

    def rows_loop(body):
        for half in halves:
            body(half)

    g_y, g_branch = r_down.at[pl.ds(0, ROWS), :], r_out.at[pl.ds(0, ROWS), :]
    g_upward, g_mixed = r_up.at[pl.ds(0, ROWS), :], r_qkv.at[pl.ds(0, ROWS), :]
    normed, attended = g_branch, g_y

    row = lax.broadcasted_iota(jnp.int32, (BLOCK, BLOCK), 0)
    col = lax.broadcasted_iota(jnp.int32, (BLOCK, BLOCK), 1)
    low_lane = col < 64

    def make_far():
        distance = col - row
        for b in range(2):
            allowed = (distance >= 0) & (distance <= positions[pl.ds(b, 1), :])
            far[b] = jnp.where(allowed, distance.astype(f32), FAR).T

    def unpack_vectors():
        for j in range(8):
            tiles = [w1[pl.ds((8 * j + i) * 16, 16), pl.ds(0, 128)].astype(f32) for i in range(8)]
            pairs = [tiles[2 * i] + tiles[2 * i + 1] for i in range(4)]
            for i in range(4):
                b_up[:, pl.ds((4 * j + i) * 128, 128)] = pairs[i][8:16]
            vec[:, pl.ds(j * 128, 128)] = ((pairs[0] + pairs[1]) + (pairs[2] + pairs[3]))[0:8]
        b_qkv[pl.ds(0, 1), pl.ds(0, D)] = vec[pl.ds(B_QUERY, 1), :]
        b_qkv[pl.ds(0, 1), pl.ds(D, D)] = jnp.zeros((1, D), f32)
        b_qkv[pl.ds(0, 1), pl.ds(2 * D, D)] = vec[pl.ds(B_VALUE, 1), :]

    def norm_rows(rows, v, xhat, rstd, gain, shift):
        center = v - jnp.mean(v, axis=-1, keepdims=True)
        r = lax.rsqrt(jnp.mean(center * center, axis=-1, keepdims=True) + EPSILON)
        h = center * r
        xhat[rows, :] = h
        rstd[rows, :] = jnp.broadcast_to(r, (chunk, 128))
        return h * vec[pl.ds(gain, 1), :] + vec[pl.ds(shift, 1), :]

    def transpose_into(dst, src):
        @pl.loop(0, D // 256, unroll=True)
        def _(j):
            dst[pl.ds(j * 8, 8)] = src[:, cols(j, 256)].T.reshape(8, 2, 16, ROWS)

    def post_lhs(a):
        mail.post(("L", a), lhs_t[a].at[:, 1 - at.c], lhs_got[a], at.other_core())

    lhs_t, lhs_got = (act_t, n2_t, n_t, a_t), (l_down, l_up, l_qkv, l_out)
    rhs = (r_down, r_up, r_qkv, r_out)

    def norm_one(rows):
        v = xin[rows, :].astype(f32)
        normed[rows, :] = norm_rows(rows, v, xhat1, rstd1, G_ONE, S_ONE).astype(bf16)

    def project(lo, hi, rows=whole):
        @pl.loop(0, hi - lo, unroll=True)
        def _(i):
            j = i + lo
            y = dot(normed[rows, :], w1[:, cols(j, 512, QKV0)])
            mixed[rows, cols(j, 512)] = (y + b_qkv[pl.ds(0, 1), cols(j, 512)]).astype(bf16)

    def pair(value):
        zero = jnp.zeros_like(value)
        return jnp.concatenate(
            [jnp.where(low_lane, value, zero), jnp.where(low_lane, zero, value)], axis=0
        )

    def unpair(value):
        return jnp.where(low_lane, value[:BLOCK], value[BLOCK:])

    def slope_rows(hp):
        first = lax.broadcasted_iota(jnp.int32, (2 * BLOCK, 1), 0) < BLOCK
        h = ((2 * hp + 2) - first.astype(jnp.int32)).astype(f32)
        return jnp.exp(h * (-0.5 * 0.6931471805599453))

    def heads(ref, b, part, hp):
        return ref[pl.ds(b * BLOCK, BLOCK), cols(hp, 128, part * D)]

    def attend(lo, hi, blocks=(0, 1)):
        @pl.loop(0, hi - lo, unroll=True)
        def _(i):
            hp = i + lo
            slope = slope_rows(hp)
            for b in blocks:
                queries = pair(heads(mixed, b, 0, hp))
                scores = dot(queries, heads(mixed, b, 1, hp), NT) * 0.125
                gap = jnp.concatenate([far[b], far[b]], axis=0)
                scores = scores - slope * gap
                e = jnp.exp(scores - jnp.max(scores, axis=-1, keepdims=True))
                p = e * (1.0 / jnp.sum(e, axis=-1, keepdims=True))
                probs[2 * hp + b] = p
                out = unpair(dot(p.astype(bf16), heads(mixed, b, 2, hp)))
                attended[pl.ds(b * BLOCK, BLOCK), cols(hp, 128)] = out.astype(bf16)

    def branch():
        @pl.loop(0, 2, unroll=True)
        def _(j):
            y = dot(attended[...], w1[:, cols(j, 512, OUT0)])
            middle[:, cols(j, 512)] = (
                xin[:, cols(j, 512)].astype(f32) + y + vec[pl.ds(B_OUT, 1), cols(j, 512)]
            )

    def norm_two():
        def two(rows):
            v = middle[rows, :]
            normed[rows, :] = norm_rows(rows, v, xhat2, rstd2, G_TWO, S_TWO).astype(bf16)

        rows_loop(two)

    def rise(lo, hi):
        @pl.loop(0, hi - lo, unroll=True)
        def _(i):
            j = i + lo
            y = dot(normed[...], w1[:, cols(j, 512, UP0)])
            u = y + b_up[pl.ds(0, 1), cols(j, 512)]
            c = 0.7978845608028654
            uu = u * u
            t = jnp.tanh(c * (u + 0.044715 * u * uu))
            half = 0.5 * (1.0 + t)
            a = (u * half).astype(bf16)
            act[:, cols(j, 512)] = a
            act_t[pl.ds(j * 4, 4)] = a.T.reshape(4, 2, 64, ROWS)
            gprime[:, cols(j, 512)] = half + 0.5 * u * (1.0 - t * t) * (
                c * (1.0 + (3 * 0.044715) * uu)
            )

    def first_part():
        def start():
            rows_loop(norm_one)
            transpose_into(n_t, normed)

        def end():
            transpose_into(a_t, attended)

        return [
            start,
            *[lambda j=j: project(2 * j, 2 * j + 2) for j in range(3)],
            *[lambda j=j: attend(2 * j, 2 * j + 2) for j in range(4)],
            end,
        ]

    def second_part():
        def start():
            branch()

        def middle_piece():
            norm_two()
            transpose_into(n2_t, normed)

        return [start, middle_piece, *[lambda j=j: rise(2 * j, 2 * j + 2) for j in range(4)]]

    def weave(steps, pieces):
        done = 0
        for k, step in enumerate(steps):
            step()
            upto = (k + 1) * len(pieces) // len(steps)
            if upto > done:

                @pl.when(first_section)
                def _(todo=tuple(pieces[done:upto])):
                    for piece in todo:
                        piece()

            done = upto

    def hop(src, dst, b, k):
        return pltpu.make_async_remote_copy(
            src_ref=src.at[halves[b], :],
            dst_ref=dst.at[halves[b], :],
            send_sem=send.at[COPIES - k - b],
            recv_sem=recv.at[COPIES - k - b],
            device_id=over_section,
            device_id_type=MESH,
        )

    forth = [hop(layer_out, xin, b, 1) for b in range(2)]
    back = [hop(input_grad, gyin, b, 3) for b in range(2)]

    g0, g1, g2 = gather_y_last(), gather_steps(1), gather_steps(2)
    for copy in placing:
        copy.wait()
    for t in (1, 2):
        post("Y", t, 0, 0, 0, at.over_y())
    for step in (g0[0], g1[0], g2[0]):
        step()
    make_far()

    @pl.when(first_section)
    def _():
        xin[...] = tokens[...]

    for step in (g0[1], g0[2], g1[1], g0[3], g0[4], g2[1], g0[5], g0[6], g1[2], g0[7]):
        step()
    for step in (g1[3], g2[2], g1[4], g0[8], g1[5], g2[3], g1[6], g1[7], g2[4], g0[9]):
        step()
    for step in (g1[8], g2[5], g0[10]):
        step()
    unpack_vectors()
    weave([g1[9], g2[6], g1[10], g2[7], g2[8]], first_part())
    second = second_part()
    weave([lambda: None], second[:4])
    weave(g2[9:10], second[4:])
    g2[10]()

    gathered = list(mail.sent)

    @pl.when(second_section)
    def _():
        mail.finish(gathered)
        for b in range(2):
            forth[b].wait_recv()
            norm_one(halves[b])
            project(0, 6, halves[b])
            attend(0, 8, (b,))
        transpose_into(n_t, normed)
        transpose_into(a_t, attended)
        branch()
        norm_two()
        transpose_into(n2_t, normed)
        rise(0, 8)

    for a in (DOWN, UP, QKV, OUT):
        post_lhs(a)

    @pl.loop(0, 2, unroll=True)
    def _(j):
        y = dot(act[...], w2[:, cols(j, 512)])
        y = middle[:, cols(j, 512)] + y + vec[pl.ds(B_DOWN, 1), cols(j, 512)]
        layer_out[:, cols(j, 512)] = y.astype(bf16)


    def post_rhs(a):
        mine, other = pl.ds(0, ROWS), pl.ds(ROWS, ROWS)
        mail.post(("R", a), rhs[a].at[mine, :], rhs[a].at[other, :], at.other_core())

    sum_neighbours = (right_p, left_p, right_q, left_q, at.over_y())

    def give_room(a):
        for device in sum_neighbours:
            pl.semaphore_signal(credits[a], inc=1, device_id=device, device_id_type=MESH)

    def ready(a):
        mail.take(("L", a), lhs_got[a], at.other_core())
        mail.take(("R", a), rhs[a].at[pl.ds(ROWS, ROWS), :], at.other_core())
        pl.semaphore_wait(credits[a], len(sum_neighbours))

    def room(a, place, count=1):
        rows, width, base = KINDS[a]
        span = pl.ds(place * rows, count * rows)
        return w2.at[span, :] if base is None else w1.at[span, pl.ds(base, width)]

    def own(r, d, e=0):
        return (r * 4 + d) * 4 + e

    def products(a, d):
        rows, width, base = KINDS[a]
        buffer = block_down if rows == 64 else block
        for r in range(2):
            for e in range(4):
                z, x = at.zx(d, e)
                index = (at.half(r) * 4 + z) * 4 + x
                spot = pl.ds((r * 4 + e) * rows, rows)
                buffer[spot, pl.ds(0, ROWS)] = lhs_t[a][index, at.c]
                buffer[spot, pl.ds(ROWS, ROWS)] = lhs_got[a][index]

        @pl.loop(0, width // 512)
        def _(j):
            y = dot(buffer[...], rhs[a][:, cols(j, 512)]).astype(bf16)
            for r in range(2):
                span = pl.ds(own(r, d) * rows, 4 * rows)
                part = y[r * 4 * rows : (r + 1) * 4 * rows]
                if base is None:
                    w2[span, cols(j, 512)] = part
                else:
                    w1[span, cols(j, 512, base)] = part

    def total(a, dst, terms):
        @pl.loop(0, KINDS[a][1] // 512, unroll=True)
        def _(j):
            value = None
            for term in terms:
                piece = term[:, cols(j, 512)].astype(f32)
                value = piece if value is None else value + piece
            dst[:, cols(j, 512)] = value.astype(dst.dtype)

    def sum_p(a, r, d, *ks):
        dst = room(a, own(r, d), 4)
        total(a, dst, (dst, *[room(a, RING_P + 4 * k, 4) for k in ks]))

    def sum_q(a, r, e, *ks):
        dst = room(a, own(r, 0, e))
        total(a, dst, (dst, *[room(a, RING_Q + k) for k in ks]))

    def post_p(a, k, r, d, device):
        src, dst = lambda: room(a, own(r, d), 4), lambda: room(a, RING_P + 4 * k, 4)
        mail.post(("P", a, k), src, dst, device)

    def take_p(a, *ks):
        for k in ks:
            mail.take(("P", a, k), room(a, RING_P + 4 * k, 4), right_p)

    def post_q(a, k, r, e, device):
        mail.post(("Q", a, k), room(a, own(r, 0, e)), room(a, RING_Q + k), device)

    def take_q(a, *ks):
        for k in ks:
            mail.take(("Q", a, k), room(a, RING_Q + k), right_q)

    over_y = at.over_y()

    def post_y(d):
        src, dst = lambda: room(DOWN, own(1, d), 4), lambda: room(DOWN, 32 + 4 * d, 4)
        mail.post(("Z", d), src, dst, over_y)

    def take_y(d):
        mail.take(("Z", d), room(DOWN, 32 + 4 * d, 4), right_p)
        dst = room(DOWN, own(0, d), 4)
        total(DOWN, dst, (dst, room(DOWN, 32 + 4 * d, 4)))

    def down_p(d, e):
        return room(DOWN, own(0, d, e), 2)

    def down_ring_p(k):
        return room(DOWN, 48 + 2 * k, 2)

    def down_rows(e, half):
        return w2.at[pl.ds(own(0, 0, e) * 64 + 32 * half, 32), :]

    def down_ring_q(k):
        return w2.at[pl.ds(60 * 64 + 32 * k, 32), :]

    def down1(a):
        ready(DOWN)
        products(DOWN, 2)
        post_y(2)

    def down2(a):
        for d in (1, 3, 0):
            products(DOWN, d)
            post_y(d)

    def down_post(k, d, e, device):
        mail.post(("P", DOWN, k), down_p(d, e), down_ring_p(k), device)

    def down_take(*ks):
        for k in ks:
            mail.take(("P", DOWN, k), down_ring_p(k), right_p)

    def down3():
        take_y(2)
        down_post(0, 2, 0, right_p)
        down_post(1, 2, 2, left_p)

    def down4():
        take_y(1)
        down_post(2, 1, 2, right_p)

    def down5():
        take_y(3)
        down_post(3, 3, 0, left_p)

    def down6():
        down_take(0)
        total(DOWN, down_p(1, 0), (down_p(1, 0), down_ring_p(0)))
        down_post(4, 1, 0, right_p)
        down_take(1)
        total(DOWN, down_p(3, 2), (down_p(3, 2), down_ring_p(1)))
        down_post(5, 3, 2, left_p)

    def down_post_q(k, e, half, device):
        mail.post(("Q", DOWN, k), down_rows(e, half), down_ring_q(k), device)

    def down_take_q(*ks):
        for k in ks:
            mail.take(("Q", DOWN, k), down_ring_q(k), right_q)

    def down7():
        take_y(0)
        down_take(2, 3, 4, 5)
        total(DOWN, down_p(0, 2), (down_p(0, 2), down_ring_p(2), down_ring_p(5)))
        down_post_q(0, 2, 0, right_q)
        down_post_q(1, 2, 1, left_q)
        down_post_q(3, 3, 0, left_q)
        total(DOWN, down_p(0, 0), (down_p(0, 0), down_ring_p(4), down_ring_p(3)))
        down_post_q(2, 1, 1, right_q)

    def down8():
        down_take_q(0)
        total(DOWN, down_rows(1, 0), (down_rows(1, 0), down_ring_q(0)))
        down_post_q(4, 1, 0, right_q)
        down_take_q(1)
        total(DOWN, down_rows(3, 1), (down_rows(3, 1), down_ring_q(1)))
        down_post_q(5, 3, 1, left_q)

    def down9():
        down_take_q(2, 3, 4, 5)
        for half, k, m in ((0, 4, 3), (1, 2, 5)):
            terms = (down_rows(0, half), down_ring_q(k), down_ring_q(m))
            total(DOWN, out_down.at[pl.ds(32 * half, 32), :], terms)

    def a1(a):
        ready(a)
        products(a, 2)
        post_p(a, 0, 0, 2, right_p)
        post_p(a, 1, 1, 2, left_p)

    def a2(a):
        products(a, 1)
        post_p(a, 2, 1, 1, right_p)
        products(a, 3)
        post_p(a, 3, 0, 3, left_p)

    def a3(a):
        take_p(a, 0)
        sum_p(a, 0, 1, 0)
        post_p(a, 4, 0, 1, right_p)
        take_p(a, 1)
        sum_p(a, 1, 3, 1)
        post_p(a, 5, 1, 3, left_p)
        products(a, 0)

    def a4(a):
        take_p(a, 2, 3, 4, 5)
        sum_p(a, 0, 0, 4, 3)
        sum_p(a, 1, 0, 2, 5)
        post_q(a, 0, 0, 2, right_q)
        post_q(a, 1, 1, 2, left_q)
        post_q(a, 2, 1, 1, right_q)
        post_q(a, 3, 0, 3, left_q)

    def a5(a):
        take_q(a, 0)
        sum_q(a, 0, 1, 0)
        post_q(a, 4, 0, 1, right_q)
        take_q(a, 1)
        sum_q(a, 1, 3, 1)
        post_q(a, 5, 1, 3, left_q)

    def a6(a):
        take_q(a, 2, 3, 4, 5)
        sum_q(a, 1, 0, 2, 5)
        mail.post(("Y", a), room(a, own(1, 0)), room(a, LAST), at.over_y())

    outs = (out_down, out_up, out_qkv, out_out)

    def a7(a):
        mail.take(("Y", a), room(a, LAST), right_p)
        terms = (room(a, own(0, 0)), room(a, RING_Q + 4), room(a, RING_Q + 3), room(a, LAST))
        total(a, outs[a], terms)

    def when_first(*steps):
        @pl.when(first_section)
        def _():
            for step, a in steps:
                step(a)

    even_p, even_q = 1 - 2 * lax.rem(at.p, 2), 1 - 2 * lax.rem(at.q, 2)
    partners = (
        at.other_core(),
        at.at(even_p, 0),
        at.at(-even_p, 0),
        at.at(0, even_q),
        at.at(0, -even_q),
        at.over_y(),
    )

    def post_vec(k):
        mail.post(("V", k), vec_sum.at[k], vec_got.at[k], partners[k])

    def take_vec(k):
        mail.take(("V", k), vec_got.at[k], partners[k])
        vec_sum[k + 1] = vec_sum[k] + vec_got[k]


    g_vec = vec_sum.at[0]
    g_vec[...] = jnp.zeros((16, D), f32)

    def grad_up(rows):
        @pl.loop(0, 8, unroll=True)
        def _(j):
            g = dot(g_y[rows, :], w2[cols(j, 512), :], NT)
            g = (g * gprime[rows, cols(j, 512)]).astype(bf16)
            g_upward[rows, cols(j, 512)] = g
            spot = (pl.ds(8 + j // 2, 1), cols(j % 2, 512))
            g_vec[spot] = g_vec[spot] + jnp.sum(g.astype(f32), axis=0, keepdims=True)

    @pl.when(first_section)
    def _():
        for b in range(2):
            forth[b].start()
        mail.finish(gathered)
        for b in range(2):
            back[b].wait_recv()
            g_y[halves[b], :] = gyin[halves[b], :]
            grad_up(halves[b])

    @pl.when(second_section)
    def _():
        g_y[...] = cotangent[...]
        grad_up(whole)

    post_rhs(DOWN)
    post_rhs(UP)
    give_room(DOWN)

    @pl.loop(0, 4, unroll=True)
    def _(j):
        grad[:, cols(j, 256)] = dot(g_upward[...], w1[cols(j, 256), pl.ds(UP0, FF)], NT)

    give_room(UP)
    when_first((down1, DOWN), (a1, UP))

    def add(index, value):
        g_vec[pl.ds(index, 1), :] = g_vec[pl.ds(index, 1), :] + jnp.sum(
            value, axis=0, keepdims=True
        )

    def norm_back(rows, xhat, rstd, gain, shift):
        dy = grad[rows, :]
        h = xhat[rows, :]
        add(gain, dy * h)
        add(shift, dy)
        dh = dy * vec[pl.ds(gain, 1), :]
        m1 = jnp.mean(dh, axis=-1, keepdims=True)
        m2 = jnp.mean(dh * h, axis=-1, keepdims=True)
        return rstd[rows, pl.ds(0, 1)] * (dh - m1 - h * m2)

    def three(rows):
        gy = g_y[rows, :].astype(f32)
        gm = gy + norm_back(rows, xhat2, rstd2, G_TWO, S_TWO)
        add(B_DOWN, gy)
        middle[rows, :] = gm
        low = gm.astype(bf16)
        g_branch[rows, :] = low
        add(B_OUT, low.astype(f32))

    rows_loop(three)
    post_rhs(OUT)

    @pl.loop(0, 4, unroll=True)
    def _(j):
        y = dot(g_branch[...], w1[cols(j, 256), pl.ds(OUT0, D)], NT)
        act[:, cols(j, 256)] = y.astype(bf16)

    give_room(OUT)
    when_first((a2, UP), (down2, DOWN))

    def attend_back(lo, hi):
        @pl.loop(0, hi - lo, unroll=True)
        def _(i):
            hp = i + lo
            for b in range(2):
                queries = pair(heads(mixed, b, 0, hp))
                keys, values = heads(mixed, b, 1, hp), heads(mixed, b, 2, hp)
                da = pair(heads(act, b, 0, hp))
                p = probs[2 * hp + b]
                dv = dot(p.astype(bf16), da, TN)
                dp = dot(da, values, NT)
                delta = jnp.sum(p * dp, axis=-1, keepdims=True)
                ds = (p * (dp - delta)).astype(bf16)
                dq = unpair(dot(ds, keys)) * 0.125
                dk = dot(ds, queries, TN) * 0.125
                for part, value in enumerate((dq, dk, dv)):
                    span = (pl.ds(b * BLOCK, BLOCK), cols(hp, 128, part * D))
                    g_mixed[span] = value.astype(bf16)

    attend_back(0, 8)
    post_rhs(QKV)
    when_first((a3, UP))

    @pl.loop(0, 4, unroll=True)
    def _(j):
        grad[:, cols(j, 256)] = dot(g_mixed[...], w1[cols(j, 256), pl.ds(QKV0, 3 * D)], NT)

    give_room(QKV)

    def four(rows):
        gx = middle[rows, :] + norm_back(rows, xhat1, rstd1, G_ONE, S_ONE)
        input_grad[rows, :] = gx.astype(bf16)
        add(B_QUERY, g_mixed[rows, pl.ds(0, D)].astype(f32))
        add(B_VALUE, g_mixed[rows, pl.ds(2 * D, D)].astype(f32))

    for b in range(2):
        four(halves[b])

        @pl.when(second_section)
        def _(b=b):
            back[b].start()

    @pl.when(second_section)
    def _():
        for step, a in ((down1, DOWN), (a1, UP), (a2, UP), (down2, DOWN), (a3, UP)):
            step(a)

    post_vec(0)
    a1(QKV)
    a2(QKV)
    a1(OUT)
    a2(OUT)
    take_vec(0)
    post_vec(1)
    down3()
    a3(QKV)
    take_vec(1)
    post_vec(2)
    a3(OUT)
    down4()
    a4(UP)
    take_vec(2)
    post_vec(3)
    a4(QKV)
    a5(UP)
    a4(OUT)
    take_vec(3)
    post_vec(4)
    down5()
    down6()
    a6(UP)
    a5(QKV)
    a5(OUT)
    take_vec(4)
    post_vec(5)
    a6(QKV)
    a6(OUT)
    down7()
    a7(UP)
    take_vec(5)
    vec_out[...] = vec_sum[6]
    down8()
    a7(QKV)
    a7(OUT)
    down9()

    @pl.when(first_section)
    def _():
        for b in range(2):
            forth[b].wait_send()

    @pl.when(second_section)
    def _():
        for b in range(2):
            back[b].wait_send()

    mail.finish([name for name in mail.sent if name not in gathered])


def step(*args):
    def out(rows, columns, kind=bf16):
        return jax.ShapeDtypeStruct((rows, columns), kind)

    return pl.pallas_call(
        step_kernel,
        out_shape=(
            out(ROWS, D),
            out(ROWS, D),
            *[out(rows, width, f32) for rows, width, _ in KINDS],
            out(16, D, f32),
        ),
        in_specs=[VMEM, VMEM, VMEM, *[ANY] * 5],
        out_specs=(VMEM,) * 7,
        scratch_shapes=[
            pltpu.VMEM((D, NA), bf16),
            pltpu.VMEM((FF, D), bf16),
            pltpu.VMEM((ROWS, D), bf16),
            pltpu.VMEM((ROWS, D), bf16),
            pltpu.VMEM((8, D), f32),
            pltpu.VMEM((8, FF), f32),
            pltpu.VMEM((8, 3 * D), f32),
            pltpu.VMEM((ROWS, D), f32),
            pltpu.VMEM((ROWS, 128), f32),
            pltpu.VMEM((ROWS, D), f32),
            pltpu.VMEM((ROWS, 128), f32),
            pltpu.VMEM((ROWS, 3 * D), bf16),
            pltpu.VMEM((2, BLOCK, BLOCK), f32),
            pltpu.VMEM((16, 2 * BLOCK, BLOCK), f32),
            pltpu.VMEM((ROWS, D), f32),
            pltpu.VMEM((ROWS, FF), f32),
            pltpu.VMEM((ROWS, FF), bf16),
            pltpu.VMEM((ROWS, D), f32),
            *[pltpu.VMEM((32, 2, rows, ROWS), bf16) for rows, _, _ in KINDS],
            *[pltpu.VMEM((32, rows, ROWS), bf16) for rows, _, _ in KINDS],
            *[pltpu.VMEM((2 * ROWS, width), bf16) for _, width, _ in KINDS],
            pltpu.VMEM((128, 2 * ROWS), bf16),
            pltpu.VMEM((512, 2 * ROWS), bf16),
            pltpu.VMEM((7, 16, D), f32),
            pltpu.VMEM((6, 16, D), f32),
            pltpu.SemaphoreType.DMA((COPIES,)),
            pltpu.SemaphoreType.DMA((COPIES,)),
            pltpu.SemaphoreType.DMA((5,)),
            *[pltpu.SemaphoreType.REGULAR] * 4,
        ],
        compiler_params=pltpu.CompilerParams(
            collective_id=0, has_side_effects=True, vmem_limit_bytes=62 * 2**20
        ),
        name="step",
    )(*args)


def lay_out_kernel(index, *refs):
    big_in, sums_in, big_out, vectors = refs[:6], refs[6], refs[7:13], refs[13:22]
    held, (sums, came, left) = refs[22:28], refs[28:]
    first = pltpu.make_async_copy(sums_in, sums, came.at[6])
    first.start()
    come = [pltpu.make_async_copy(big_in[k], held[k], came.at[k]) for k in range(6)]
    leave = [pltpu.make_async_copy(held[k], big_out[k], left.at[k]) for k in range(6)]
    for copy in come:
        copy.start()
    for k in range(6):
        come[k].wait()
        leave[k].start()
    first.wait()
    i = index[0]
    own = sums[pl.ds(0, 8), cols(i // 8, 128)]
    own = pltpu.roll(own, lax.rem(128 - lax.rem(i, 8) * 16, 128), 1)
    for k in range(8):
        vectors[k][...] = own[k : k + 1, 0:16]
    rows = sums[pl.ds(8, 8), cols(lax.rem(i, 16) // 2, 128)]
    rows = pltpu.roll(rows, lax.rem(128 - lax.rem(i, 2) * 64, 128), 1)
    row = lax.broadcasted_iota(jnp.int32, (8, 128), 0) == i // 16
    vectors[8][...] = jnp.sum(jnp.where(row, rows, 0.0), axis=0, keepdims=True)[:, 0:64]
    for copy in leave:
        copy.wait()


def lay_out(index, big, sums):
    return pl.pallas_call(
        lay_out_kernel,
        out_shape=(
            *[jax.ShapeDtypeStruct(v.shape, v.dtype) for v in big],
            *[jax.ShapeDtypeStruct((1, 16), f32)] * 8,
            jax.ShapeDtypeStruct((1, 64), f32),
        ),
        in_specs=[SMEM, *[ANY] * 7],
        out_specs=(*[ANY] * 6, *[VMEM] * 9),
        scratch_shapes=[
            *[pltpu.VMEM(v.shape, v.dtype) for v in big],
            pltpu.VMEM((16, D), f32),
            pltpu.SemaphoreType.DMA((7,)),
            pltpu.SemaphoreType.DMA((6,)),
        ],
        compiler_params=pltpu.CompilerParams(vmem_limit_bytes=62 * 2**20),
        name="lay_out",
    )(index, *big, sums)


def body(
    tokens,
    positions,
    cotangent,
    w_qkv,
    b_query,
    b_value,
    w_out,
    b_out,
    w_up,
    b_up,
    w_down,
    b_down,
    gain_one,
    shift_one,
    gain_two,
    shift_two,
):
    index = lax.axis_index(DP)
    small = (b_query, b_value, b_out, b_down, gain_one, shift_one, gain_two, shift_two)
    lane = jnp.arange(128)[None]
    rows = jnp.tile(jnp.concatenate(small, axis=0), (1, 8))
    rows = jnp.where(lane // 16 == index % 8, rows, jnp.zeros_like(rows))
    wide = jnp.tile(b_up, (8, 2))
    wide = jnp.where(lane // 64 == index % 2, wide, jnp.zeros_like(wide))
    *big, sums = step(
        tokens.reshape(ROWS, D),
        positions,
        cotangent.reshape(ROWS, D),
        jnp.concatenate([rows, wide], axis=0),
        w_qkv[0],
        w_out[0],
        w_up[0],
        w_down[0],
    )
    layer_out, input_grad, down, up, qkv, out, *vectors = lay_out(
        jnp.reshape(index, (1,)).astype(jnp.int32), big, sums
    )
    return (
        layer_out.reshape(1, 2, BLOCK, D),
        input_grad.reshape(1, 2, BLOCK, D),
        qkv[None],
        vectors[B_QUERY],
        vectors[B_VALUE],
        out[None],
        vectors[B_OUT],
        up[None],
        vectors[8],
        down[None],
        vectors[B_DOWN],
        vectors[G_ONE],
        vectors[S_ONE],
        vectors[G_TWO],
        vectors[S_TWO],
    )


def solution(mesh):
    torus = Mesh(mesh.devices.reshape(2, 2, 4, 4, 2), AXES)
    rows, matrix, vector = P(None, DP, None), P("section", DP, None), P("section", DP)
    of_layer = P("section", None, DP, None)
    return jax.shard_map(
        body,
        mesh=torus,
        in_specs=(
            rows,
            P(None, DP),
            rows,
            matrix,
            vector,
            vector,
            matrix,
            vector,
            matrix,
            vector,
            matrix,
            vector,
            vector,
            vector,
            vector,
            vector,
        ),
        out_specs=(
            of_layer,
            of_layer,
            matrix,
            vector,
            vector,
            matrix,
            vector,
            matrix,
            vector,
            matrix,
            vector,
            vector,
            vector,
            vector,
            vector,
        ),
        check_vma=False,
    )
```

```python
import jax
import jax.numpy as jnp
from jax import lax
from jax.experimental import pallas as pl
from jax.experimental.pallas import tpu as pltpu
from jax.sharding import Mesh
from jax.sharding import PartitionSpec as P

HEADS = 16
D = 1024
FF = 4096
ROWS = 256
BLOCK = 128
QKV0, OUT0, UP0, NA = 128, 3200, 4224, 8320
HALF = 1664
AXES = ("section", "dp_0", "dp_1", "dp_2", "dp_3")
DP = AXES[1:]
MESH = pl.DeviceIdType.MESH
EPSILON = 1e-05
FAR = 1e30
ANY = pl.BlockSpec(memory_space=pl.ANY)
VMEM = pl.BlockSpec(memory_space=pltpu.VMEM)
SMEM = pl.BlockSpec(memory_space=pltpu.SMEM)
bf16 = jnp.bfloat16
f32 = jnp.float32


class Place:
    def __init__(self):
        self.s, self.yh, self.z, self.x, self.c = [lax.axis_index(a) for a in AXES]
        self.p = jnp.where(self.c == 0, self.z, self.x)
        self.q = jnp.where(self.c == 0, self.x, self.z)

    def zx(self, dp, dq):
        pp, qq = lax.rem(self.p + (dp + 4), 4), lax.rem(self.q + (dq + 4), 4)
        return jnp.where(self.c == 0, pp, qq), jnp.where(self.c == 0, qq, pp)

    def at(self, dp, dq):
        z, x = self.zx(dp, dq)
        return (self.s, self.yh, z, x, self.c)

    def half(self, r):
        return lax.rem(self.yh + r, 2)

    def over_y(self):
        return (self.s, 1 - self.yh, self.z, self.x, self.c)

    def other_core(self):
        return (self.s, self.yh, self.z, self.x, 1 - self.c)

    def neighbours(self):
        return (
            self.over_y(),
            self.other_core(),
            self.at(1, 0),
            self.at(-1, 0),
            self.at(0, 1),
            self.at(0, -1),
        )


def greet(devices):
    barrier = pltpu.get_barrier_semaphore()
    for device in devices:
        pl.semaphore_signal(barrier, inc=1, device_id=device, device_id_type=MESH)
    pl.semaphore_wait(barrier, len(devices))


class Mail:
    def __init__(self, send, recv):
        self.send, self.recv, self.sent, self.number = send, recv, {}, {}

    def post(self, name, src, dst, device):
        self.number.setdefault(name, len(self.number))
        self.sent[name] = (src, dst, device)
        self.copy(name).start()

    def copy(self, name):
        src, dst, device = self.sent[name]
        k = self.number[name]
        return pltpu.make_async_remote_copy(
            src_ref=src() if callable(src) else src,
            dst_ref=dst() if callable(dst) else dst,
            send_sem=self.send.at[k],
            recv_sem=self.recv.at[k],
            device_id=device,
            device_id_type=MESH,
        )

    def take(self, name, dst, device):
        k = self.number[name]
        pltpu.make_async_remote_copy(
            src_ref=dst,
            dst_ref=dst,
            send_sem=self.send.at[k],
            recv_sem=self.recv.at[k],
            device_id=device,
            device_id_type=MESH,
        ).wait_recv()

    def finish(self, names):
        for name in names:
            self.copy(name).wait_send()


def dot(a, b, dims=((1,), (0,))):
    return lax.dot_general(a, b, (dims, ((), ())), preferred_element_type=f32)


NT = ((1,), (1,))
TN = ((0,), (0,))


def cols(j, width, base=0):
    return pl.ds(pl.multiple_of(base + j * width, 128), width)


def tiles(lo, hi, step):
    def run(body):
        @pl.loop(0, (hi - lo) // step)
        def _(i):
            for k in range(step):
                body(lo + i * step + k)

    return run


B_QUERY, B_VALUE, B_OUT, B_DOWN, G_ONE, S_ONE, G_TWO, S_TWO = range(8)
DOWN, UP, QKV, OUT = range(4)
KINDS = ((64, D, None), (16, FF, UP0), (16, 3 * D, QKV0), (16, D, OUT0))
COPIES = 68 + 2 * 63 + 4 * (2 + 6 + 6) + 3 + 4 + 6 + 4
RING_P, RING_Q, LAST = 32, 56, 62


def step_kernel(
    tokens,
    positions,
    cotangent,
    vec_tile,
    in_qkv,
    in_out,
    in_up,
    in_down,
    layer_out,
    input_grad,
    out_down,
    out_up,
    out_qkv,
    out_out,
    vec_out,
    w1,
    w2,
    xin,
    gyin,
    vec,
    b_up,
    b_qkv,
    xhat1,
    rstd1,
    xhat2,
    rstd2,
    mixed,
    far,
    probs,
    middle,
    gprime,
    act,
    grad,
    act_t,
    n2_t,
    n_t,
    a_t,
    l_down,
    l_up,
    l_qkv,
    l_out,
    r_down,
    r_up,
    r_qkv,
    r_out,
    block,
    block_down,
    vec_sum,
    vec_got,
    send,
    recv,
    load,
    *credits,
):
    at = Place()
    mail = Mail(send, recv)
    section = at.s
    first_section, second_section = section == 0, section == 1
    over_section = (1 - at.s, at.yh, at.z, at.x, at.c)
    my_index = ((at.yh * 4 + at.z) * 4 + at.x) * 2 + at.c
    right_p, left_p, right_q, left_q = at.at(1, 0), at.at(-1, 0), at.at(0, 1), at.at(0, -1)

    def shard_rows(index, rows):
        return pl.ds(pl.multiple_of(index * rows, rows), rows)

    here = shard_rows(my_index, 16)
    placing = [
        pltpu.make_async_copy(vec_tile, w1.at[here, pl.ds(0, 128)], load.at[0]),
        pltpu.make_async_copy(in_qkv, w1.at[here, pl.ds(QKV0, 3 * D)], load.at[1]),
        pltpu.make_async_copy(in_out, w1.at[here, pl.ds(OUT0, D)], load.at[2]),
        pltpu.make_async_copy(in_up, w1.at[here, pl.ds(UP0, FF)], load.at[3]),
        pltpu.make_async_copy(in_down, w2.at[shard_rows(my_index, 64), :], load.at[4]),
    ]
    for copy in placing:
        copy.start()
    rows_in = {
        0: pltpu.make_async_copy(tokens, xin, load.at[5]),
        1: pltpu.make_async_copy(cotangent, gyin, load.at[5]),
    }

    @pl.when(first_section)
    def _():
        rows_in[0].start()

    @pl.when(second_section)
    def _():
        rows_in[1].start()

    greet((*at.neighbours(), over_section))


    def view(t, r, dp, dq, core=None, part=None):
        z, x = at.zx(dp, dq)
        index = ((at.half(r) * 4 + z) * 4 + x) * 2 + (at.c if core is None else core)
        if t == 2:
            return w2.at[shard_rows(index, 64), :]
        span = (pl.ds(0, OUT0), pl.ds(OUT0, NA - OUT0))[t]
        if part is not None:
            span = (pl.ds(0, HALF), pl.ds(HALF, OUT0 - HALF))[part]
        return w1.at[shard_rows(index, 16), span]

    def post(kind, t, r, dp, dq, device):
        v = view(t, r, dp, dq)
        mail.post((kind, t, r, dp, dq), v, v, device)

    def take(kind, t, sent, got):
        mail.take((kind, t, *sent), view(t, *got), right_p)

    def hand_over(t, r, dp, dq):
        post("C", t, r, dp, dq, at.other_core())

    def spread(t, r, dq):
        post("PR", t, r, 0, dq, right_p)
        post("PL", t, r, 0, dq, left_p)
        hand_over(t, r, 0, dq)

    def pass_on(t, dq):
        take("PR", t, (0, 0, dq), (0, -1, dq))
        post("PR2", t, 0, -1, dq, right_p)
        take("PL", t, (1, 0, dq), (1, 1, dq))
        post("PL2", t, 1, 1, dq, left_p)
        hand_over(t, 0, -1, dq)
        hand_over(t, 1, 1, dq)
        take("PL", t, (0, 0, dq), (0, 1, dq))
        take("PR", t, (1, 0, dq), (1, -1, dq))
        hand_over(t, 0, 1, dq)
        hand_over(t, 1, -1, dq)

    def gather_y_last():
        around = (0, -1, 1, 2)

        def post_half(kind, part, dp, dq, device):
            v = view(0, 0, dp, dq, part=part)
            mail.post((kind, dp, dq), v, v, device)

        def take_half(kind, part, sent, got):
            mail.take((kind, *sent), view(0, 0, *got, part=part), right_p)

        def onward(dp, dq):
            post("Y", 0, 0, dp, dq, at.over_y())
            hand_over(0, 0, dp, dq)

        def here(dq):
            post("PR", 0, 0, 0, dq, right_p)
            post("PL", 0, 0, 0, dq, left_p)
            onward(0, dq)

        def s0():
            post("QR", 0, 0, 0, 0, right_q)
            post("QL", 0, 0, 0, 0, left_q)
            here(0)

        def s1():
            take("QR", 0, (0, 0, 0), (0, 0, -1))
            post_half("QH", 0, 0, -1, right_q)
            here(-1)
            take("QL", 0, (0, 0, 0), (0, 0, 1))
            post_half("QG", 1, 0, 1, left_q)
            here(1)

        def s2():
            take_half("QH", 0, (0, -1), (0, -2))
            take_half("QG", 1, (0, 1), (0, 2))
            here(2)

        def s3(dq):
            take("PR", 0, (0, 0, dq), (0, -1, dq))
            post_half("PH", 0, -1, dq, right_p)
            onward(-1, dq)
            take("PL", 0, (0, 0, dq), (0, 1, dq))
            post_half("PG", 1, 1, dq, left_p)
            onward(1, dq)

        def s4():
            for dq in around:
                take_half("PH", 0, (-1, dq), (-2, dq))
                take_half("PG", 1, (1, dq), (2, dq))
                onward(2, dq)

        def from_y(dp, dqs):
            for dq in dqs:
                take("Y", 0, (0, dp, dq), (1, dp, dq))
                hand_over(0, 1, dp, dq)

        def over_y():
            from_y(0, around)
            from_y(-1, (0,))
            from_y(1, (0,))

        def over_y_too():
            for dq in (-1, 1, 2):
                from_y(-1, (dq,))
                from_y(1, (dq,))
            from_y(2, around)

        def s10():
            for r in range(2):
                for dp in around:
                    for dq in around:
                        name = ("C", 0, r, dp, dq)
                        mail.take(name, view(0, r, dq, dp, 1 - at.c), at.other_core())

        return [s0, s1, s2, *[lambda dq=dq: s3(dq) for dq in around], s4, over_y, over_y_too, s10]

    def gather_steps(t):
        def s0():
            post("QR", t, 0, 0, 0, right_q)
            post("QL", t, 0, 0, 0, left_q)
            spread(t, 0, 0)

        def s1():
            take("Y", t, (0, 0, 0), (1, 0, 0))
            post("QR", t, 1, 0, 0, right_q)
            post("QL", t, 1, 0, 0, left_q)
            spread(t, 1, 0)

        def s2():
            take("QR", t, (0, 0, 0), (0, 0, -1))
            post("QR2", t, 0, 0, -1, right_q)
            spread(t, 0, -1)
            take("QL", t, (0, 0, 0), (0, 0, 1))
            spread(t, 0, 1)

        def s3():
            take("QL", t, (1, 0, 0), (1, 0, 1))
            post("QL2", t, 1, 0, 1, left_q)
            spread(t, 1, 1)
            take("QR", t, (1, 0, 0), (1, 0, -1))
            spread(t, 1, -1)

        def s4():
            pass_on(t, 0)

        def s5():
            take("QR2", t, (0, 0, -1), (0, 0, -2))
            spread(t, 0, 2)
            take("QL2", t, (1, 0, 1), (1, 0, 2))
            spread(t, 1, 2)

        def s9():
            for dq in (0, -1, 1, 2):
                take("PR2", t, (0, -1, dq), (0, -2, dq))
                take("PL2", t, (1, 1, dq), (1, 2, dq))
                hand_over(t, 0, 2, dq)
                hand_over(t, 1, 2, dq)

        def s10():
            for r in range(2):
                for dp in (0, -1, 1, 2):
                    for dq in (0, -1, 1, 2):
                        name = ("C", t, r, dp, dq)
                        mail.take(name, view(t, r, dq, dp, 1 - at.c), at.other_core())

        passing = [lambda dq=dq: pass_on(t, dq) for dq in (-1, 1, 2)]
        return [s0, s1, s2, s3, s4, s5, *passing, s9, s10]


    chunk = BLOCK
    halves = (pl.ds(0, BLOCK), pl.ds(BLOCK, BLOCK))
    whole = pl.ds(0, ROWS)

    def rows_loop(body):
        for half in halves:
            body(half)

    g_y, g_branch = r_down.at[pl.ds(0, ROWS), :], r_out.at[pl.ds(0, ROWS), :]
    g_upward, g_mixed = r_up.at[pl.ds(0, ROWS), :], r_qkv.at[pl.ds(0, ROWS), :]
    normed, attended = g_branch, g_y

    row = lax.broadcasted_iota(jnp.int32, (BLOCK, BLOCK), 0)
    col = lax.broadcasted_iota(jnp.int32, (BLOCK, BLOCK), 1)
    low_lane = col < 64

    def make_far():
        distance = col - row
        for b in range(2):
            allowed = (distance >= 0) & (distance <= positions[pl.ds(b, 1), :])
            far[b] = jnp.where(allowed, distance.astype(f32), FAR).T

    def unpack_vectors():
        for j in range(8):
            tiles = [w1[pl.ds((8 * j + i) * 16, 16), pl.ds(0, 128)].astype(f32) for i in range(8)]
            pairs = [tiles[2 * i] + tiles[2 * i + 1] for i in range(4)]
            for i in range(4):
                b_up[:, pl.ds((4 * j + i) * 128, 128)] = pairs[i][8:16]
            vec[:, pl.ds(j * 128, 128)] = ((pairs[0] + pairs[1]) + (pairs[2] + pairs[3]))[0:8]
        b_qkv[pl.ds(0, 1), pl.ds(0, D)] = vec[pl.ds(B_QUERY, 1), :]
        b_qkv[pl.ds(0, 1), pl.ds(D, D)] = jnp.zeros((1, D), f32)
        b_qkv[pl.ds(0, 1), pl.ds(2 * D, D)] = vec[pl.ds(B_VALUE, 1), :]

    def norm_rows(rows, v, xhat, rstd, gain, shift):
        center = v - jnp.mean(v, axis=-1, keepdims=True)
        r = lax.rsqrt(jnp.mean(center * center, axis=-1, keepdims=True) + EPSILON)
        h = center * r
        xhat[rows, :] = h
        rstd[rows, :] = jnp.broadcast_to(r, (chunk, 128))
        return h * vec[pl.ds(gain, 1), :] + vec[pl.ds(shift, 1), :]

    def transpose_into(dst, src):
        @pl.loop(0, D // 256, unroll=True)
        def _(j):
            dst[pl.ds(j * 8, 8)] = src[:, cols(j, 256)].T.reshape(8, 2, 16, ROWS)

    def post_lhs(a):
        mail.post(("L", a), lhs_t[a].at[:, 1 - at.c], lhs_got[a], at.other_core())

    lhs_t, lhs_got = (act_t, n2_t, n_t, a_t), (l_down, l_up, l_qkv, l_out)
    rhs = (r_down, r_up, r_qkv, r_out)

    def norm_one(rows):
        v = xin[rows, :].astype(f32)
        normed[rows, :] = norm_rows(rows, v, xhat1, rstd1, G_ONE, S_ONE).astype(bf16)

    def project(lo, hi, rows=whole, step=1):
        @tiles(lo, hi, step)
        def _(j):
            y = dot(normed[rows, :], w1[:, cols(j, 512, QKV0)])
            mixed[rows, cols(j, 512)] = (y + b_qkv[pl.ds(0, 1), cols(j, 512)]).astype(bf16)

    def pair(value):
        zero = jnp.zeros_like(value)
        return jnp.concatenate(
            [jnp.where(low_lane, value, zero), jnp.where(low_lane, zero, value)], axis=0
        )

    def unpair(value):
        return jnp.where(low_lane, value[:BLOCK], value[BLOCK:])

    def slope_rows(hp):
        first = lax.broadcasted_iota(jnp.int32, (2 * BLOCK, 1), 0) < BLOCK
        h = ((2 * hp + 2) - first.astype(jnp.int32)).astype(f32)
        return jnp.exp(h * (-0.5 * 0.6931471805599453))

    def heads(ref, b, part, hp):
        return ref[pl.ds(b * BLOCK, BLOCK), cols(hp, 128, part * D)]

    def attend(lo, hi, blocks=(0, 1), step=1):
        @tiles(lo, hi, step)
        def _(hp):
            slope = slope_rows(hp)
            for b in blocks:
                queries = pair(heads(mixed, b, 0, hp))
                scores = dot(queries, heads(mixed, b, 1, hp), NT) * 0.125
                gap = jnp.concatenate([far[b], far[b]], axis=0)
                scores = scores - slope * gap
                e = jnp.exp(scores - jnp.max(scores, axis=-1, keepdims=True))
                p = e * (1.0 / jnp.sum(e, axis=-1, keepdims=True))
                probs[2 * hp + b] = p
                out = unpair(dot(p.astype(bf16), heads(mixed, b, 2, hp)))
                attended[pl.ds(b * BLOCK, BLOCK), cols(hp, 128)] = out.astype(bf16)

    def branch():
        @pl.loop(0, 2, unroll=True)
        def _(j):
            y = dot(attended[...], w1[:, cols(j, 512, OUT0)])
            middle[:, cols(j, 512)] = (
                xin[:, cols(j, 512)].astype(f32) + y + vec[pl.ds(B_OUT, 1), cols(j, 512)]
            )

    def norm_two():
        def two(rows):
            v = middle[rows, :]
            normed[rows, :] = norm_rows(rows, v, xhat2, rstd2, G_TWO, S_TWO).astype(bf16)

        rows_loop(two)

    def rise(lo, hi, step=1):
        @tiles(lo, hi, step)
        def _(j):
            y = dot(normed[...], w1[:, cols(j, 512, UP0)])
            u = y + b_up[pl.ds(0, 1), cols(j, 512)]
            c = 0.7978845608028654
            uu = u * u
            t = jnp.tanh(c * (u + 0.044715 * u * uu))
            half = 0.5 * (1.0 + t)
            a = (u * half).astype(bf16)
            act[:, cols(j, 512)] = a
            act_t[pl.ds(j * 4, 4)] = a.T.reshape(4, 2, 64, ROWS)
            gprime[:, cols(j, 512)] = half + 0.5 * u * (1.0 - t * t) * (
                c * (1.0 + (3 * 0.044715) * uu)
            )

    def first_part():
        def start():
            rows_loop(norm_one)
            transpose_into(n_t, normed)

        def end():
            transpose_into(a_t, attended)

        return [
            start,
            *[lambda j=j: project(2 * j, 2 * j + 2, step=2) for j in range(3)],
            *[lambda j=j: attend(2 * j, 2 * j + 2, step=2) for j in range(4)],
            end,
        ]

    def second_part():
        def start():
            branch()

        def middle_piece():
            norm_two()
            transpose_into(n2_t, normed)

        return [start, middle_piece, *[lambda j=j: rise(2 * j, 2 * j + 2, 2) for j in range(4)]]

    def weave(steps, pieces):
        done = 0
        for k, step in enumerate(steps):
            step()
            upto = (k + 1) * len(pieces) // len(steps)
            if upto > done:

                @pl.when(first_section)
                def _(todo=tuple(pieces[done:upto])):
                    for piece in todo:
                        piece()

            done = upto

    def hop(src, dst, b, k):
        return pltpu.make_async_remote_copy(
            src_ref=src.at[halves[b], :],
            dst_ref=dst.at[halves[b], :],
            send_sem=send.at[COPIES - k - b],
            recv_sem=recv.at[COPIES - k - b],
            device_id=over_section,
            device_id_type=MESH,
        )

    forth = [hop(layer_out, xin, b, 1) for b in range(2)]
    back = [hop(input_grad, gyin, b, 3) for b in range(2)]

    g0, g1, g2 = gather_y_last(), gather_steps(1), gather_steps(2)
    for copy in placing:
        copy.wait()
    for t in (1, 2):
        post("Y", t, 0, 0, 0, at.over_y())
    for step in (g0[0], g1[0], g2[0]):
        step()
    make_far()

    @pl.when(first_section)
    def _():
        rows_in[0].wait()

    for step in (g0[1], g0[2], g1[1], g0[3], g0[4], g2[1], g0[5], g0[6], g1[2], g0[7]):
        step()
    for step in (g1[3], g2[2], g1[4], g0[8], g1[5], g2[3], g1[6], g1[7], g2[4], g0[9]):
        step()
    for step in (g1[8], g2[5], g0[10]):
        step()
    unpack_vectors()
    weave([g1[9], g2[6], g1[10], g2[7], g2[8]], first_part())
    second = second_part()
    weave([lambda: None], second[:4])
    weave(g2[9:10], second[4:])
    g2[10]()

    gathered = list(mail.sent)

    @pl.when(second_section)
    def _():
        mail.finish(gathered)
        for b in range(2):
            forth[b].wait_recv()
            norm_one(halves[b])
            project(0, 6, halves[b], 3)
            attend(0, 8, (b,), 4)
        transpose_into(n_t, normed)
        transpose_into(a_t, attended)
        branch()
        norm_two()
        transpose_into(n2_t, normed)
        rise(0, 8, 4)

    for a in (DOWN, UP, QKV, OUT):
        post_lhs(a)

    @pl.loop(0, 2, unroll=True)
    def _(j):
        y = dot(act[...], w2[:, cols(j, 512)])
        y = middle[:, cols(j, 512)] + y + vec[pl.ds(B_DOWN, 1), cols(j, 512)]
        layer_out[:, cols(j, 512)] = y.astype(bf16)


    def post_rhs(a):
        mine, other = pl.ds(0, ROWS), pl.ds(ROWS, ROWS)
        mail.post(("R", a), rhs[a].at[mine, :], rhs[a].at[other, :], at.other_core())

    sum_neighbours = (right_p, left_p, right_q, left_q, at.over_y())

    def give_room(a):
        for device in sum_neighbours:
            pl.semaphore_signal(credits[a], inc=1, device_id=device, device_id_type=MESH)

    def ready(a):
        mail.take(("L", a), lhs_got[a], at.other_core())
        mail.take(("R", a), rhs[a].at[pl.ds(ROWS, ROWS), :], at.other_core())
        pl.semaphore_wait(credits[a], len(sum_neighbours))

    def room(a, place, count=1):
        rows, width, base = KINDS[a]
        span = pl.ds(place * rows, count * rows)
        return w2.at[span, :] if base is None else w1.at[span, pl.ds(base, width)]

    def own(r, d, e=0):
        return (r * 4 + d) * 4 + e

    def products(a, d):
        rows, width, base = KINDS[a]
        buffer = block_down if rows == 64 else block
        for r in range(2):
            for e in range(4):
                z, x = at.zx(d, e)
                index = (at.half(r) * 4 + z) * 4 + x
                spot = pl.ds((r * 4 + e) * rows, rows)
                buffer[spot, pl.ds(0, ROWS)] = lhs_t[a][index, at.c]
                buffer[spot, pl.ds(ROWS, ROWS)] = lhs_got[a][index]

        @pl.loop(0, width // 512)
        def _(j):
            y = dot(buffer[...], rhs[a][:, cols(j, 512)]).astype(bf16)
            for r in range(2):
                span = pl.ds(own(r, d) * rows, 4 * rows)
                part = y[r * 4 * rows : (r + 1) * 4 * rows]
                if base is None:
                    w2[span, cols(j, 512)] = part
                else:
                    w1[span, cols(j, 512, base)] = part

    def total(a, dst, terms):
        @pl.loop(0, KINDS[a][1] // 512)
        def _(j):
            value = None
            for term in terms:
                piece = term[:, cols(j, 512)].astype(f32)
                value = piece if value is None else value + piece
            dst[:, cols(j, 512)] = value.astype(dst.dtype)

    def sum_p(a, r, d, *ks):
        dst = room(a, own(r, d), 4)
        total(a, dst, (dst, *[room(a, RING_P + 4 * k, 4) for k in ks]))

    def sum_q(a, r, e, *ks):
        dst = room(a, own(r, 0, e))
        total(a, dst, (dst, *[room(a, RING_Q + k) for k in ks]))

    def post_p(a, k, r, d, device):
        src, dst = lambda: room(a, own(r, d), 4), lambda: room(a, RING_P + 4 * k, 4)
        mail.post(("P", a, k), src, dst, device)

    def take_p(a, *ks):
        for k in ks:
            mail.take(("P", a, k), room(a, RING_P + 4 * k, 4), right_p)

    def post_q(a, k, r, e, device):
        mail.post(("Q", a, k), room(a, own(r, 0, e)), room(a, RING_Q + k), device)

    def take_q(a, *ks):
        for k in ks:
            mail.take(("Q", a, k), room(a, RING_Q + k), right_q)

    over_y = at.over_y()

    def post_y(d):
        src, dst = lambda: room(DOWN, own(1, d), 4), lambda: room(DOWN, 32 + 4 * d, 4)
        mail.post(("Z", d), src, dst, over_y)

    def take_y(d):
        mail.take(("Z", d), room(DOWN, 32 + 4 * d, 4), right_p)
        dst = room(DOWN, own(0, d), 4)
        total(DOWN, dst, (dst, room(DOWN, 32 + 4 * d, 4)))

    def down_p(d, e):
        return room(DOWN, own(0, d, e), 2)

    def down_ring_p(k):
        return room(DOWN, 48 + 2 * k, 2)

    def down_rows(e, half):
        return w2.at[pl.ds(own(0, 0, e) * 64 + 32 * half, 32), :]

    def down_ring_q(k):
        return w2.at[pl.ds(60 * 64 + 32 * k, 32), :]

    def down1(a):
        ready(DOWN)
        products(DOWN, 2)
        post_y(2)

    def down2(a):
        for d in (1, 3, 0):
            products(DOWN, d)
            post_y(d)

    def down_post(k, d, e, device):
        mail.post(("P", DOWN, k), down_p(d, e), down_ring_p(k), device)

    def down_take(*ks):
        for k in ks:
            mail.take(("P", DOWN, k), down_ring_p(k), right_p)

    def down3():
        take_y(2)
        down_post(0, 2, 0, right_p)
        down_post(1, 2, 2, left_p)

    def down4():
        take_y(1)
        down_post(2, 1, 2, right_p)

    def down5():
        take_y(3)
        down_post(3, 3, 0, left_p)

    def down6():
        down_take(0)
        total(DOWN, down_p(1, 0), (down_p(1, 0), down_ring_p(0)))
        down_post(4, 1, 0, right_p)
        down_take(1)
        total(DOWN, down_p(3, 2), (down_p(3, 2), down_ring_p(1)))
        down_post(5, 3, 2, left_p)

    def down_post_q(k, e, half, device):
        mail.post(("Q", DOWN, k), down_rows(e, half), down_ring_q(k), device)

    def down_take_q(*ks):
        for k in ks:
            mail.take(("Q", DOWN, k), down_ring_q(k), right_q)

    def down7():
        take_y(0)
        down_take(2, 3, 4, 5)
        total(DOWN, down_p(0, 2), (down_p(0, 2), down_ring_p(2), down_ring_p(5)))
        down_post_q(0, 2, 0, right_q)
        down_post_q(1, 2, 1, left_q)
        down_post_q(3, 3, 0, left_q)
        total(DOWN, down_p(0, 0), (down_p(0, 0), down_ring_p(4), down_ring_p(3)))
        down_post_q(2, 1, 1, right_q)

    def down8():
        down_take_q(0)
        total(DOWN, down_rows(1, 0), (down_rows(1, 0), down_ring_q(0)))
        down_post_q(4, 1, 0, right_q)
        down_take_q(1)
        total(DOWN, down_rows(3, 1), (down_rows(3, 1), down_ring_q(1)))
        down_post_q(5, 3, 1, left_q)

    def down9():
        down_take_q(2, 3, 4, 5)
        for half, k, m in ((0, 4, 3), (1, 2, 5)):
            terms = (down_rows(0, half), down_ring_q(k), down_ring_q(m))
            total(DOWN, out_down.at[pl.ds(32 * half, 32), :], terms)

    def a1(a):
        ready(a)
        products(a, 2)
        post_p(a, 0, 0, 2, right_p)
        post_p(a, 1, 1, 2, left_p)

    def a2(a):
        products(a, 1)
        post_p(a, 2, 1, 1, right_p)
        products(a, 3)
        post_p(a, 3, 0, 3, left_p)

    def a3(a):
        take_p(a, 0)
        sum_p(a, 0, 1, 0)
        post_p(a, 4, 0, 1, right_p)
        take_p(a, 1)
        sum_p(a, 1, 3, 1)
        post_p(a, 5, 1, 3, left_p)
        products(a, 0)

    def a4(a):
        take_p(a, 2, 3, 4, 5)
        sum_p(a, 0, 0, 4, 3)
        sum_p(a, 1, 0, 2, 5)
        post_q(a, 0, 0, 2, right_q)
        post_q(a, 1, 1, 2, left_q)
        post_q(a, 2, 1, 1, right_q)
        post_q(a, 3, 0, 3, left_q)

    def a5(a):
        take_q(a, 0)
        sum_q(a, 0, 1, 0)
        post_q(a, 4, 0, 1, right_q)
        take_q(a, 1)
        sum_q(a, 1, 3, 1)
        post_q(a, 5, 1, 3, left_q)

    def a6(a):
        take_q(a, 2, 3, 4, 5)
        sum_q(a, 1, 0, 2, 5)
        mail.post(("Y", a), room(a, own(1, 0)), room(a, LAST), at.over_y())

    outs = (out_down, out_up, out_qkv, out_out)

    def a7(a):
        mail.take(("Y", a), room(a, LAST), right_p)
        terms = (room(a, own(0, 0)), room(a, RING_Q + 4), room(a, RING_Q + 3), room(a, LAST))
        total(a, outs[a], terms)

    def when_first(*steps):
        @pl.when(first_section)
        def _():
            for step, a in steps:
                step(a)

    even_p, even_q = 1 - 2 * lax.rem(at.p, 2), 1 - 2 * lax.rem(at.q, 2)
    partners = (
        at.other_core(),
        at.at(even_p, 0),
        at.at(-even_p, 0),
        at.at(0, even_q),
        at.at(0, -even_q),
        at.over_y(),
    )

    def post_vec(k):
        mail.post(("V", k), vec_sum.at[k], vec_got.at[k], partners[k])

    def take_vec(k):
        mail.take(("V", k), vec_got.at[k], partners[k])
        vec_sum[k + 1] = vec_sum[k] + vec_got[k]


    g_vec = vec_sum.at[0]
    g_vec[...] = jnp.zeros((16, D), f32)

    def grad_up(rows):
        @tiles(0, 8, 4)
        def _(j):
            g = dot(g_y[rows, :], w2[cols(j, 512), :], NT)
            g = (g * gprime[rows, cols(j, 512)]).astype(bf16)
            g_upward[rows, cols(j, 512)] = g
            spot = (pl.ds(8 + j // 2, 1), cols(j % 2, 512))
            g_vec[spot] = g_vec[spot] + jnp.sum(g.astype(f32), axis=0, keepdims=True)

    @pl.when(first_section)
    def _():
        for b in range(2):
            forth[b].start()
        mail.finish(gathered)
        for b in range(2):
            back[b].wait_recv()
            g_y[halves[b], :] = gyin[halves[b], :]
            grad_up(halves[b])

    @pl.when(second_section)
    def _():
        rows_in[1].wait()
        g_y[...] = gyin[...]
        grad_up(whole)

    post_rhs(DOWN)
    post_rhs(UP)
    give_room(DOWN)

    @tiles(0, 4, 2)
    def _(j):
        grad[:, cols(j, 256)] = dot(g_upward[...], w1[cols(j, 256), pl.ds(UP0, FF)], NT)

    give_room(UP)
    when_first((down1, DOWN), (a1, UP))

    def add(index, value):
        g_vec[pl.ds(index, 1), :] = g_vec[pl.ds(index, 1), :] + jnp.sum(
            value, axis=0, keepdims=True
        )

    def norm_back(rows, xhat, rstd, gain, shift):
        dy = grad[rows, :]
        h = xhat[rows, :]
        add(gain, dy * h)
        add(shift, dy)
        dh = dy * vec[pl.ds(gain, 1), :]
        m1 = jnp.mean(dh, axis=-1, keepdims=True)
        m2 = jnp.mean(dh * h, axis=-1, keepdims=True)
        return rstd[rows, pl.ds(0, 1)] * (dh - m1 - h * m2)

    def three(rows):
        gy = g_y[rows, :].astype(f32)
        gm = gy + norm_back(rows, xhat2, rstd2, G_TWO, S_TWO)
        add(B_DOWN, gy)
        middle[rows, :] = gm
        low = gm.astype(bf16)
        g_branch[rows, :] = low
        add(B_OUT, low.astype(f32))

    rows_loop(three)
    post_rhs(OUT)

    @tiles(0, 4, 2)
    def _(j):
        y = dot(g_branch[...], w1[cols(j, 256), pl.ds(OUT0, D)], NT)
        act[:, cols(j, 256)] = y.astype(bf16)

    give_room(OUT)
    when_first((a2, UP), (down2, DOWN))

    def attend_back(lo, hi, step=1):
        @tiles(lo, hi, step)
        def _(hp):
            for b in range(2):
                queries = pair(heads(mixed, b, 0, hp))
                keys, values = heads(mixed, b, 1, hp), heads(mixed, b, 2, hp)
                da = pair(heads(act, b, 0, hp))
                p = probs[2 * hp + b]
                dv = dot(p.astype(bf16), da, TN)
                dp = dot(da, values, NT)
                delta = jnp.sum(p * dp, axis=-1, keepdims=True)
                ds = (p * (dp - delta)).astype(bf16)
                dq = unpair(dot(ds, keys)) * 0.125
                dk = dot(ds, queries, TN) * 0.125
                for part, value in enumerate((dq, dk, dv)):
                    span = (pl.ds(b * BLOCK, BLOCK), cols(hp, 128, part * D))
                    g_mixed[span] = value.astype(bf16)

    attend_back(0, 8, 2)
    post_rhs(QKV)
    when_first((a3, UP))

    @tiles(0, 4, 2)
    def _(j):
        grad[:, cols(j, 256)] = dot(g_mixed[...], w1[cols(j, 256), pl.ds(QKV0, 3 * D)], NT)

    give_room(QKV)

    def four(rows):
        gx = middle[rows, :] + norm_back(rows, xhat1, rstd1, G_ONE, S_ONE)
        input_grad[rows, :] = gx.astype(bf16)
        add(B_QUERY, g_mixed[rows, pl.ds(0, D)].astype(f32))
        add(B_VALUE, g_mixed[rows, pl.ds(2 * D, D)].astype(f32))

    for b in range(2):
        four(halves[b])

        @pl.when(second_section)
        def _(b=b):
            back[b].start()

    @pl.when(second_section)
    def _():
        for step, a in ((down1, DOWN), (a1, UP), (a2, UP), (down2, DOWN), (a3, UP)):
            step(a)

    post_vec(0)
    a1(QKV)
    a2(QKV)
    a1(OUT)
    a2(OUT)
    take_vec(0)
    post_vec(1)
    down3()
    a3(QKV)
    take_vec(1)
    post_vec(2)
    a3(OUT)
    down4()
    a4(UP)
    take_vec(2)
    post_vec(3)
    a4(QKV)
    a5(UP)
    a4(OUT)
    take_vec(3)
    post_vec(4)
    down5()
    down6()
    a6(UP)
    a5(QKV)
    a5(OUT)
    take_vec(4)
    post_vec(5)
    a6(QKV)
    a6(OUT)
    down7()
    a7(UP)
    take_vec(5)
    vec_out[...] = vec_sum[6]
    down8()
    a7(QKV)
    a7(OUT)
    down9()

    @pl.when(first_section)
    def _():
        for b in range(2):
            forth[b].wait_send()

    @pl.when(second_section)
    def _():
        for b in range(2):
            back[b].wait_send()

    mail.finish([name for name in mail.sent if name not in gathered])


def step(*args):
    def out(rows, columns, kind=bf16):
        return jax.ShapeDtypeStruct((rows, columns), kind)

    return pl.pallas_call(
        step_kernel,
        out_shape=(
            out(ROWS, D),
            out(ROWS, D),
            *[out(rows, width, f32) for rows, width, _ in KINDS],
            out(16, D, f32),
        ),
        in_specs=[ANY, VMEM, ANY, *[ANY] * 5],
        out_specs=(VMEM,) * 7,
        scratch_shapes=[
            pltpu.VMEM((D, NA), bf16),
            pltpu.VMEM((FF, D), bf16),
            pltpu.VMEM((ROWS, D), bf16),
            pltpu.VMEM((ROWS, D), bf16),
            pltpu.VMEM((8, D), f32),
            pltpu.VMEM((8, FF), f32),
            pltpu.VMEM((8, 3 * D), f32),
            pltpu.VMEM((ROWS, D), f32),
            pltpu.VMEM((ROWS, 128), f32),
            pltpu.VMEM((ROWS, D), f32),
            pltpu.VMEM((ROWS, 128), f32),
            pltpu.VMEM((ROWS, 3 * D), bf16),
            pltpu.VMEM((2, BLOCK, BLOCK), f32),
            pltpu.VMEM((16, 2 * BLOCK, BLOCK), f32),
            pltpu.VMEM((ROWS, D), f32),
            pltpu.VMEM((ROWS, FF), f32),
            pltpu.VMEM((ROWS, FF), bf16),
            pltpu.VMEM((ROWS, D), f32),
            *[pltpu.VMEM((32, 2, rows, ROWS), bf16) for rows, _, _ in KINDS],
            *[pltpu.VMEM((32, rows, ROWS), bf16) for rows, _, _ in KINDS],
            *[pltpu.VMEM((2 * ROWS, width), bf16) for _, width, _ in KINDS],
            pltpu.VMEM((128, 2 * ROWS), bf16),
            pltpu.VMEM((512, 2 * ROWS), bf16),
            pltpu.VMEM((7, 16, D), f32),
            pltpu.VMEM((6, 16, D), f32),
            pltpu.SemaphoreType.DMA((COPIES,)),
            pltpu.SemaphoreType.DMA((COPIES,)),
            pltpu.SemaphoreType.DMA((6,)),
            *[pltpu.SemaphoreType.REGULAR] * 4,
        ],
        compiler_params=pltpu.CompilerParams(
            collective_id=0, has_side_effects=True, vmem_limit_bytes=62 * 2**20
        ),
        name="step",
    )(*args)


def lay_out_kernel(index, *refs):
    big_in, sums_in, big_out, vectors = refs[:6], refs[6], refs[7:13], refs[13:22]
    held, (sums, came, left) = refs[22:28], refs[28:]
    first = pltpu.make_async_copy(sums_in, sums, came.at[6])
    first.start()
    come = [pltpu.make_async_copy(big_in[k], held[k], came.at[k]) for k in range(6)]
    leave = [pltpu.make_async_copy(held[k], big_out[k], left.at[k]) for k in range(6)]
    for copy in come:
        copy.start()
    for k in range(6):
        come[k].wait()
        leave[k].start()
    first.wait()
    i = index[0]
    own = sums[pl.ds(0, 8), cols(i // 8, 128)]
    own = pltpu.roll(own, lax.rem(128 - lax.rem(i, 8) * 16, 128), 1)
    for k in range(8):
        vectors[k][...] = own[k : k + 1, 0:16]
    rows = sums[pl.ds(8, 8), cols(lax.rem(i, 16) // 2, 128)]
    rows = pltpu.roll(rows, lax.rem(128 - lax.rem(i, 2) * 64, 128), 1)
    row = lax.broadcasted_iota(jnp.int32, (8, 128), 0) == i // 16
    vectors[8][...] = jnp.sum(jnp.where(row, rows, 0.0), axis=0, keepdims=True)[:, 0:64]
    for copy in leave:
        copy.wait()


def lay_out(index, big, sums):
    return pl.pallas_call(
        lay_out_kernel,
        out_shape=(
            *[jax.ShapeDtypeStruct(v.shape, v.dtype) for v in big],
            *[jax.ShapeDtypeStruct((1, 16), f32)] * 8,
            jax.ShapeDtypeStruct((1, 64), f32),
        ),
        in_specs=[SMEM, *[ANY] * 7],
        out_specs=(*[ANY] * 6, *[VMEM] * 9),
        scratch_shapes=[
            *[pltpu.VMEM(v.shape, v.dtype) for v in big],
            pltpu.VMEM((16, D), f32),
            pltpu.SemaphoreType.DMA((7,)),
            pltpu.SemaphoreType.DMA((6,)),
        ],
        compiler_params=pltpu.CompilerParams(vmem_limit_bytes=62 * 2**20),
        name="lay_out",
    )(index, *big, sums)


def body(
    tokens,
    positions,
    cotangent,
    w_qkv,
    b_query,
    b_value,
    w_out,
    b_out,
    w_up,
    b_up,
    w_down,
    b_down,
    gain_one,
    shift_one,
    gain_two,
    shift_two,
):
    index = lax.axis_index(DP)
    small = (b_query, b_value, b_out, b_down, gain_one, shift_one, gain_two, shift_two)
    lane = jnp.arange(128)[None]
    rows = jnp.tile(jnp.concatenate(small, axis=0), (1, 8))
    rows = jnp.where(lane // 16 == index % 8, rows, jnp.zeros_like(rows))
    wide = jnp.tile(b_up, (8, 2))
    wide = jnp.where(lane // 64 == index % 2, wide, jnp.zeros_like(wide))
    *big, sums = step(
        tokens.reshape(ROWS, D),
        positions,
        cotangent.reshape(ROWS, D),
        jnp.concatenate([rows, wide], axis=0),
        w_qkv[0],
        w_out[0],
        w_up[0],
        w_down[0],
    )
    layer_out, input_grad, down, up, qkv, out, *vectors = lay_out(
        jnp.reshape(index, (1,)).astype(jnp.int32), big, sums
    )
    return (
        layer_out.reshape(1, 2, BLOCK, D),
        input_grad.reshape(1, 2, BLOCK, D),
        qkv[None],
        vectors[B_QUERY],
        vectors[B_VALUE],
        out[None],
        vectors[B_OUT],
        up[None],
        vectors[8],
        down[None],
        vectors[B_DOWN],
        vectors[G_ONE],
        vectors[S_ONE],
        vectors[G_TWO],
        vectors[S_TWO],
    )


def solution(mesh):
    torus = Mesh(mesh.devices.reshape(2, 2, 4, 4, 2), AXES)
    rows, matrix, vector = P(None, DP, None), P("section", DP, None), P("section", DP)
    of_layer = P("section", None, DP, None)
    return jax.shard_map(
        body,
        mesh=torus,
        in_specs=(
            rows,
            P(None, DP),
            rows,
            matrix,
            vector,
            vector,
            matrix,
            vector,
            matrix,
            vector,
            matrix,
            vector,
            vector,
            vector,
            vector,
            vector,
        ),
        out_specs=(
            of_layer,
            of_layer,
            matrix,
            vector,
            vector,
            matrix,
            vector,
            matrix,
            vector,
            matrix,
            vector,
            vector,
            vector,
            vector,
            vector,
        ),
        check_vma=False,
    )
```
